32 devices in a mesh: groups: 2 (over x), row: 4 (over y, core), col: 4 (over z).
Axes of the slice: x: 2, y: 2, z: 4, core: 2. Of those that a mesh axis runs over, the one named last changes fastest.
Arguments:
- pair_act: bfloat16 [1536, 768, 128], P(('groups', 'row'), 'col'), parts along dimension 0, may hold values from -6 to 6
- ln_gain: float32 [128], replicated, may hold values from 0.1 to 1.9
- ln_bias: float32 [128], replicated, may hold values from -3 to 3
- w_proj: bfloat16 [128, 512], replicated, may hold values from -0.5 to 0.5
- w_gate: bfloat16 [128, 128], replicated, may hold values from -0.5 to 0.5
- out_gain: float32 [128], replicated, may hold values from 0.1 to 1.9
- out_bias: float32 [128], replicated, may hold values from -3 to 3
- w_out: bfloat16 [128, 128], replicated, may hold values from -0.5 to 0.5
Outputs:
- update: bfloat16 [1536, 768, 128], P(('groups', 'row'), 'col'), parts along dimension 0
The draws below stay inside these ranges and needn't reach their ends.
There are 2 independent parts, one for each index of `groups`. The reference program is written for one: setup_inputs(seed, part) draws one part's arguments, and reference() takes and returns one part's arrays. A program takes and returns all parts, laid end to end along the dimension named above; an argument that names none is the same for every part. Nothing has to cross between parts.
All inputs are finite; a program needn't handle non-finite values.
Results may differ from the reference program's by a relative error of at most 0.013.
Values may be sent and summed in bfloat16 or wider, within the bound.
No kernel may reach another device: no remote copies, remote signals or barrier semaphores. Data moves between devices by JAX's collectives and lax.ppermute only.
A program may use at most 192 MiB of HBM per device.

```python
import jax
import jax.numpy as jnp
from jax import lax

PAIR_CH = 128
HIDDEN_CH = 128
TOKENS = 768
N_COL = 4


def level_of(own_key, extent, shards, low, high):
    factor_of, own = 1.0, jax.random.fold_in(own_key, 6)
    for dim, parts in shards:
        steps = jnp.exp(jax.random.uniform(jax.random.fold_in(own, dim), (parts,), jnp.float32, low / len(shards), high / len(shards)))
        factor_of = factor_of * jnp.repeat(steps, extent[dim] // parts).reshape([-1 if axis == dim else 1 for axis in range(len(extent))])
    return factor_of


def bell_draw(own_key, shape, width, most, cuts=(), held_as=jnp.bfloat16):
    entries = width * jax.random.normal(own_key, shape, jnp.float32)
    if cuts:
        entries = entries * level_of(own_key, shape, cuts, -0.22, 0.18)
    return jnp.clip(entries, -most, most).astype(held_as)


def setup_inputs(seed: int = 0, part: int = 0) -> dict:
    key_list = jax.random.split(jax.random.key(seed), 9)
    own_keys = jax.random.split(jax.random.fold_in(key_list[8], part), 9)
    pair_act = bell_draw(own_keys[0], (TOKENS, TOKENS, PAIR_CH), 1.0, 6.0, ((0, 4), (1, 4)))
    ln_gain = jnp.clip(1.0 + 0.18 * jax.random.normal(key_list[1], (PAIR_CH,), jnp.float32), 0.1, 1.9)
    ln_bias = bell_draw(key_list[2], (PAIR_CH,), 0.5, 3.0, (), jnp.float32)
    w_proj = bell_draw(key_list[3], (PAIR_CH, 4 * HIDDEN_CH), PAIR_CH ** -0.5, 0.5)
    w_gate = bell_draw(key_list[4], (PAIR_CH, PAIR_CH), PAIR_CH ** -0.5, 0.5)
    out_gain = jnp.clip(1.0 + 0.18 * jax.random.normal(key_list[5], (HIDDEN_CH,), jnp.float32), 0.1, 1.9)
    out_bias = bell_draw(key_list[6], (HIDDEN_CH,), 0.5, 3.0, (), jnp.float32)
    w_out = bell_draw(key_list[7], (HIDDEN_CH, PAIR_CH), HIDDEN_CH ** -0.5, 0.5)
    return {"pair_act": pair_act, "ln_gain": ln_gain, "ln_bias": ln_bias, "w_proj": w_proj, "w_gate": w_gate, "out_gain": out_gain, "out_bias": out_bias, "w_out": w_out}


def layer_norm(values, scale_gain, shift_bias):
    average = lax.optimization_barrier(jnp.mean(values, axis=-1, keepdims=True))
    centred = values - average
    variance = lax.optimization_barrier(jnp.mean(centred * centred, axis=-1, keepdims=True))
    return centred * lax.rsqrt(variance + 1e-05) * scale_gain + shift_bias

def reference(pair_act, ln_gain, ln_bias, w_proj, w_gate, out_gain, out_bias, w_out):
    hidden_width = HIDDEN_CH
    normed = layer_norm(pair_act.astype(jnp.float32), ln_gain, ln_bias).astype(jnp.bfloat16)
    flattened = normed.reshape(TOKENS * TOKENS, PAIR_CH)
    projected = jnp.dot(flattened, w_proj, preferred_element_type=jnp.float32)
    left_side = (jax.nn.sigmoid(projected[:, :hidden_width]) * projected[:, hidden_width:2 * hidden_width]).astype(jnp.bfloat16)
    right_side = (jax.nn.sigmoid(projected[:, 2 * hidden_width:3 * hidden_width]) * projected[:, 3 * hidden_width:]).astype(jnp.bfloat16)
    left_side = left_side.reshape(TOKENS, TOKENS, hidden_width)
    right_side = right_side.reshape(TOKENS, TOKENS, hidden_width)
    gating = jax.nn.sigmoid(jnp.dot(flattened, w_gate, preferred_element_type=jnp.float32)).astype(jnp.bfloat16)
    gating = gating.reshape(TOKENS, TOKENS, PAIR_CH)
    block_size = TOKENS // N_COL

    def add_block(block_index, running):
        first_col = (block_index * block_size).astype(jnp.int32)
        left_block = lax.dynamic_slice_in_dim(left_side, first_col, block_size, 1).astype(jnp.float32)
        right_block = lax.dynamic_slice_in_dim(right_side, first_col, block_size, 1).astype(jnp.float32)
        partial_sum = jnp.einsum('ikh,jkh->ijh', left_block, right_block)
        partial_sum = lax.optimization_barrier(partial_sum.astype(jnp.bfloat16)).astype(jnp.float32)
        return running + partial_sum
    tri_sum = lax.fori_loop(0, N_COL, add_block, jnp.zeros((TOKENS, TOKENS, hidden_width), jnp.float32))
    out_normed = layer_norm(tri_sum, out_gain, out_bias).astype(jnp.bfloat16)
    result = jnp.dot(out_normed.reshape(TOKENS * TOKENS, hidden_width), w_out, preferred_element_type=jnp.float32)
    result = result.reshape(TOKENS, TOKENS, PAIR_CH)
    return (result * gating.astype(jnp.float32)).astype(jnp.bfloat16)
```

```python
import functools
import math

import jax
import jax.numpy as jnp
from jax import lax
from jax.experimental import pallas as pl
from jax.experimental.pallas import tpu as pltpu
from jax.sharding import PartitionSpec as P

CHUNKS = 3
EPS = 1e-05
F32, BF16 = jnp.float32, jnp.bfloat16
PARAMS = pltpu.CompilerParams(vmem_limit_bytes=52 * 1024 * 1024)


def contract(left, right, left_dim, right_dim):
    return lax.dot_general(
        left, right, (((left_dim,), (right_dim,)), ((), ())), preferred_element_type=F32
    )


def project_kernel(n_pieces, *refs):
    pieces, (weights, centre, gain, bias, left_out, right_out, left_rows, right_rows) = (
        refs[:n_pieces],
        refs[n_pieces:],
    )
    hidden, rows, depth = left_out.shape

    def one_row(i, carry):
        values = jnp.concatenate([piece[i] for piece in pieces], axis=0)
        centred = contract(centre[...], values, 1, 1)
        variance = jnp.mean(centred * centred, axis=0, keepdims=True)
        normed = centred * lax.rsqrt(variance + EPS) * gain[...] + bias[...]
        halved = contract(weights[...], normed.astype(BF16), 1, 0)
        for first, held in ((0, left_rows), (2 * hidden, right_rows)):
            gate, value = halved[first : first + hidden], halved[first + hidden : first + 2 * hidden]
            side = value + value * jnp.tanh(gate)
            for n in range(depth // 128):
                held[n, pl.ds(i, hidden, stride=rows), :] = side[:, n * 128 : (n + 1) * 128]
        return carry

    lax.fori_loop(0, rows, one_row, 0, unroll=2)
    for held, out in ((left_rows, left_out), (right_rows, right_out)):
        for n in range(depth // 128):
            out[:, :, n * 128 : (n + 1) * 128] = held[n].reshape(hidden, rows, 128).astype(BF16)


def project(pieces, firsts, count, weights, centre, gain, bias):
    rows = 16
    hidden = weights.shape[0] // 4
    channels = weights.shape[1]
    depth = sum(piece.shape[1] for piece in pieces)
    whole = lambda x: pl.BlockSpec(x.shape, lambda i: (0,) * x.ndim)
    in_specs = [
        pl.BlockSpec((rows, piece.shape[1], channels), functools.partial(lambda f, i: (i + f, 0, 0), first // rows))
        for piece, first in zip(pieces, firsts)
    ] + [whole(x) for x in (weights, centre, gain, bias)]
    shape = jax.ShapeDtypeStruct((hidden, count, depth), BF16)
    return pl.pallas_call(
        functools.partial(project_kernel, len(pieces)),
        grid=(count // rows,),
        in_specs=in_specs,
        out_specs=[pl.BlockSpec((hidden, rows, depth), lambda i: (0, i, 0))] * 2,
        out_shape=[shape, shape],
        scratch_shapes=[pltpu.VMEM((depth // 128, hidden * rows, 128), F32)] * 2,
        compiler_params=PARAMS,
        name="project",
    )(*pieces, weights, centre, gain, bias)


def triangle_kernel(n_sides, group, which, left, *refs):
    sides, out = refs[:n_sides], refs[n_sides]

    def go(side):
        for first in range(0, left.shape[0], group):
            parts = [contract(left[h], side[h], 1, 1) for h in range(first, first + group)]
            out[first // group] = jnp.concatenate(parts, axis=-1).astype(BF16)

    for n, side in enumerate(sides):
        pl.when(which[0] == n)(functools.partial(go, side))


def group_of(columns):
    return 128 // math.gcd(columns, 128)


def triangle(left, sides, which):
    hidden, rows, depth = left.shape
    columns = sides[0].shape[1]
    group = group_of(columns)
    step = max(16, group)

    def side_spec(n):
        return pl.BlockSpec((step, columns, depth), lambda h, which: (jnp.where(which[0] == n, h, 0), 0, 0))

    return pl.pallas_call(
        functools.partial(triangle_kernel, len(sides), group),
        grid_spec=pltpu.PrefetchScalarGridSpec(
            num_scalar_prefetch=1,
            grid=(hidden // step,),
            in_specs=[pl.BlockSpec((step, rows, depth), lambda h, which: (h, 0, 0))]
            + [side_spec(n) for n in range(len(sides))],
            out_specs=pl.BlockSpec((step // group, rows, group * columns), lambda h, which: (h, 0, 0)),
        ),
        out_shape=jax.ShapeDtypeStruct((hidden // group, rows, group * columns), BF16),
        compiler_params=PARAMS,
        name="triangle",
    )(which, left, *sides)


def gate_kernel(pair, centre, mean, gain, bias, weights, out):
    rows, columns, channels = pair.shape
    values = pair[...].reshape(rows * columns, channels)
    centred = contract(values, centre[...], 1, 0)
    square = centred * centred
    high = square.astype(BF16)
    low = (square - high.astype(F32)).astype(BF16)
    variance = contract(jnp.concatenate([high, low], axis=1), mean[...], 1, 0)
    normed = (centred * lax.rsqrt(variance + EPS) * gain[...] + bias[...]).astype(BF16)
    gate = 0.5 + 0.5 * jnp.tanh(contract(normed, weights[...], 1, 0))
    out[...] = gate.astype(BF16).reshape(rows, columns, channels)


def gate_of(pair, centre, mean, gain, bias, weights):
    rows = 8
    count, columns, channels = pair.shape
    whole = lambda x: pl.BlockSpec(x.shape, lambda i: (0,) * x.ndim)
    block = pl.BlockSpec((rows, columns, channels), lambda i: (i, 0, 0))
    return pl.pallas_call(
        gate_kernel,
        grid=(count // rows,),
        in_specs=[block] + [whole(x) for x in (centre, mean, gain, bias, weights)],
        out_specs=block,
        out_shape=jax.ShapeDtypeStruct(pair.shape, BF16),
        compiler_params=PARAMS,
        name="gate",
    )(pair, centre, mean, gain, bias, weights)


def finish_kernel(n_parts, group, hidden, *refs):
    own, sent = refs[:n_parts], refs[n_parts : 2 * n_parts]
    gate, weights, gain, bias, _, out, rows_of = refs[2 * n_parts :]
    packed, rows, lanes = own[0].shape
    columns = lanes // group

    def over_hidden(x):
        total = jnp.sum(x, axis=0)
        shift = columns
        while shift < lanes:
            total = total + pltpu.roll(total, shift, 1)
            shift *= 2
        return total * (1.0 / hidden)

    for n in range(n_parts):
        total = own[n][...].astype(F32) + sent[n][...].astype(F32)
        centred = total - over_hidden(total)[None]
        scale = lax.rsqrt(over_hidden(centred * centred) + EPS)
        normed = centred * scale[None] * gain[...] + bias[...]
        rows_of[n] = normed.reshape(packed * rows, lanes)
    for i in range(rows):
        parts = []
        for n in range(n_parts):
            held = rows_of[n, pl.ds(i, packed, stride=rows), :]
            parts.append(
                jnp.concatenate([held[:, g * columns : (g + 1) * columns] for g in range(group)], axis=0)
            )
        normed = jnp.concatenate(parts, axis=1).astype(BF16)
        result = contract(normed, weights[...], 0, 0)
        out[i] = (result * gate[i].astype(F32)).astype(BF16)


def finish(own, sent, gate, first, weights, gain, bias, held):
    rows = 8
    packed, count, lanes = own[0].shape
    hidden = weights.shape[0]
    group = hidden // packed
    whole = lambda x: pl.BlockSpec(x.shape, lambda i: (0,) * x.ndim)
    part = pl.BlockSpec((packed, rows, lanes), lambda i: (0, i, 0))
    block = pl.BlockSpec((rows,) + gate.shape[1:], lambda i: (i + first // rows, 0, 0))
    n_parts = len(own)
    return pl.pallas_call(
        functools.partial(finish_kernel, n_parts, group, hidden),
        grid=(count // rows,),
        in_specs=[part] * (2 * n_parts)
        + [block, whole(weights), whole(gain), whole(bias), pl.BlockSpec(memory_space=pl.ANY)],
        out_specs=block,
        out_shape=jax.ShapeDtypeStruct(gate.shape, BF16),
        scratch_shapes=[pltpu.VMEM((n_parts, packed * rows, lanes), F32)],
        input_output_aliases={2 * n_parts + 4: 0},
        compiler_params=PARAMS,
        name="finish",
    )(*own, *sent, gate, weights, gain, bias, held)


def after(value, *others):
    return lax.optimization_barrier((value,) + others)[0]


def on_device(n_row, n_col, pair_act, ln_gain, ln_bias, w_proj, w_gate, out_gain, out_bias, w_out):
    tile_rows, tile_cols, channels = pair_act.shape
    hidden = w_proj.shape[1] // 4
    half = n_col // 2
    top = n_row // 2
    share = n_row // n_col
    row, col = lax.axis_index("row"), lax.axis_index("col")
    axes = ("row", "col")
    place = lambda r, c: r * n_col + c
    step = tile_rows // CHUNKS
    group = group_of(step)
    packed = hidden // group

    halves = (w_proj * 0.5).astype(BF16).T
    centre = (jnp.eye(channels, dtype=F32) - 1.0 / channels).astype(BF16)
    mean = jnp.full((2 * channels, channels), 1.0 / channels, BF16)
    half_gate = (w_gate * 0.5).astype(BF16)
    by_hidden = lambda v: jnp.repeat(v.reshape(packed, group), step, axis=1)[:, None, :]
    gain_out, bias_out = by_hidden(out_gain), by_hidden(out_bias)
    w_last = w_out.reshape(packed, group, channels).swapaxes(0, 1).reshape(hidden, channels)

    def holds(r, c):
        return (r // share) % half == c % half

    def spread(near):
        far = lax.ppermute(
            near,
            axes,
            [(place(r, c), place(r ^ top, c)) for r in range(n_row) for c in range(n_col) if holds(r, c)],
        )
        bit = top // 2
        while bit >= share:
            alike = (bit * 2 - 1) & ~(share - 1)
            sends = [
                (place(r, c), place(r ^ bit, c))
                for r in range(n_row)
                for c in range(n_col)
                if (r ^ (c * share)) & alike == 0
            ]
            near_in, far_in = lax.ppermute(near, axes, sends), lax.ppermute(far, axes, sends)
            keep = ((row ^ (col * share)) & bit) == 0
            if bit == 1:
                return [near, near_in, far, far_in], jnp.where(keep, 0, 1)
            near, far = jnp.where(keep, near, near_in), jnp.where(keep, far, far_in)
            bit //= 2
        sides = [[near], [far]]
        while bit >= 1:
            swap = [(r, r ^ bit) for r in range(n_row)]
            first = (row & bit) == 0
            for n in range(2):
                others = [lax.ppermute(x, "row", swap) for x in sides[n]]
                sides[n] = [jnp.where(first, a, b) for a, b in zip(sides[n] + others, others + sides[n])]
            bit //= 2
        return sides, jnp.int32(0)

    near_is_own = (row // top) == (col // half)
    swap_half = [(c, c ^ half) for c in range(n_col)]
    lefts, spreads, sent = [], [], {}

    def product(i, j, s, own):
        sides, choice = spreads[j]
        take_near = near_is_own if own else jnp.logical_not(near_is_own)
        if share == 1:
            which = jnp.where(take_near, choice, choice + len(sides) // 2)
            return triangle(lefts[i], sides, which.astype(jnp.int32).reshape(1))
        which = jnp.where(take_near, 0, 1)
        return triangle(lefts[i], [sides[0][s], sides[1][s]], which.astype(jnp.int32).reshape(1))

    blocks = [pair_act[t * step : (t + 1) * step] for t in range(CHUNKS)]
    last = None
    for t in range(CHUNKS):
        block = blocks[t] if last is None else after(blocks[t], last)
        pieces = [block]
        for offset in range(1, half):
            pieces.append(lax.ppermute(block, "col", [(c, c ^ offset) for c in range(n_col)]))
        last = pieces[-1]
        left, right = project(
            [pair_act] + pieces[1:],
            [t * step] + [0] * (half - 1),
            step,
            halves,
            centre,
            ln_gain[:, None],
            ln_bias[:, None],
        )
        lefts.append(left)
        spreads.append(spread(right))
        for i, j in [(a, t) for a in range(t)] + [(t, b) for b in range(t + 1)]:
            for s in range(share):
                sent[i, j, s] = lax.ppermute(product(i, j, s, False), "col", swap_half)

    gate = gate_of(pair_act, centre, mean, ln_gain[None], ln_bias[None], half_gate)
    order = [(j, s) for s in range(share) for j in range(CHUNKS)]
    out = jnp.zeros(pair_act.shape, BF16)
    for i in range(CHUNKS):
        own = [product(i, j, s, True) for j, s in order]
        out = finish(own, [sent[i, j, s] for j, s in order], gate, i * step, w_last, gain_out, bias_out, out)
    return out


def solution(mesh):
    n_row, n_col = mesh.shape["row"], mesh.shape["col"]
    in_specs = (P(("groups", "row"), "col", None), P(), P(), P(), P(), P(), P(), P())
    out_specs = P(("groups", "row"), "col", None)
    return jax.shard_map(
        functools.partial(on_device, n_row, n_col),
        mesh=mesh,
        in_specs=in_specs,
        out_specs=out_specs,
        check_vma=False,
    )
```

```python
import functools
import math

import jax
import jax.numpy as jnp
from jax import lax
from jax.experimental import pallas as pl
from jax.experimental.pallas import tpu as pltpu
from jax.sharding import PartitionSpec as P

CHUNKS = 6
EPS = 1e-05
F32, BF16 = jnp.float32, jnp.bfloat16
PARAMS = pltpu.CompilerParams(vmem_limit_bytes=52 * 1024 * 1024)


def contract(left, right, left_dim, right_dim):
    return lax.dot_general(
        left, right, (((left_dim,), (right_dim,)), ((), ())), preferred_element_type=F32
    )


def at_least(macs, transcendentals, *arrays):
    return pl.CostEstimate(
        flops=2 * macs,
        transcendentals=transcendentals,
        bytes_accessed=sum(math.prod(x.shape) * x.dtype.itemsize for x in arrays),
    )


def project_kernel(n_pieces, *refs):
    pieces, (weights, centre, gain, bias, left_out, right_out, left_rows, right_rows) = (
        refs[:n_pieces],
        refs[n_pieces:],
    )
    hidden, rows, depth = left_out.shape

    def one_row(i, carry):
        values = jnp.concatenate([piece[i] for piece in pieces], axis=0)
        centred = contract(centre[...], values, 1, 1)
        variance = jnp.mean(centred * centred, axis=0, keepdims=True)
        normed = centred * lax.rsqrt(variance + EPS) * gain[...] + bias[...]
        halved = contract(weights[...], normed.astype(BF16), 1, 0)
        for first, held in ((0, left_rows), (2 * hidden, right_rows)):
            gate, value = halved[first : first + hidden], halved[first + hidden : first + 2 * hidden]
            side = value + value * jnp.tanh(gate)
            for n in range(depth // 128):
                held[n, pl.ds(i, hidden, stride=rows), :] = side[:, n * 128 : (n + 1) * 128]
        return carry

    lax.fori_loop(0, rows, one_row, 0, unroll=8)
    for held, out in ((left_rows, left_out), (right_rows, right_out)):
        for n in range(depth // 128):
            out[:, :, n * 128 : (n + 1) * 128] = held[n].reshape(hidden, rows, 128).astype(BF16)


def project(pieces, firsts, count, weights, centre, gain, bias):
    rows = 16
    hidden = weights.shape[0] // 4
    channels = weights.shape[1]
    depth = sum(piece.shape[1] for piece in pieces)
    whole = lambda x: pl.BlockSpec(x.shape, lambda i: (0,) * x.ndim)
    in_specs = [
        pl.BlockSpec((rows, piece.shape[1], channels), functools.partial(lambda f, i: (i + f, 0, 0), first // rows))
        for piece, first in zip(pieces, firsts)
    ] + [whole(x) for x in (weights, centre, gain, bias)]
    shape = jax.ShapeDtypeStruct((hidden, count, depth), BF16)
    return pl.pallas_call(
        functools.partial(project_kernel, len(pieces)),
        grid=(count // rows,),
        in_specs=in_specs,
        out_specs=[pl.BlockSpec((hidden, rows, depth), lambda i: (0, i, 0))] * 2,
        out_shape=[shape, shape],
        scratch_shapes=[pltpu.VMEM((depth // 128, hidden * rows, 128), F32)] * 2,
        compiler_params=PARAMS,
        cost_estimate=at_least(
            count * depth * channels * (channels + 4 * hidden), 2 * count * depth * hidden, shape, shape
        ),
        name="project",
    )(*pieces, weights, centre, gain, bias)


def triangle_kernel(n_left, n_sides, group, pairs, which, *refs):
    lefts, out = refs[:n_left], refs[-1]
    sides = refs[n_left:-1]
    step = lefts[0].shape[0]

    def go(choice):
        for first in range(0, step, group):
            for n, (i, j) in enumerate(pairs):
                side = sides[j * n_sides + choice]
                parts = [contract(lefts[i][h], side[h], 1, 1) for h in range(first, first + group)]
                out[n, first // group] = jnp.concatenate(parts, axis=-1).astype(BF16)

    for n in range(n_sides):
        pl.when(which[0] == n)(functools.partial(go, n))


def group_of(columns):
    return 128 // math.gcd(columns, 128)


def triangle(lefts, rights, pairs, which):
    hidden, rows, depth = lefts[0].shape
    columns = rights[0][0].shape[1]
    n_sides = len(rights[0])
    group = group_of(columns)
    step = max(8, group)
    shape = jax.ShapeDtypeStruct((len(pairs), hidden // group, rows, group * columns), BF16)

    def side_spec(n):
        return pl.BlockSpec((step, columns, depth), lambda h, which: (jnp.where(which[0] == n, h, 0), 0, 0))

    return pl.pallas_call(
        functools.partial(triangle_kernel, len(lefts), n_sides, group, pairs),
        grid_spec=pltpu.PrefetchScalarGridSpec(
            num_scalar_prefetch=1,
            grid=(hidden // step,),
            in_specs=[pl.BlockSpec((step, rows, depth), lambda h, which: (h, 0, 0))] * len(lefts)
            + [side_spec(n) for _ in rights for n in range(n_sides)],
            out_specs=pl.BlockSpec(
                (len(pairs), step // group, rows, group * columns), lambda h, which: (0, h, 0, 0)
            ),
        ),
        out_shape=shape,
        compiler_params=PARAMS,
        cost_estimate=at_least(
            len(pairs) * hidden * rows * columns * depth, 0, shape, *lefts, *[side[0] for side in rights]
        ),
        name="triangle",
    )(which, *lefts, *[x for side in rights for x in side])


def gate_kernel(pair, centre, mean, gain, bias, weights, out):
    rows, columns, channels = pair.shape
    values = pair[...].reshape(rows * columns, channels)
    centred = contract(values, centre[...], 1, 0)
    square = centred * centred
    high = square.astype(BF16)
    low = (square - high.astype(F32)).astype(BF16)
    variance = contract(jnp.concatenate([high, low], axis=1), mean[...], 1, 0)
    normed = (centred * lax.rsqrt(variance + EPS) * gain[...] + bias[...]).astype(BF16)
    gate = 0.5 + 0.5 * jnp.tanh(contract(normed, weights[...], 1, 0))
    out[...] = gate.astype(BF16).reshape(rows, columns, channels)


def gate_of(pair, centre, mean, gain, bias, weights):
    rows = 8
    count, columns, channels = pair.shape
    whole = lambda x: pl.BlockSpec(x.shape, lambda i: (0,) * x.ndim)
    block = pl.BlockSpec((rows, columns, channels), lambda i: (i, 0, 0))
    return pl.pallas_call(
        gate_kernel,
        grid=(count // rows,),
        in_specs=[block] + [whole(x) for x in (centre, mean, gain, bias, weights)],
        out_specs=block,
        out_shape=jax.ShapeDtypeStruct(pair.shape, BF16),
        compiler_params=PARAMS,
        cost_estimate=at_least(
            count * columns * channels * 4 * channels, count * columns * channels, pair, pair
        ),
        name="gate",
    )(pair, centre, mean, gain, bias, weights)


def finish_kernel(n_parts, group, hidden, *refs):
    own, sent = refs[:n_parts], refs[n_parts : 2 * n_parts]
    gate, weights, gain, bias = refs[2 * n_parts : 2 * n_parts + 4]
    out, rows_of = refs[-2:]
    packed, rows, lanes = own[0].shape
    columns = lanes // group

    def over_hidden(x):
        total = jnp.sum(x, axis=0)
        shift = columns
        while shift < lanes:
            total = total + pltpu.roll(total, shift, 1)
            shift *= 2
        return total * (1.0 / hidden)

    for n in range(n_parts):
        total = own[n][...].astype(F32) + sent[n][...].astype(F32)
        centred = total - over_hidden(total)[None]
        scale = lax.rsqrt(over_hidden(centred * centred) + EPS)
        normed = centred * scale[None] * gain[...] + bias[...]
        rows_of[n] = normed.reshape(packed * rows, lanes)
    for i in range(rows):
        parts = []
        for n in range(n_parts):
            held = rows_of[n, pl.ds(i, packed, stride=rows), :]
            parts.append(
                jnp.concatenate([held[:, g * columns : (g + 1) * columns] for g in range(group)], axis=0)
            )
        normed = jnp.concatenate(parts, axis=1).astype(BF16)
        result = contract(normed, weights[...], 0, 0)
        out[i] = (result * gate[i].astype(F32)).astype(BF16)


def finish(own, sent, gate, first, weights, gain, bias, held):
    rows = 16
    _, packed, count, lanes = own[0][0].shape
    hidden = weights.shape[0]
    group = hidden // packed
    whole = lambda x: pl.BlockSpec(x.shape, lambda i: (0,) * x.ndim)
    part = lambda n: pl.BlockSpec((None, packed, rows, lanes), lambda i: (n, 0, i, 0))
    block = pl.BlockSpec((rows,) + gate.shape[1:], lambda i: (i + first // rows, 0, 0))
    n_parts = len(own)
    parts = own + sent
    earlier = [] if held is None else [held]
    return pl.pallas_call(
        functools.partial(finish_kernel, n_parts, group, hidden),
        grid=(count // rows,),
        in_specs=[part(n) for _, n in parts]
        + [block, whole(weights), whole(gain), whole(bias)]
        + [pl.BlockSpec(memory_space=pl.ANY)] * len(earlier),
        out_specs=block,
        out_shape=jax.ShapeDtypeStruct(gate.shape, BF16),
        scratch_shapes=[pltpu.VMEM((n_parts, packed * rows, lanes), F32)],
        input_output_aliases={2 * n_parts + 4: 0} if earlier else {},
        compiler_params=PARAMS,
        cost_estimate=at_least(
            count * gate.shape[1] * hidden * gate.shape[2],
            count * gate.shape[1],
            *[jax.ShapeDtypeStruct(x.shape[1:], x.dtype) for x, _ in parts],
        ),
        name="finish",
    )(*[x for x, _ in parts], gate, weights, gain, bias, *earlier)


def after(value, *others):
    return lax.optimization_barrier((value,) + others)[0]


def on_device(n_row, n_col, pair_act, ln_gain, ln_bias, w_proj, w_gate, out_gain, out_bias, w_out):
    tile_rows, tile_cols, channels = pair_act.shape
    hidden = w_proj.shape[1] // 4
    half = n_col // 2
    top = n_row // 2
    share = n_row // n_col
    row, col = lax.axis_index("row"), lax.axis_index("col")
    axes = ("row", "col")
    place = lambda r, c: r * n_col + c
    chunks = min(CHUNKS, tile_rows // 16)
    step = tile_rows // chunks
    group = group_of(step)
    packed = hidden // group

    halves = (w_proj * 0.5).astype(BF16).T
    centre = (jnp.eye(channels, dtype=F32) - 1.0 / channels).astype(BF16)
    mean = jnp.full((2 * channels, channels), 1.0 / channels, BF16)
    half_gate = (w_gate * 0.5).astype(BF16)
    by_hidden = lambda v: jnp.repeat(v.reshape(packed, group), step, axis=1)[:, None, :]
    gain_out, bias_out = by_hidden(out_gain), by_hidden(out_bias)
    w_last = w_out.reshape(packed, group, channels).swapaxes(0, 1).reshape(hidden, channels)

    def holds(r, c):
        return (r // share) % half == c % half

    def across_top(near):
        pairs = [(place(r, c), place(r ^ top, c)) for r in range(n_row) for c in range(n_col) if holds(r, c)]
        return lax.ppermute(near, axes, pairs)

    def to_all_rows(held):
        bit = top // 2
        while bit >= share:
            alike = (bit * 2 - 1) & ~(share - 1)
            sends = [
                (place(r, c), place(r ^ bit, c))
                for r in range(n_row)
                for c in range(n_col)
                if (r ^ (c * share)) & alike == 0
            ]
            came = lax.ppermute(held, axes, sends)
            if bit == 1:
                return [[held, came]]
            held = jnp.where(((row ^ (col * share)) & bit) == 0, held, came)
            bit //= 2
        slabs = [held]
        while bit >= 1:
            swap = [(r, r ^ bit) for r in range(n_row)]
            others = [lax.ppermute(x, "row", swap) for x in slabs]
            slabs = [jnp.where((row & bit) == 0, a, b) for a, b in zip(slabs + others, others + slabs)]
            bit //= 2
        return [[x] for x in slabs]

    near_is_own = (row // top) == (col // half)
    swap_half = [(c, c ^ half) for c in range(n_col)]
    lefts, nears, fars, units = [], [], [], []

    def product(pairs, own):
        take_near = near_is_own if own else jnp.logical_not(near_is_own)
        which = jnp.where(take_near, 0, len(nears[0][0]))
        if share == 1 and top > 1:
            which = which + ((row ^ col) & 1)
        used_left = sorted({i for i, _, _ in pairs})
        used_right = sorted({(j, s) for _, j, s in pairs})
        return triangle(
            [lefts[i] for i in used_left],
            [units[j][s] for j, s in used_right],
            [(used_left.index(i), used_right.index((j, s))) for i, j, s in pairs],
            which.astype(jnp.int32).reshape(1),
        )

    wide = lambda v: jnp.broadcast_to(v[:, None], (channels, half * tile_cols))
    gain_in, bias_in = wide(ln_gain), wide(ln_bias)
    shards = range(share)
    waves = []
    for t in range(chunks):
        by_column = [(i, t, s) for i in range(t) for s in shards]
        by_row = [(t, j, s) for j in range(t + 1) for s in shards]
        waves.append([by_column, by_row] if t == chunks - 1 and t else [by_column + by_row])

    exchanged, arrived, own_parts, sent_parts = [], {}, {}, {}

    def exchange(t):
        block = pair_act[t * step : (t + 1) * step]
        if exchanged:
            block = after(block, exchanged[-1][-1])
        exchanged.append([lax.ppermute(block, "col", [(c, c ^ o) for c in range(n_col)]) for o in range(1, half)])

    def prepare(t, *held):
        exchange(t)
        scale = after(gain_in, *held) if held else gain_in
        left, right = project(
            [pair_act] + exchanged[t],
            [t * step] + [0] * (half - 1),
            step,
            halves,
            centre,
            scale,
            bias_in,
        )
        lefts.append(left)
        fars.append(across_top(right))
        nears.append(to_all_rows(right))
        return left

    def complete(t):
        waits = nears[t + 1][-1][-1:] if t + 1 < len(nears) else []
        far = to_all_rows(after(fars[t], *waits))
        units.append([a + b for a, b in zip(nears[t], far)])

    ahead = 2
    token = []
    moved = []
    for t in range(min(ahead, chunks)):
        token = [prepare(t, *token)]
    for t in range(chunks):
        complete(t)
        for pairs in waves[t]:
            lefts[t] = after(lefts[t], *token)
            made = product(pairs, False)
            token = [made]
            moved.append(lax.ppermute(made, "col", swap_half))
            for n, pair in enumerate(pairs):
                sent_parts[pair] = (moved[-1], n)
        if t + ahead < chunks:
            token = [prepare(t + ahead, *token, *(moved[t - 1 : t] if t in (1, 2) else []))]
    for t in range(chunks):
        pairs = [pair for part in waves[t] for pair in part]
        if t == 0 and chunks > 3:
            token = token + [moved[chunks - 3]]
        if t == chunks // 2:
            token = token + [moved[chunks - 2]]
        lefts[t] = after(lefts[t], *token)
        made = product(pairs, True)
        token = [made]
        for n, pair in enumerate(pairs):
            own_parts[pair] = (made, n)
    gate = gate_of(pair_act, centre, mean, after(ln_gain[None], *token), ln_bias[None], half_gate)
    out = None
    for i in range(chunks):
        pairs = [(i, j, s) for s in shards for j in range(chunks)]
        out = finish(
            [own_parts[pair] for pair in pairs],
            [sent_parts[pair] for pair in pairs],
            gate,
            i * step,
            w_last,
            gain_out,
            bias_out,
            out,
        )
    return out


def solution(mesh):
    n_row, n_col = mesh.shape["row"], mesh.shape["col"]
    in_specs = (P(("groups", "row"), "col", None), P(), P(), P(), P(), P(), P(), P())
    out_specs = P(("groups", "row"), "col", None)
    return jax.shard_map(
        functools.partial(on_device, n_row, n_col),
        mesh=mesh,
        in_specs=in_specs,
        out_specs=out_specs,
        check_vma=False,
    )
```

```python
import functools
import math

import jax
import jax.numpy as jnp
from jax import lax
from jax.experimental import pallas as pl
from jax.experimental.pallas import tpu as pltpu
from jax.sharding import PartitionSpec as P

CHUNKS = 6
EPS = 1e-05
F32, BF16 = jnp.float32, jnp.bfloat16
PARAMS = pltpu.CompilerParams(vmem_limit_bytes=52 * 1024 * 1024)


def contract(left, right, left_dim, right_dim):
    return lax.dot_general(
        left, right, (((left_dim,), (right_dim,)), ((), ())), preferred_element_type=F32
    )


def at_least(macs, transcendentals, *arrays):
    return pl.CostEstimate(
        flops=2 * macs,
        transcendentals=transcendentals,
        bytes_accessed=sum(math.prod(x.shape) * x.dtype.itemsize for x in arrays),
    )


def swap_eight(arrays):
    place = lax.broadcasted_iota(jnp.int32, arrays[0].shape, 1)
    for shift in (4, 2, 1):
        low = (place & shift) == 0
        swapped = list(arrays)
        for n in range(8):
            if n & shift == 0:
                one, two = arrays[n], arrays[n + shift]
                swapped[n] = jnp.where(low, one, pltpu.roll(two, shift, 1))
                swapped[n + shift] = jnp.where(low, pltpu.roll(one, 8 - shift, 1), two)
        arrays = swapped
    return arrays


def project_kernel(n_pieces, *refs):
    pieces, (weights, centre, gain, bias, left_out, right_out, left_rows, right_rows) = (
        refs[:n_pieces],
        refs[n_pieces:],
    )
    eights, _, rows, depth = left_out.shape
    hidden = eights * 8

    def one_row(i, carry):
        values = jnp.concatenate([piece[i] for piece in pieces], axis=0)
        centred = contract(centre[...], values, 1, 1)
        variance = jnp.mean(centred * centred, axis=0, keepdims=True)
        normed = centred * lax.rsqrt(variance + EPS) * gain[...] + bias[...]
        halved = contract(weights[...], normed.astype(BF16), 1, 0)
        for first, held in ((0, left_rows), (2 * hidden, right_rows)):
            gate, value = halved[first : first + hidden], halved[first + hidden : first + 2 * hidden]
            held[i] = value + value * jnp.tanh(gate)
        return carry

    lax.fori_loop(0, rows, one_row, 0, unroll=4)

    def one_group(e, carry):
        at = pl.ds(pl.multiple_of(e * 8, 8), 8)
        for held, out in ((left_rows, left_out), (right_rows, right_out)):
            for n in range(depth // 128):
                lanes = slice(n * 128, (n + 1) * 128)
                halves = [
                    swap_eight([held[first + i, at, lanes][None] for i in range(8)]) for first in range(0, rows, 8)
                ]
                for h in range(8):
                    out[e, h, :, lanes] = jnp.concatenate([half[h][0] for half in halves], axis=0).astype(BF16)
        return carry

    lax.fori_loop(0, eights, one_group, 0, unroll=2)


def project(pieces, firsts, count, weights, centre, gain, bias):
    rows = 16
    hidden = weights.shape[0] // 4
    channels = weights.shape[1]
    depth = sum(piece.shape[1] for piece in pieces)
    whole = lambda x: pl.BlockSpec(x.shape, lambda i: (0,) * x.ndim)
    in_specs = [
        pl.BlockSpec((rows, piece.shape[1], channels), functools.partial(lambda f, i: (i + f, 0, 0), first // rows))
        for piece, first in zip(pieces, firsts)
    ] + [whole(x) for x in (weights, centre, gain, bias)]
    shape = jax.ShapeDtypeStruct((hidden // 8, 8, count, depth), BF16)
    left, right = pl.pallas_call(
        functools.partial(project_kernel, len(pieces)),
        grid=(count // rows,),
        in_specs=in_specs,
        out_specs=[pl.BlockSpec((hidden // 8, 8, rows, depth), lambda i: (0, 0, i, 0))] * 2,
        out_shape=[shape, shape],
        scratch_shapes=[pltpu.VMEM((rows, hidden, depth), F32)] * 2,
        compiler_params=PARAMS,
        cost_estimate=at_least(
            count * depth * channels * (channels + 4 * hidden), 2 * count * depth * hidden, shape, shape
        ),
        name="project",
    )(*pieces, weights, centre, gain, bias)
    return left.reshape(hidden, count, depth), right.reshape(hidden, count, depth)


def triangle_kernel(n_left, n_sides, group, pairs, which, *refs):
    lefts, out = refs[:n_left], refs[-1]
    sides = refs[n_left:-1]
    step = lefts[0].shape[0]

    def go(choice):
        for first in range(0, step, group):
            for n, (i, j) in enumerate(pairs):
                side = sides[j * n_sides + choice]
                parts = [contract(lefts[i][h], side[h], 1, 1) for h in range(first, first + group)]
                out[n, first // group] = jnp.concatenate(parts, axis=-1).astype(BF16)

    for n in range(n_sides):
        pl.when(which[0] == n)(functools.partial(go, n))


def group_of(columns):
    return 128 // math.gcd(columns, 128)


def triangle(lefts, rights, pairs, which):
    hidden, rows, depth = lefts[0].shape
    columns = rights[0][0].shape[1]
    n_sides = len(rights[0])
    group = group_of(columns)
    step = max(8, group)
    shape = jax.ShapeDtypeStruct((len(pairs), hidden // group, rows, group * columns), BF16)

    def side_spec(n):
        return pl.BlockSpec((step, columns, depth), lambda h, which: (jnp.where(which[0] == n, h, 0), 0, 0))

    return pl.pallas_call(
        functools.partial(triangle_kernel, len(lefts), n_sides, group, pairs),
        grid_spec=pltpu.PrefetchScalarGridSpec(
            num_scalar_prefetch=1,
            grid=(hidden // step,),
            in_specs=[pl.BlockSpec((step, rows, depth), lambda h, which: (h, 0, 0))] * len(lefts)
            + [side_spec(n) for _ in rights for n in range(n_sides)],
            out_specs=pl.BlockSpec(
                (len(pairs), step // group, rows, group * columns), lambda h, which: (0, h, 0, 0)
            ),
        ),
        out_shape=shape,
        compiler_params=PARAMS,
        cost_estimate=at_least(
            len(pairs) * hidden * rows * columns * depth, 0, shape, *lefts, *[side[0] for side in rights]
        ),
        name="triangle",
    )(which, *lefts, *[x for side in rights for x in side])


def gate_kernel(pair, centre, mean, gain, bias, weights, out):
    rows, columns, channels = pair.shape
    values = pair[...].reshape(rows * columns, channels)
    centred = contract(values, centre[...], 1, 0)
    square = centred * centred
    high = square.astype(BF16)
    low = (square - high.astype(F32)).astype(BF16)
    variance = contract(jnp.concatenate([high, low], axis=1), mean[...], 1, 0)
    normed = (centred * lax.rsqrt(variance + EPS) * gain[...] + bias[...]).astype(BF16)
    gate = 0.5 + 0.5 * jnp.tanh(contract(normed, weights[...], 1, 0))
    out[...] = gate.astype(BF16).reshape(rows, columns, channels)


def gate_of(pair, centre, mean, gain, bias, weights):
    rows = 8
    count, columns, channels = pair.shape
    whole = lambda x: pl.BlockSpec(x.shape, lambda i: (0,) * x.ndim)
    block = pl.BlockSpec((rows, columns, channels), lambda i: (i, 0, 0))
    return pl.pallas_call(
        gate_kernel,
        grid=(count // rows,),
        in_specs=[block] + [whole(x) for x in (centre, mean, gain, bias, weights)],
        out_specs=block,
        out_shape=jax.ShapeDtypeStruct(pair.shape, BF16),
        compiler_params=PARAMS,
        cost_estimate=at_least(
            count * columns * channels * 4 * channels, count * columns * channels, pair, pair
        ),
        name="gate",
    )(pair, centre, mean, gain, bias, weights)


def finish_kernel(n_parts, group, hidden, *refs):
    own, sent = refs[:n_parts], refs[n_parts : 2 * n_parts]
    gate, weights, gain, bias = refs[2 * n_parts : 2 * n_parts + 4]
    out, rows_of = refs[-2:]
    packed, rows, lanes = own[0].shape
    columns = lanes // group

    def over_hidden(x):
        total = jnp.sum(x, axis=0)
        shift = columns
        while shift < lanes:
            total = total + pltpu.roll(total, shift, 1)
            shift *= 2
        return total * (1.0 / hidden)

    for n in range(n_parts):
        total = own[n][...].astype(F32) + sent[n][...].astype(F32)
        centred = total - over_hidden(total)[None]
        scale = lax.rsqrt(over_hidden(centred * centred) + EPS)
        normed = centred * scale[None] * gain[...] + bias[...]
        rows_of[n] = normed.reshape(packed * rows, lanes)
    for i in range(rows):
        parts = []
        for n in range(n_parts):
            held = rows_of[n, pl.ds(i, packed, stride=rows), :]
            parts.append(
                jnp.concatenate([held[:, g * columns : (g + 1) * columns] for g in range(group)], axis=0)
            )
        normed = jnp.concatenate(parts, axis=1).astype(BF16)
        result = contract(normed, weights[...], 0, 0)
        out[i] = (result * gate[i].astype(F32)).astype(BF16)


def finish(own, sent, gate, first, weights, gain, bias, held):
    rows = 16
    _, packed, count, lanes = own[0][0].shape
    hidden = weights.shape[0]
    group = hidden // packed
    whole = lambda x: pl.BlockSpec(x.shape, lambda i: (0,) * x.ndim)
    part = lambda n: pl.BlockSpec((None, packed, rows, lanes), lambda i: (n, 0, i, 0))
    block = pl.BlockSpec((rows,) + gate.shape[1:], lambda i: (i + first // rows, 0, 0))
    n_parts = len(own)
    parts = own + sent
    earlier = [] if held is None else [held]
    return pl.pallas_call(
        functools.partial(finish_kernel, n_parts, group, hidden),
        grid=(count // rows,),
        in_specs=[part(n) for _, n in parts]
        + [block, whole(weights), whole(gain), whole(bias)]
        + [pl.BlockSpec(memory_space=pl.ANY)] * len(earlier),
        out_specs=block,
        out_shape=jax.ShapeDtypeStruct(gate.shape, BF16),
        scratch_shapes=[pltpu.VMEM((n_parts, packed * rows, lanes), F32)],
        input_output_aliases={2 * n_parts + 4: 0} if earlier else {},
        compiler_params=PARAMS,
        cost_estimate=at_least(
            count * gate.shape[1] * hidden * gate.shape[2],
            count * gate.shape[1],
            *[jax.ShapeDtypeStruct(x.shape[1:], x.dtype) for x, _ in parts],
        ),
        name="finish",
    )(*[x for x, _ in parts], gate, weights, gain, bias, *earlier)


def after(value, *others):
    return lax.optimization_barrier((value,) + others)[0]


def on_device(n_row, n_col, pair_act, ln_gain, ln_bias, w_proj, w_gate, out_gain, out_bias, w_out):
    tile_rows, tile_cols, channels = pair_act.shape
    hidden = w_proj.shape[1] // 4
    half = n_col // 2
    top = n_row // 2
    share = n_row // n_col
    row, col = lax.axis_index("row"), lax.axis_index("col")
    axes = ("row", "col")
    place = lambda r, c: r * n_col + c
    chunks = min(CHUNKS, tile_rows // 16)
    step = tile_rows // chunks
    group = group_of(step)
    packed = hidden // group

    halves = (w_proj * 0.5).astype(BF16).T
    centre = (jnp.eye(channels, dtype=F32) - 1.0 / channels).astype(BF16)
    mean = jnp.full((2 * channels, channels), 1.0 / channels, BF16)
    half_gate = (w_gate * 0.5).astype(BF16)
    by_hidden = lambda v: jnp.repeat(v.reshape(packed, group), step, axis=1)[:, None, :]
    gain_out, bias_out = by_hidden(out_gain), by_hidden(out_bias)
    w_last = w_out.reshape(packed, group, channels).swapaxes(0, 1).reshape(hidden, channels)

    def holds(r, c):
        return (r // share) % half == c % half

    def across_top(near):
        pairs = [(place(r, c), place(r ^ top, c)) for r in range(n_row) for c in range(n_col) if holds(r, c)]
        return lax.ppermute(near, axes, pairs)

    def to_all_rows(held):
        bit = top // 2
        while bit >= share:
            alike = (bit * 2 - 1) & ~(share - 1)
            sends = [
                (place(r, c), place(r ^ bit, c))
                for r in range(n_row)
                for c in range(n_col)
                if (r ^ (c * share)) & alike == 0
            ]
            came = lax.ppermute(held, axes, sends)
            if bit == 1:
                return [[held, came]]
            held = jnp.where(((row ^ (col * share)) & bit) == 0, held, came)
            bit //= 2
        slabs = [held]
        while bit >= 1:
            swap = [(r, r ^ bit) for r in range(n_row)]
            others = [lax.ppermute(x, "row", swap) for x in slabs]
            slabs = [jnp.where((row & bit) == 0, a, b) for a, b in zip(slabs + others, others + slabs)]
            bit //= 2
        return [[x] for x in slabs]

    near_is_own = (row // top) == (col // half)
    swap_half = [(c, c ^ half) for c in range(n_col)]
    two_chips = share == 1 and top == 2
    holder = ((row ^ col) & 1) == 0
    lefts, rights, fars, units = [], [], [], []

    def first_step(right):
        if not two_chips:
            return across_top(right)
        pairs = [(place(r, c), place(r ^ top ^ 1, c)) for r in range(n_row) for c in range(n_col) if holds(r, c)]
        return lax.ppermute(right, axes, pairs)

    def second_step(right, far, *waits):
        if not two_chips:
            return [a + b for a, b in zip(to_all_rows(right), to_all_rows(far))]
        given = jnp.where(holder, right, after(far, *waits))
        got = lax.ppermute(given, "row", [(r, r ^ 1) for r in range(n_row)])
        return [[right, got, far]]

    def product(pairs, own):
        take_near = near_is_own if own else jnp.logical_not(near_is_own)
        if two_chips:
            which = jnp.where(holder, 0, 1) + jnp.where(take_near, 0, 1)
        else:
            which = jnp.where(take_near, 0, 1)
        used_left = sorted({i for i, _, _ in pairs})
        used_right = sorted({(j, s) for _, j, s in pairs})
        return triangle(
            [lefts[i] for i in used_left],
            [units[j][s] for j, s in used_right],
            [(used_left.index(i), used_right.index((j, s))) for i, j, s in pairs],
            which.astype(jnp.int32).reshape(1),
        )

    wide = lambda v: jnp.broadcast_to(v[:, None], (channels, half * tile_cols))
    gain_in, bias_in = wide(ln_gain), wide(ln_bias)
    shards = range(share)
    waves = []
    for t in range(chunks):
        by_column = [(i, t, s) for i in range(t) for s in shards]
        by_row = [(t, j, s) for j in range(t + 1) for s in shards]
        waves.append([by_column, by_row] if t == chunks - 1 and t else [by_column + by_row])

    exchanged, arrived, own_parts, sent_parts = [], {}, {}, {}

    def prepare(t, *held):
        left, right = project(
            [pair_act] + exchanged[t],
            [t * step] + [0] * (half - 1),
            step,
            halves,
            centre,
            after(gain_in, *held) if held else gain_in,
            bias_in,
        )
        lefts.append(left)
        rights.append(right)
        return left

    def exchange(n, *waits):
        block = pair_act[n * step : (n + 1) * step]
        block = after(block, *waits) if waits else block
        exchanged.append([lax.ppermute(block, "col", [(c, c ^ o) for c in range(n_col)]) for o in range(1, half)])

    exchange(0)
    token = []
    moved = []
    for n in range(chunks + 2):
        waits = token + (exchanged[n][-1:] if n < chunks else []) + (moved[n - 4 : n - 3] if n >= 4 else [])
        if n + 1 < chunks:
            exchange(n + 1, *waits)
        if 0 < n <= chunks:
            fars.append(first_step(after(rights[n - 1], *waits)))
        if n >= 2:
            units.append(second_step(rights[n - 2], fars[n - 2], *waits))
        if n < chunks:
            token = [prepare(n, *token)]
        if n >= 2:
            t = n - 2
            for pairs in waves[t]:
                lefts[t] = after(lefts[t], *token)
                made = product(pairs, False)
                token = [made]
                waits = moved[t - 1 : t] if t < chunks - 1 else []
                moved.append(lax.ppermute(after(made, *waits) if waits else made, "col", swap_half))
                for p, pair in enumerate(pairs):
                    sent_parts[pair] = (moved[-1], p)
    for t in range(chunks):
        pairs = [pair for part in waves[t] for pair in part]
        lefts[t] = after(lefts[t], *token)
        made = product(pairs, True)
        token = [made]
        for n, pair in enumerate(pairs):
            own_parts[pair] = (made, n)
    gate = gate_of(pair_act, centre, mean, after(ln_gain[None], *token), ln_bias[None], half_gate)
    out = None
    for i in range(chunks):
        pairs = [(i, j, s) for s in shards for j in range(chunks)]
        out = finish(
            [own_parts[pair] for pair in pairs],
            [sent_parts[pair] for pair in pairs],
            gate,
            i * step,
            w_last,
            gain_out,
            bias_out,
            out,
        )
    return out


def solution(mesh):
    n_row, n_col = mesh.shape["row"], mesh.shape["col"]
    in_specs = (P(("groups", "row"), "col", None), P(), P(), P(), P(), P(), P(), P())
    out_specs = P(("groups", "row"), "col", None)
    return jax.shard_map(
        functools.partial(on_device, n_row, n_col),
        mesh=mesh,
        in_specs=in_specs,
        out_specs=out_specs,
        check_vma=False,
    )
```

```python
import functools
import math

import jax
import jax.numpy as jnp
from jax import lax
from jax.experimental import pallas as pl
from jax.experimental.pallas import tpu as pltpu
from jax.sharding import PartitionSpec as P

CHUNKS = 6
EPS = 1e-05
F32, BF16 = jnp.float32, jnp.bfloat16
PARAMS = pltpu.CompilerParams(vmem_limit_bytes=52 * 1024 * 1024)


def sigmoid(x):
    return pl.reciprocal(1.0 + jnp.exp(-x), approx=True)


def contract(left, right, left_dim, right_dim):
    return lax.dot_general(
        left, right, (((left_dim,), (right_dim,)), ((), ())), preferred_element_type=F32
    )


def at_least(macs, transcendentals, *arrays):
    return pl.CostEstimate(
        flops=2 * macs,
        transcendentals=transcendentals,
        bytes_accessed=sum(math.prod(x.shape) * x.dtype.itemsize for x in arrays),
    )


def swap_eight(arrays):
    place = lax.broadcasted_iota(jnp.int32, arrays[0].shape, 1)
    for shift in (4, 2, 1):
        low = (place & shift) == 0
        swapped = list(arrays)
        for n in range(8):
            if n & shift == 0:
                one, two = arrays[n], arrays[n + shift]
                swapped[n] = jnp.where(low, one, pltpu.roll(two, shift, 1))
                swapped[n + shift] = jnp.where(low, pltpu.roll(one, 8 - shift, 1), two)
        arrays = swapped
    return arrays


def project_kernel(n_pieces, *refs):
    pieces, (weights, centre, gain, bias, left_out, right_out, left_rows, right_rows) = (
        refs[:n_pieces],
        refs[n_pieces:],
    )
    eights, _, rows, depth = left_out.shape
    hidden = eights * 8

    def one_row(i, carry):
        values = jnp.concatenate([piece[i] for piece in pieces], axis=0)
        centred = contract(centre[...], values, 1, 1)
        variance = jnp.mean(centred * centred, axis=0, keepdims=True)
        normed = centred * lax.rsqrt(variance + EPS) * gain[...] + bias[...]
        projected = contract(weights[...], normed.astype(BF16), 1, 0)
        for first, held in ((0, left_rows), (2 * hidden, right_rows)):
            gate = projected[first : first + hidden]
            held[i] = sigmoid(gate) * projected[first + hidden : first + 2 * hidden]
        return carry

    lax.fori_loop(0, rows, one_row, 0, unroll=4)

    def one_group(e, carry):
        at = pl.ds(pl.multiple_of(e * 8, 8), 8)
        for held, out in ((left_rows, left_out), (right_rows, right_out)):
            for n in range(depth // 128):
                lanes = slice(n * 128, (n + 1) * 128)
                halves = [
                    swap_eight([held[first + i, at, lanes][None] for i in range(8)]) for first in range(0, rows, 8)
                ]
                for h in range(8):
                    out[e, h, :, lanes] = jnp.concatenate([half[h][0] for half in halves], axis=0).astype(BF16)
        return carry

    lax.fori_loop(0, eights, one_group, 0, unroll=2)


def project(pieces, firsts, count, weights, centre, gain, bias):
    rows = 16
    hidden = weights.shape[0] // 4
    channels = weights.shape[1]
    depth = sum(piece.shape[1] for piece in pieces)
    whole = lambda x: pl.BlockSpec(x.shape, lambda i: (0,) * x.ndim)
    in_specs = [
        pl.BlockSpec((rows, piece.shape[1], channels), functools.partial(lambda f, i: (i + f, 0, 0), first // rows))
        for piece, first in zip(pieces, firsts)
    ] + [whole(x) for x in (weights, centre, gain, bias)]
    shape = jax.ShapeDtypeStruct((hidden // 8, 8, count, depth), BF16)
    left, right = pl.pallas_call(
        functools.partial(project_kernel, len(pieces)),
        grid=(count // rows,),
        in_specs=in_specs,
        out_specs=[pl.BlockSpec((hidden // 8, 8, rows, depth), lambda i: (0, 0, i, 0))] * 2,
        out_shape=[shape, shape],
        scratch_shapes=[pltpu.VMEM((rows, hidden, depth), F32)] * 2,
        compiler_params=PARAMS,
        cost_estimate=at_least(
            count * depth * channels * (channels + 4 * hidden), 2 * count * depth * hidden, shape, shape
        ),
        name="project",
    )(*pieces, weights, centre, gain, bias)
    return left.reshape(hidden, count, depth), right.reshape(hidden, count, depth)


def triangle_kernel(n_left, n_sides, group, pairs, which, *refs):
    lefts, out = refs[:n_left], refs[-1]
    sides = refs[n_left:-1]
    step = lefts[0].shape[0]

    def go(choice):
        def one_group(g, carry):
            for n, (i, j) in enumerate(pairs):
                side = sides[j * n_sides + choice]
                parts = [contract(lefts[i][g * group + h], side[g * group + h], 1, 1) for h in range(group)]
                out[n, g] = jnp.concatenate(parts, axis=-1).astype(BF16)
            return carry

        lax.fori_loop(0, step // group, one_group, 0, unroll=2)

    for n in range(n_sides):
        pl.when(which[0] == n)(functools.partial(go, n))


def group_of(columns):
    return 128 // math.gcd(columns, 128)


def triangle(lefts, rights, pairs, which):
    hidden, rows, depth = lefts[0].shape
    columns = rights[0][0].shape[1]
    n_sides = len(rights[0])
    group = group_of(columns)
    step = max(16 if len(rights) > 3 else 32, group)
    shape = jax.ShapeDtypeStruct((len(pairs), hidden // group, rows, group * columns), BF16)

    def side_spec(n):
        return pl.BlockSpec((step, columns, depth), lambda h, which: (jnp.where(which[0] == n, h, 0), 0, 0))

    return pl.pallas_call(
        functools.partial(triangle_kernel, len(lefts), n_sides, group, pairs),
        grid_spec=pltpu.PrefetchScalarGridSpec(
            num_scalar_prefetch=1,
            grid=(hidden // step,),
            in_specs=[pl.BlockSpec((step, rows, depth), lambda h, which: (h, 0, 0))] * len(lefts)
            + [side_spec(n) for _ in rights for n in range(n_sides)],
            out_specs=pl.BlockSpec(
                (len(pairs), step // group, rows, group * columns), lambda h, which: (0, h, 0, 0)
            ),
        ),
        out_shape=shape,
        compiler_params=PARAMS,
        cost_estimate=at_least(
            len(pairs) * hidden * rows * columns * depth, 0, shape, *lefts, *[side[0] for side in rights]
        ),
        name="triangle",
    )(which, *lefts, *[x for side in rights for x in side])


def gate_kernel(pair, centre, mean, gain, bias, weights, out):
    rows, columns, channels = pair.shape
    values = pair[...].reshape(rows * columns, channels)
    centred = contract(values, centre[...], 1, 0)
    square = centred * centred
    high = square.astype(BF16)
    low = (square - high.astype(F32)).astype(BF16)
    variance = contract(jnp.concatenate([high, low], axis=1), mean[...], 1, 0)
    normed = (centred * lax.rsqrt(variance + EPS) * gain[...] + bias[...]).astype(BF16)
    gate = sigmoid(contract(normed, weights[...], 1, 0))
    out[...] = gate.astype(BF16).reshape(rows, columns, channels)


def gate_of(pair, centre, mean, gain, bias, weights):
    rows = 8
    count, columns, channels = pair.shape
    whole = lambda x: pl.BlockSpec(x.shape, lambda i: (0,) * x.ndim)
    block = pl.BlockSpec((rows, columns, channels), lambda i: (i, 0, 0))
    return pl.pallas_call(
        gate_kernel,
        grid=(count // rows,),
        in_specs=[block] + [whole(x) for x in (centre, mean, gain, bias, weights)],
        out_specs=block,
        out_shape=jax.ShapeDtypeStruct(pair.shape, BF16),
        compiler_params=PARAMS,
        cost_estimate=at_least(
            count * columns * channels * 4 * channels, count * columns * channels, pair, pair
        ),
        name="gate",
    )(pair, centre, mean, gain, bias, weights)


def finish_kernel(group, hidden, own, sent, gate, weights, gain, bias, *refs):
    out, rows_of = refs[-2:]
    packed, rows, lanes = own.shape
    columns = lanes // group

    def over_hidden(x):
        total = jnp.sum(x, axis=0)
        shift = columns
        while shift < lanes:
            total = total + pltpu.roll(total, shift, 1)
            shift *= 2
        return total * (1.0 / hidden)

    total = own[...].astype(F32) + sent[...].astype(F32)
    centred = total - over_hidden(total)[None]
    scale = lax.rsqrt(over_hidden(centred * centred) + EPS)
    normed = centred * scale[None] * gain[...] + bias[...]
    rows_of[...] = normed.reshape(packed * rows, lanes)
    for i in range(rows):
        held = rows_of[pl.ds(i, packed, stride=rows), :]
        parts = [held[:, g * columns : (g + 1) * columns] for g in range(group)]
        result = contract(jnp.concatenate(parts, axis=0).astype(BF16), weights[...], 0, 0)
        out[i] = (result * gate[i].astype(F32)).astype(BF16)


def finish(own, sent, gate, t, chunks, share, weights, gain, bias, held):
    rows = 16
    pieces, packed, count, lanes = own.shape
    hidden, channels = weights.shape
    group = hidden // packed
    steps = count // rows
    before = t * share

    def row_of(p):
        return jnp.where(p < before, p // share, t)

    def column_of(p):
        of_row = p - before
        return jnp.where(p < before, (p % share) * chunks + t, (of_row % share) * chunks + of_row // share)

    whole = lambda x: pl.BlockSpec(x.shape, lambda p, r: (0,) * x.ndim)
    part = pl.BlockSpec((None, packed, rows, lanes), lambda p, r: (p, 0, r, 0))
    block = pl.BlockSpec((rows, lanes // group, channels), lambda p, r: (row_of(p) * steps + r, column_of(p), 0))
    earlier = [] if held is None else [held]
    return pl.pallas_call(
        functools.partial(finish_kernel, group, hidden),
        grid=(pieces, steps),
        in_specs=[part, part, block, whole(weights), whole(gain), whole(bias)]
        + [pl.BlockSpec(memory_space=pl.ANY)] * len(earlier),
        out_specs=block,
        out_shape=jax.ShapeDtypeStruct(gate.shape, BF16),
        scratch_shapes=[pltpu.VMEM((packed * rows, lanes), F32)],
        input_output_aliases={6: 0} if earlier else {},
        compiler_params=PARAMS,
        cost_estimate=at_least(
            pieces * count * (lanes // group) * hidden * channels, pieces * count * (lanes // group), own, sent
        ),
        name="finish",
    )(own, sent, gate, weights, gain, bias, *earlier)


def after(value, *others):
    return lax.optimization_barrier((value,) + others)[0]


def on_device(n_row, n_col, pair_act, ln_gain, ln_bias, w_proj, w_gate, out_gain, out_bias, w_out):
    tile_rows, tile_cols, channels = pair_act.shape
    hidden = w_proj.shape[1] // 4
    half = n_col // 2
    top = n_row // 2
    share = n_row // n_col
    row, col = lax.axis_index("row"), lax.axis_index("col")
    axes = ("row", "col")
    place = lambda r, c: r * n_col + c
    chunks = min(CHUNKS, tile_rows // 16)
    step = tile_rows // chunks
    group = group_of(step)
    packed = hidden // group

    w_sides = w_proj.T
    centre = (jnp.eye(channels, dtype=F32) - 1.0 / channels).astype(BF16)
    mean = jnp.full((2 * channels, channels), 1.0 / channels, BF16)
    by_hidden = lambda v: jnp.repeat(v.reshape(packed, group), step, axis=1)[:, None, :]
    gain_out, bias_out = by_hidden(out_gain), by_hidden(out_bias)
    w_last = w_out.reshape(packed, group, channels).swapaxes(0, 1).reshape(hidden, channels)

    def holds(r, c):
        return (r // share) % half == c % half

    def across_top(near):
        pairs = [(place(r, c), place(r ^ top, c)) for r in range(n_row) for c in range(n_col) if holds(r, c)]
        return lax.ppermute(near, axes, pairs)

    def to_all_rows(held):
        bit = top // 2
        while bit >= share:
            alike = (bit * 2 - 1) & ~(share - 1)
            sends = [
                (place(r, c), place(r ^ bit, c))
                for r in range(n_row)
                for c in range(n_col)
                if (r ^ (c * share)) & alike == 0
            ]
            came = lax.ppermute(held, axes, sends)
            if bit == 1:
                return [[held, came]]
            held = jnp.where(((row ^ (col * share)) & bit) == 0, held, came)
            bit //= 2
        slabs = [held]
        while bit >= 1:
            swap = [(r, r ^ bit) for r in range(n_row)]
            others = [lax.ppermute(x, "row", swap) for x in slabs]
            slabs = [jnp.where((row & bit) == 0, a, b) for a, b in zip(slabs + others, others + slabs)]
            bit //= 2
        return [[x] for x in slabs]

    near_is_own = (row // top) == (col // half)
    swap_half = [(c, c ^ half) for c in range(n_col)]
    two_chips = share == 1 and top == 2
    holder = ((row ^ col) & 1) == 0
    lefts, rights, fars, units = [], [], [], []

    def first_step(right):
        if not two_chips:
            return across_top(right)
        pairs = [(place(r, c), place(r ^ top ^ 1, c)) for r in range(n_row) for c in range(n_col) if holds(r, c)]
        return lax.ppermute(right, axes, pairs)

    def second_step(right, far, *waits):
        if not two_chips:
            return [a + b for a, b in zip(to_all_rows(right), to_all_rows(far))]
        given = jnp.where(holder, right, after(far, *waits))
        got = lax.ppermute(given, "row", [(r, r ^ 1) for r in range(n_row)])
        return [[right, got, far]]

    def product(pairs, own):
        take_near = near_is_own if own else jnp.logical_not(near_is_own)
        if two_chips:
            which = jnp.where(holder, 0, 1) + jnp.where(take_near, 0, 1)
        else:
            which = jnp.where(take_near, 0, 1)
        used_left = sorted({i for i, _, _ in pairs})
        used_right = sorted({(j, s) for _, j, s in pairs})
        return triangle(
            [lefts[i] for i in used_left],
            [units[j][s] for j, s in used_right],
            [(used_left.index(i), used_right.index((j, s))) for i, j, s in pairs],
            which.astype(jnp.int32).reshape(1),
        )

    wide = lambda v: jnp.broadcast_to(v[:, None], (channels, half * tile_cols))
    gain_in, bias_in = wide(ln_gain), wide(ln_bias)
    shards = range(share)
    waves = []
    for t in range(chunks):
        by_column = [(i, t, s) for i in range(t) for s in shards]
        by_row = [(t, j, s) for j in range(t + 1) for s in shards]
        waves.append(by_column + by_row)

    exchanged = []

    def prepare(t, *held):
        left, right = project(
            [pair_act] + exchanged[t],
            [t * step] + [0] * (half - 1),
            step,
            w_sides,
            centre,
            after(gain_in, *held) if held else gain_in,
            bias_in,
        )
        lefts.append(left)
        rights.append(right)
        return left

    def exchange(n, *waits):
        block = (after(pair_act, *waits) if waits else pair_act)[n * step : (n + 1) * step]
        exchanged.append([lax.ppermute(block, "col", [(c, c ^ o) for c in range(n_col)]) for o in range(1, half)])

    def keep_own():
        t = len(own)
        lefts[t] = after(lefts[t], *token)
        own.append(product(waves[t], True))
        token[:] = own[-1:]

    exchange(0)
    token, moved, own = [], [], []
    for n in range(chunks + 2):
        waits = token + (exchanged[n][-1:] if n < chunks else []) + (moved[n - 4 : n - 3] if n >= 4 else [])
        if n + 1 < chunks:
            exchange(n + 1, *waits)
        if 0 < n <= chunks:
            fars.append(first_step(after(rights[n - 1], *waits)))
        if n >= 2:
            units.append(second_step(rights[n - 2], fars[n - 2], *waits))
        if n < chunks:
            token = [prepare(n, *token)]
        if n >= 2:
            t = n - 2
            if t == chunks - 1:
                while len(own) < t - 1:
                    keep_own()
            lefts[t] = after(lefts[t], *token)
            made = product(waves[t], False)
            token = [made]
            waits = moved[t - 1 : t]
            moved.append(lax.ppermute(after(made, *waits) if waits else made, "col", swap_half))
    while len(own) < chunks:
        keep_own()
    gate = gate_of(pair_act, centre, mean, after(ln_gain[None], *token), ln_bias[None], w_gate)
    out = None
    for t in range(chunks):
        out = finish(own[t], moved[t], gate, t, chunks, share, w_last, gain_out, bias_out, out)
    return out


def solution(mesh):
    n_row, n_col = mesh.shape["row"], mesh.shape["col"]
    in_specs = (P(("groups", "row"), "col", None), P(), P(), P(), P(), P(), P(), P())
    out_specs = P(("groups", "row"), "col", None)
    return jax.shard_map(
        functools.partial(on_device, n_row, n_col),
        mesh=mesh,
        in_specs=in_specs,
        out_specs=out_specs,
        check_vma=False,
    )
```

```python
import functools
import math

import jax
import jax.numpy as jnp
from jax import lax
from jax.experimental import pallas as pl
from jax.experimental.pallas import tpu as pltpu
from jax.sharding import PartitionSpec as P

CHUNKS = 6
EPS = 1e-05
F32, BF16 = jnp.float32, jnp.bfloat16
PARAMS = pltpu.CompilerParams(vmem_limit_bytes=52 * 1024 * 1024)


def sigmoid(x):
    return pl.reciprocal(1.0 + jnp.exp(-x), approx=True)


def contract(left, right, left_dim, right_dim):
    return lax.dot_general(
        left, right, (((left_dim,), (right_dim,)), ((), ())), preferred_element_type=F32
    )


def at_least(macs, transcendentals, *arrays):
    return pl.CostEstimate(
        flops=2 * macs,
        transcendentals=transcendentals,
        bytes_accessed=sum(math.prod(x.shape) * x.dtype.itemsize for x in arrays),
    )


def swap_eight(arrays):
    place = lax.broadcasted_iota(jnp.int32, arrays[0].shape, 1)
    for shift in (4, 2, 1):
        low = (place & shift) == 0
        swapped = list(arrays)
        for n in range(8):
            if n & shift == 0:
                one, two = arrays[n], arrays[n + shift]
                swapped[n] = jnp.where(low, one, pltpu.roll(two, shift, 1))
                swapped[n + shift] = jnp.where(low, pltpu.roll(one, 8 - shift, 1), two)
        arrays = swapped
    return arrays


def project_kernel(n_pieces, *refs):
    pieces, (weights, centre, gain, bias, left_out, right_out, left_rows, right_rows) = (
        refs[:n_pieces],
        refs[n_pieces:],
    )
    eights, _, rows, depth = left_out.shape
    hidden = eights * 8

    def two_rows(n, carry):
        values = jnp.concatenate([piece[2 * n + i] for i in range(2) for piece in pieces], axis=0)
        centred = contract(centre[...], values, 1, 1)
        variance = jnp.mean(centred * centred, axis=0, keepdims=True)
        normed = centred * lax.rsqrt(variance + EPS) * gain[...] + bias[...]
        projected = contract(weights[...], normed.astype(BF16), 1, 0)
        for first, held in ((0, left_rows), (2 * hidden, right_rows)):
            gate = projected[first : first + hidden]
            side = sigmoid(gate) * projected[first + hidden : first + 2 * hidden]
            held[2 * n] = side[:, :depth]
            held[2 * n + 1] = side[:, depth:]
        return carry

    lax.fori_loop(0, rows // 2, two_rows, 0, unroll=2)

    def one_group(e, carry):
        at = pl.ds(pl.multiple_of(e * 8, 8), 8)
        for held, out in ((left_rows, left_out), (right_rows, right_out)):
            for n in range(depth // 128):
                lanes = slice(n * 128, (n + 1) * 128)
                halves = [
                    swap_eight([held[first + i, at, lanes][None] for i in range(8)]) for first in range(0, rows, 8)
                ]
                for h in range(8):
                    out[e, h, :, lanes] = jnp.concatenate([half[h][0] for half in halves], axis=0).astype(BF16)
        return carry

    lax.fori_loop(0, eights, one_group, 0, unroll=2)


def project(pieces, firsts, count, weights, centre, gain, bias):
    rows = 16
    hidden = weights.shape[0] // 4
    channels = weights.shape[1]
    depth = sum(piece.shape[1] for piece in pieces)
    whole = lambda x: pl.BlockSpec(x.shape, lambda i: (0,) * x.ndim)
    in_specs = [
        pl.BlockSpec((rows, piece.shape[1], channels), functools.partial(lambda f, i: (i + f, 0, 0), first // rows))
        for piece, first in zip(pieces, firsts)
    ] + [whole(x) for x in (weights, centre, gain, bias)]
    shape = jax.ShapeDtypeStruct((hidden // 8, 8, count, depth), BF16)
    left, right = pl.pallas_call(
        functools.partial(project_kernel, len(pieces)),
        grid=(count // rows,),
        in_specs=in_specs,
        out_specs=[pl.BlockSpec((hidden // 8, 8, rows, depth), lambda i: (0, 0, i, 0))] * 2,
        out_shape=[shape, shape],
        scratch_shapes=[pltpu.VMEM((rows, hidden, depth), F32)] * 2,
        compiler_params=PARAMS,
        cost_estimate=at_least(
            count * depth * channels * (channels + 4 * hidden), 2 * count * depth * hidden, shape, shape
        ),
        name="project",
    )(*pieces, weights, centre, gain, bias)
    return left.reshape(hidden, count, depth), right.reshape(hidden, count, depth)


def triangle_kernel(n_left, n_sides, group, pairs, which, *refs):
    lefts, out = refs[:n_left], refs[-1]
    sides = refs[n_left:-1]
    step = lefts[0].shape[0]

    def go(choice):
        def one_group(g, carry):
            for n, (i, j) in enumerate(pairs):
                side = sides[j * n_sides + choice]
                parts = [contract(lefts[i][g * group + h], side[g * group + h], 1, 1) for h in range(group)]
                out[n, g] = jnp.concatenate(parts, axis=-1).astype(BF16)
            return carry

        lax.fori_loop(0, step // group, one_group, 0, unroll=2)

    for n in range(n_sides):
        pl.when(which[0] == n)(functools.partial(go, n))


def group_of(columns):
    return 128 // math.gcd(columns, 128)


def triangle(lefts, rights, pairs, which):
    hidden, rows, depth = lefts[0].shape
    columns = rights[0][0].shape[1]
    n_sides = len(rights[0])
    group = group_of(columns)
    step = max(16 if len(rights) > 3 else 32, group)
    shape = jax.ShapeDtypeStruct((len(pairs), hidden // group, rows, group * columns), BF16)

    def side_spec(n):
        return pl.BlockSpec((step, columns, depth), lambda h, which: (jnp.where(which[0] == n, h, 0), 0, 0))

    return pl.pallas_call(
        functools.partial(triangle_kernel, len(lefts), n_sides, group, pairs),
        grid_spec=pltpu.PrefetchScalarGridSpec(
            num_scalar_prefetch=1,
            grid=(hidden // step,),
            in_specs=[pl.BlockSpec((step, rows, depth), lambda h, which: (h, 0, 0))] * len(lefts)
            + [side_spec(n) for _ in rights for n in range(n_sides)],
            out_specs=pl.BlockSpec(
                (len(pairs), step // group, rows, group * columns), lambda h, which: (0, h, 0, 0)
            ),
        ),
        out_shape=shape,
        compiler_params=PARAMS,
        cost_estimate=at_least(
            len(pairs) * hidden * rows * columns * depth, 0, shape, *lefts, *[side[0] for side in rights]
        ),
        name="triangle",
    )(which, *lefts, *[x for side in rights for x in side])


def gate_kernel(pair, centre, mean, gain, bias, weights, out):
    rows, columns, channels = pair.shape
    values = pair[...].reshape(rows * columns, channels)
    centred = contract(values, centre[...], 1, 0)
    square = centred * centred
    high = square.astype(BF16)
    low = (square - high.astype(F32)).astype(BF16)
    variance = contract(jnp.concatenate([high, low], axis=1), mean[...], 1, 0)
    normed = (centred * lax.rsqrt(variance + EPS) * gain[...] + bias[...]).astype(BF16)
    gate = sigmoid(contract(normed, weights[...], 1, 0))
    out[...] = gate.astype(BF16).reshape(rows, columns, channels)


def gate_of(pair, centre, mean, gain, bias, weights):
    rows = 8
    count, columns, channels = pair.shape
    whole = lambda x: pl.BlockSpec(x.shape, lambda i: (0,) * x.ndim)
    block = pl.BlockSpec((rows, columns, channels), lambda i: (i, 0, 0))
    return pl.pallas_call(
        gate_kernel,
        grid=(count // rows,),
        in_specs=[block] + [whole(x) for x in (centre, mean, gain, bias, weights)],
        out_specs=block,
        out_shape=jax.ShapeDtypeStruct(pair.shape, BF16),
        compiler_params=PARAMS,
        cost_estimate=at_least(
            count * columns * channels * 4 * channels, count * columns * channels, pair, pair
        ),
        name="gate",
    )(pair, centre, mean, gain, bias, weights)


def finish_kernel(group, hidden, own, sent, gate, weights, gain, bias, *refs):
    out, rows_of = refs[-2:]
    packed, rows, lanes = own.shape
    columns = lanes // group

    def over_hidden(x):
        total = jnp.sum(x, axis=0)
        shift = columns
        while shift < lanes:
            total = total + pltpu.roll(total, shift, 1)
            shift *= 2
        return total * (1.0 / hidden)

    total = own[...].astype(F32) + sent[...].astype(F32)
    centred = total - over_hidden(total)[None]
    scale = lax.rsqrt(over_hidden(centred * centred) + EPS)
    normed = centred * scale[None] * gain[...] + bias[...]
    rows_of[...] = normed.reshape(packed * rows, lanes)
    for i in range(rows):
        held = rows_of[pl.ds(i, packed, stride=rows), :]
        parts = [held[:, g * columns : (g + 1) * columns] for g in range(group)]
        result = contract(jnp.concatenate(parts, axis=0).astype(BF16), weights[...], 0, 0)
        out[i] = (result * gate[i].astype(F32)).astype(BF16)


def finish(own, sent, gate, t, chunks, share, weights, gain, bias, held):
    pieces, packed, count, lanes = own.shape
    rows = count if count <= 32 else 16
    hidden, channels = weights.shape
    group = hidden // packed
    steps = count // rows
    before = t * share

    def row_of(p):
        return jnp.where(p < before, p // share, t)

    def column_of(p):
        of_row = p - before
        return jnp.where(p < before, (p % share) * chunks + t, (of_row % share) * chunks + of_row // share)

    whole = lambda x: pl.BlockSpec(x.shape, lambda p, r: (0,) * x.ndim)
    part = pl.BlockSpec((None, packed, rows, lanes), lambda p, r: (p, 0, r, 0))
    block = pl.BlockSpec((rows, lanes // group, channels), lambda p, r: (row_of(p) * steps + r, column_of(p), 0))
    earlier = [] if held is None else [held]
    return pl.pallas_call(
        functools.partial(finish_kernel, group, hidden),
        grid=(pieces, steps),
        in_specs=[part, part, block, whole(weights), whole(gain), whole(bias)]
        + [pl.BlockSpec(memory_space=pl.ANY)] * len(earlier),
        out_specs=block,
        out_shape=jax.ShapeDtypeStruct(gate.shape, BF16),
        scratch_shapes=[pltpu.VMEM((packed * rows, lanes), F32)],
        input_output_aliases={6: 0} if earlier else {},
        compiler_params=PARAMS,
        cost_estimate=at_least(
            pieces * count * (lanes // group) * hidden * channels, pieces * count * (lanes // group), own, sent
        ),
        name="finish",
    )(own, sent, gate, weights, gain, bias, *earlier)


def after(value, *others):
    return lax.optimization_barrier((value,) + others)[0]


def on_device(n_row, n_col, pair_act, ln_gain, ln_bias, w_proj, w_gate, out_gain, out_bias, w_out):
    tile_rows, tile_cols, channels = pair_act.shape
    hidden = w_proj.shape[1] // 4
    half = n_col // 2
    top = n_row // 2
    share = n_row // n_col
    row, col = lax.axis_index("row"), lax.axis_index("col")
    axes = ("row", "col")
    place = lambda r, c: r * n_col + c
    chunks = min(CHUNKS, tile_rows // 16)
    step = tile_rows // chunks
    group = group_of(step)
    packed = hidden // group

    w_sides = w_proj.T
    centre = (jnp.eye(channels, dtype=F32) - 1.0 / channels).astype(BF16)
    mean = jnp.full((2 * channels, channels), 1.0 / channels, BF16)
    by_hidden = lambda v: jnp.repeat(v.reshape(packed, group), step, axis=1)[:, None, :]
    gain_out, bias_out = by_hidden(out_gain), by_hidden(out_bias)
    w_last = w_out.reshape(packed, group, channels).swapaxes(0, 1).reshape(hidden, channels)

    def holds(r, c):
        return (r // share) % half == c % half

    def across_top(near):
        pairs = [(place(r, c), place(r ^ top, c)) for r in range(n_row) for c in range(n_col) if holds(r, c)]
        return lax.ppermute(near, axes, pairs)

    def to_all_rows(held):
        bit = top // 2
        while bit >= share:
            alike = (bit * 2 - 1) & ~(share - 1)
            sends = [
                (place(r, c), place(r ^ bit, c))
                for r in range(n_row)
                for c in range(n_col)
                if (r ^ (c * share)) & alike == 0
            ]
            came = lax.ppermute(held, axes, sends)
            if bit == 1:
                return [[held, came]]
            held = jnp.where(((row ^ (col * share)) & bit) == 0, held, came)
            bit //= 2
        slabs = [held]
        while bit >= 1:
            swap = [(r, r ^ bit) for r in range(n_row)]
            others = [lax.ppermute(x, "row", swap) for x in slabs]
            slabs = [jnp.where((row & bit) == 0, a, b) for a, b in zip(slabs + others, others + slabs)]
            bit //= 2
        return [[x] for x in slabs]

    near_is_own = (row // top) == (col // half)
    swap_half = [(c, c ^ half) for c in range(n_col)]
    two_chips = share == 1 and top == 2
    holder = ((row ^ col) & 1) == 0
    lefts, rights, fars, units = [], [], [], []

    def first_step(right):
        if not two_chips:
            return across_top(right)
        pairs = [(place(r, c), place(r ^ top ^ 1, c)) for r in range(n_row) for c in range(n_col) if holds(r, c)]
        return lax.ppermute(right, axes, pairs)

    def second_step(right, far, *waits):
        if not two_chips:
            return [a + b for a, b in zip(to_all_rows(right), to_all_rows(far))]
        near, far = after(right, *waits), after(far, *waits)
        cells = [(r, c, holds(r, c)) for r in range(n_row) for c in range(n_col)]
        near_in = lax.ppermute(near, axes, [(place(r, c), place(r ^ 1, c)) for r, c, held in cells if held])
        far_in = lax.ppermute(far, axes, [(place(r, c), place(r ^ 1, c)) for r, c, held in cells if not held])
        return [[right, near_in, far, far_in]]

    def product(pairs, own):
        take_near = near_is_own if own else jnp.logical_not(near_is_own)
        if two_chips:
            which = jnp.where(take_near, jnp.where(holder, 0, 1), jnp.where(holder, 3, 2))
        else:
            which = jnp.where(take_near, 0, 1)
        used_left = sorted({i for i, _, _ in pairs})
        used_right = sorted({(j, s) for _, j, s in pairs})
        return triangle(
            [lefts[i] for i in used_left],
            [units[j][s] for j, s in used_right],
            [(used_left.index(i), used_right.index((j, s))) for i, j, s in pairs],
            which.astype(jnp.int32).reshape(1),
        )

    wide = lambda v: jnp.broadcast_to(v[:, None], (channels, 2 * half * tile_cols))
    gain_in, bias_in = wide(ln_gain), wide(ln_bias)
    shards = range(share)
    waves = []
    for t in range(chunks):
        by_column = [(i, t, s) for i in range(t) for s in shards]
        by_row = [(t, j, s) for j in range(t + 1) for s in shards]
        waves.append(by_column + by_row)

    exchanged = []

    def prepare(t, *held):
        left, right = project(
            [pair_act] + exchanged[t],
            [t * step] + [0] * (half - 1),
            step,
            w_sides,
            centre,
            after(gain_in, *held) if held else gain_in,
            bias_in,
        )
        lefts.append(left)
        rights.append(right)
        return left

    def exchange(n, *waits):
        block = after(slabs[n], *waits) if waits else slabs[n]
        exchanged.append([lax.ppermute(block, "col", [(c, c ^ o) for c in range(n_col)]) for o in range(1, half)])

    def keep_own():
        t = len(own)
        lefts[t] = after(lefts[t], *token)
        own.append(product(waves[t], True))
        token[:] = own[-1:]

    def slab(n, *waits):
        return (after(pair_act, *waits) if waits else pair_act)[n * step : (n + 1) * step]

    slabs = [slab(0)]
    if chunks > 1:
        slabs.append(slab(1, slabs[0]))
    exchange(0)
    token, moved, own = [], [], []
    for n in range(chunks + 2):
        waits = token + (exchanged[n][-1:] if n < chunks else []) + (moved[n - 4 : n - 3] if n >= 4 else [])
        if n + 1 < chunks:
            exchange(n + 1, *waits)
        if 0 < n <= chunks:
            fars.append(first_step(after(rights[n - 1], *waits)))
        if n >= 2:
            units.append(second_step(rights[n - 2], fars[n - 2], *waits))
        if n + 2 < chunks:
            slabs.append(slab(n + 2, *waits))
        if n < chunks:
            token = [prepare(n, *token, *slabs[n + 2 : n + 3])]
        if n >= 2:
            t = n - 2
            if t == chunks - 1:
                while len(own) < t:
                    keep_own()
            lefts[t] = after(lefts[t], *token)
            made = product(waves[t], False)
            token = [made]
            waits = moved[t - 1 : t]
            moved.append(lax.ppermute(after(made, *waits) if waits else made, "col", swap_half))
            if t == chunks - 2:
                while len(own) < t // 2:
                    keep_own()
                gate = gate_of(pair_act, centre, mean, after(ln_gain[None], *token), ln_bias[None], w_gate)
                token = [gate]
    while len(own) < chunks:
        keep_own()
    out = None
    for t in range(chunks):
        out = finish(own[t], moved[t], gate, t, chunks, share, w_last, gain_out, bias_out, out)
    return out


def solution(mesh):
    n_row, n_col = mesh.shape["row"], mesh.shape["col"]
    in_specs = (P(("groups", "row"), "col", None), P(), P(), P(), P(), P(), P(), P())
    out_specs = P(("groups", "row"), "col", None)
    return jax.shard_map(
        functools.partial(on_device, n_row, n_col),
        mesh=mesh,
        in_specs=in_specs,
        out_specs=out_specs,
        check_vma=False,
    )
```

```python
import functools
import math

import jax
import jax.numpy as jnp
from jax import lax
from jax.experimental import pallas as pl
from jax.experimental.pallas import tpu as pltpu
from jax.sharding import PartitionSpec as P

CHUNKS = 6
EPS = 1e-05
F32, BF16 = jnp.float32, jnp.bfloat16
PARAMS = pltpu.CompilerParams(vmem_limit_bytes=52 * 1024 * 1024)


def sigmoid(x):
    return pl.reciprocal(1.0 + jnp.exp(-x), approx=True)


def contract(left, right, left_dim, right_dim):
    return lax.dot_general(
        left, right, (((left_dim,), (right_dim,)), ((), ())), preferred_element_type=F32
    )


def at_least(macs, transcendentals, *arrays):
    return pl.CostEstimate(
        flops=2 * macs,
        transcendentals=transcendentals,
        bytes_accessed=sum(math.prod(x.shape) * x.dtype.itemsize for x in arrays),
    )


def swap_eight(arrays):
    place = lax.broadcasted_iota(jnp.int32, arrays[0].shape, 1)
    for shift in (4, 2, 1):
        low = (place & shift) == 0
        swapped = list(arrays)
        for n in range(8):
            if n & shift == 0:
                one, two = arrays[n], arrays[n + shift]
                swapped[n] = jnp.where(low, one, pltpu.roll(two, shift, 1))
                swapped[n + shift] = jnp.where(low, pltpu.roll(one, 8 - shift, 1), two)
        arrays = swapped
    return arrays


def project_kernel(n_pieces, n_slabs, which, *refs):
    pieces = refs[: n_pieces * n_slabs]
    weights, centre, gain, bias, out, held = refs[n_pieces * n_slabs :]
    eights, _, rows, depth = out.shape
    hidden = eights * 8

    def go(first):
        def two_rows(n, carry):
            values = jnp.concatenate(
                [piece[2 * n + i] for i in range(2) for piece in pieces[first : first + n_pieces]], axis=0
            )
            centred = contract(centre[...], values, 1, 1)
            variance = jnp.mean(centred * centred, axis=0, keepdims=True)
            normed = centred * lax.rsqrt(variance + EPS) * gain[...] + bias[...]
            projected = contract(weights[...], normed.astype(BF16), 1, 0)
            side = sigmoid(projected[:hidden]) * projected[hidden:]
            held[2 * n] = side[:, :depth]
            held[2 * n + 1] = side[:, depth:]
            return carry

        lax.fori_loop(0, rows // 2, two_rows, 0, unroll=2)

    for n in range(n_slabs):
        pl.when(which[0] == n)(functools.partial(go, n * n_pieces))

    def one_group(e, carry):
        at = pl.ds(pl.multiple_of(e * 8, 8), 8)
        for n in range(depth // 128):
            lanes = slice(n * 128, (n + 1) * 128)
            halves = [
                swap_eight([held[first + i, at, lanes][None] for i in range(8)]) for first in range(0, rows, 8)
            ]
            for h in range(8):
                out[e, h, :, lanes] = jnp.concatenate([half[h][0] for half in halves], axis=0).astype(BF16)
        return carry

    lax.fori_loop(0, eights, one_group, 0, unroll=2)


def project(slabs, which, n_pieces, weights, centre, gain, bias):
    rows = 16
    hidden, channels = weights.shape[0] // 2, weights.shape[1]
    count, columns = slabs[0].shape[0] // n_pieces, slabs[0].shape[1]
    depth = n_pieces * columns
    steps = count // rows
    whole = lambda x: pl.BlockSpec(x.shape, lambda i, which: (0,) * x.ndim)

    def piece_spec(n, p):
        return pl.BlockSpec(
            (rows, columns, channels), lambda i, which: (p * steps + jnp.where(which[0] == n, i, 0), 0, 0)
        )

    shape = jax.ShapeDtypeStruct((hidden // 8, 8, count, depth), BF16)
    side = pl.pallas_call(
        functools.partial(project_kernel, n_pieces, len(slabs)),
        grid_spec=pltpu.PrefetchScalarGridSpec(
            num_scalar_prefetch=1,
            grid=(steps,),
            in_specs=[piece_spec(n, p) for n in range(len(slabs)) for p in range(n_pieces)]
            + [whole(x) for x in (weights, centre, gain, bias)],
            out_specs=pl.BlockSpec((hidden // 8, 8, rows, depth), lambda i, which: (0, 0, i, 0)),
            scratch_shapes=[pltpu.VMEM((rows, hidden, depth), F32)],
        ),
        out_shape=shape,
        compiler_params=PARAMS,
        cost_estimate=at_least(count * depth * channels * (channels + 2 * hidden), count * depth * hidden, shape),
        name="project",
    )(which, *[slab for slab in slabs for _ in range(n_pieces)], weights, centre, gain, bias)
    return side.reshape(hidden, count, depth)


def triangle_kernel(n_left, n_sides, group, pairs, which, *refs):
    lefts, out = refs[:n_left], refs[-1]
    sides = refs[n_left:-1]
    step = lefts[0].shape[0]

    def go(choice):
        def one_group(g, carry):
            for n, (i, j) in enumerate(pairs):
                side = sides[j * n_sides + choice]
                parts = [contract(lefts[i][g * group + h], side[g * group + h], 1, 1) for h in range(group)]
                out[n, g] = jnp.concatenate(parts, axis=-1).astype(BF16)
            return carry

        lax.fori_loop(0, step // group, one_group, 0, unroll=2)

    for n in range(n_sides):
        pl.when(which[0] == n)(functools.partial(go, n))


def group_of(columns):
    return 128 // math.gcd(columns, 128)


def triangle(lefts, rights, pairs, which):
    hidden, rows, depth = lefts[0].shape
    columns = rights[0][0].shape[1]
    n_sides = len(rights[0])
    group = group_of(columns)
    step = max(16 if len(rights) > 3 else 32, group)
    shape = jax.ShapeDtypeStruct((len(pairs), hidden // group, rows, group * columns), BF16)

    def side_spec(n):
        return pl.BlockSpec((step, columns, depth), lambda h, which: (jnp.where(which[0] == n, h, 0), 0, 0))

    return pl.pallas_call(
        functools.partial(triangle_kernel, len(lefts), n_sides, group, pairs),
        grid_spec=pltpu.PrefetchScalarGridSpec(
            num_scalar_prefetch=1,
            grid=(hidden // step,),
            in_specs=[pl.BlockSpec((step, rows, depth), lambda h, which: (h, 0, 0))] * len(lefts)
            + [side_spec(n) for _ in rights for n in range(n_sides)],
            out_specs=pl.BlockSpec(
                (len(pairs), step // group, rows, group * columns), lambda h, which: (0, h, 0, 0)
            ),
        ),
        out_shape=shape,
        compiler_params=PARAMS,
        cost_estimate=at_least(
            len(pairs) * hidden * rows * columns * depth, 0, shape, *lefts, *[side[0] for side in rights]
        ),
        name="triangle",
    )(which, *lefts, *[x for side in rights for x in side])


def gate_kernel(pair, centre, mean, gain, bias, weights, out):
    rows, columns, channels = pair.shape
    values = pair[...].reshape(rows * columns, channels)
    centred = contract(values, centre[...], 1, 0)
    square = centred * centred
    high = square.astype(BF16)
    low = (square - high.astype(F32)).astype(BF16)
    variance = contract(jnp.concatenate([high, low], axis=1), mean[...], 1, 0)
    normed = (centred * lax.rsqrt(variance + EPS) * gain[...] + bias[...]).astype(BF16)
    gate = sigmoid(contract(normed, weights[...], 1, 0))
    out[...] = gate.astype(BF16).reshape(rows, columns, channels)


def gate_of(pair, centre, mean, gain, bias, weights):
    rows = 8
    count, columns, channels = pair.shape
    whole = lambda x: pl.BlockSpec(x.shape, lambda i: (0,) * x.ndim)
    block = pl.BlockSpec((rows, columns, channels), lambda i: (i, 0, 0))
    return pl.pallas_call(
        gate_kernel,
        grid=(count // rows,),
        in_specs=[block] + [whole(x) for x in (centre, mean, gain, bias, weights)],
        out_specs=block,
        out_shape=jax.ShapeDtypeStruct(pair.shape, BF16),
        compiler_params=PARAMS,
        cost_estimate=at_least(
            count * columns * channels * 4 * channels, count * columns * channels, pair, pair
        ),
        name="gate",
    )(pair, centre, mean, gain, bias, weights)


def finish_kernel(group, hidden, own, sent, gate, weights, gain, bias, *refs):
    out, rows_of = refs[-2:]
    packed, rows, lanes = own.shape
    columns = lanes // group

    def over_hidden(x):
        total = jnp.sum(x, axis=0)
        shift = columns
        while shift < lanes:
            total = total + pltpu.roll(total, shift, 1)
            shift *= 2
        return total * (1.0 / hidden)

    total = own[...].astype(F32) + sent[...].astype(F32)
    centred = total - over_hidden(total)[None]
    scale = lax.rsqrt(over_hidden(centred * centred) + EPS)
    normed = centred * scale[None] * gain[...] + bias[...]
    rows_of[...] = normed.reshape(packed * rows, lanes)
    for i in range(rows):
        held = rows_of[pl.ds(i, packed, stride=rows), :]
        parts = [held[:, g * columns : (g + 1) * columns] for g in range(group)]
        result = contract(jnp.concatenate(parts, axis=0).astype(BF16), weights[...], 0, 0)
        out[i] = (result * gate[i].astype(F32)).astype(BF16)


def finish(own, sent, gate, t, chunks, share, weights, gain, bias, held):
    pieces, packed, count, lanes = own.shape
    rows = count if count <= 32 else 16
    hidden, channels = weights.shape
    group = hidden // packed
    steps = count // rows
    before = t * share

    def row_of(p):
        return jnp.where(p < before, p // share, t)

    def column_of(p):
        of_row = p - before
        return jnp.where(p < before, (p % share) * chunks + t, (of_row % share) * chunks + of_row // share)

    whole = lambda x: pl.BlockSpec(x.shape, lambda p, r: (0,) * x.ndim)
    part = pl.BlockSpec((None, packed, rows, lanes), lambda p, r: (p, 0, r, 0))
    block = pl.BlockSpec((rows, lanes // group, channels), lambda p, r: (row_of(p) * steps + r, column_of(p), 0))
    earlier = [] if held is None else [held]
    return pl.pallas_call(
        functools.partial(finish_kernel, group, hidden),
        grid=(pieces, steps),
        in_specs=[part, part, block, whole(weights), whole(gain), whole(bias)]
        + [pl.BlockSpec(memory_space=pl.ANY)] * len(earlier),
        out_specs=block,
        out_shape=jax.ShapeDtypeStruct(gate.shape, BF16),
        scratch_shapes=[pltpu.VMEM((packed * rows, lanes), F32)],
        input_output_aliases={6: 0} if earlier else {},
        compiler_params=PARAMS,
        cost_estimate=at_least(
            pieces * count * (lanes // group) * hidden * channels, pieces * count * (lanes // group), own, sent
        ),
        name="finish",
    )(own, sent, gate, weights, gain, bias, *earlier)


def after(value, *others):
    return lax.optimization_barrier((value,) + others)[0]


def on_device(n_row, n_col, pair_act, ln_gain, ln_bias, w_proj, w_gate, out_gain, out_bias, w_out):
    tile_rows, tile_cols, channels = pair_act.shape
    hidden = w_proj.shape[1] // 4
    half = n_col // 2
    top = n_row // 2
    share = n_row // n_col
    row, col = lax.axis_index("row"), lax.axis_index("col")
    axes = ("row", "col")
    place = lambda r, c: r * n_col + c
    chunks = min(CHUNKS, tile_rows // 16)
    step = tile_rows // chunks
    group = group_of(step)
    packed = hidden // group

    w_left, w_right = w_proj.T[: 2 * hidden], w_proj.T[2 * hidden :]
    centre = (jnp.eye(channels, dtype=F32) - 1.0 / channels).astype(BF16)
    mean = jnp.full((2 * channels, channels), 1.0 / channels, BF16)
    by_hidden = lambda v: jnp.repeat(v.reshape(packed, group), step, axis=1)[:, None, :]
    gain_out, bias_out = by_hidden(out_gain), by_hidden(out_bias)
    w_last = w_out.reshape(packed, group, channels).swapaxes(0, 1).reshape(hidden, channels)

    def holds(r, c):
        return (r // share) % half == c % half

    def across_top(near):
        pairs = [(place(r, c), place(r ^ top, c)) for r in range(n_row) for c in range(n_col) if holds(r, c)]
        return lax.ppermute(near, axes, pairs)

    def to_all_rows(held):
        bit = top // 2
        while bit >= share:
            alike = (bit * 2 - 1) & ~(share - 1)
            sends = [
                (place(r, c), place(r ^ bit, c))
                for r in range(n_row)
                for c in range(n_col)
                if (r ^ (c * share)) & alike == 0
            ]
            came = lax.ppermute(held, axes, sends)
            if bit == 1:
                return [[held, came]]
            held = jnp.where(((row ^ (col * share)) & bit) == 0, held, came)
            bit //= 2
        slabs = [held]
        while bit >= 1:
            swap = [(r, r ^ bit) for r in range(n_row)]
            others = [lax.ppermute(x, "row", swap) for x in slabs]
            slabs = [jnp.where((row & bit) == 0, a, b) for a, b in zip(slabs + others, others + slabs)]
            bit //= 2
        return [[x] for x in slabs]

    near_is_own = (row // top) == (col // half)
    swap_half = [(c, c ^ half) for c in range(n_col)]
    two_chips = share == 1 and top == 2
    holder = ((row ^ col) & 1) == 0
    number = lambda x: jnp.asarray(x, jnp.int32).reshape(1)
    slabs, firsts, lefts, units = [], [], [], []

    def first_step(slab):
        if not two_chips:
            return across_top(slab)
        pairs = [(place(r, c), place(r ^ top ^ 1, c)) for r in range(n_row) for c in range(n_col) if holds(r, c)]
        return lax.ppermute(slab, axes, pairs)

    def second_step(slab, far, *waits):
        if not two_chips:
            return [[(x, 0 if len(x) == 1 else (row ^ col) & 1) for x in to_all_rows(held)] for held in (slab, far)]
        given = jnp.where(holder, slab, after(far, *waits))
        got = lax.ppermute(given, "row", [(r, r ^ 1) for r in range(n_row)])
        return [[([slab, got], jnp.where(holder, 0, 1))], [([got, far], jnp.where(holder, 0, 1))]]

    def product(pairs, own):
        take_near = near_is_own if own else jnp.logical_not(near_is_own)
        used_left = sorted({i for i, _, _ in pairs})
        used_right = sorted({(j, s) for _, j, s in pairs})
        return triangle(
            [lefts[i] for i in used_left],
            [units[j][s] for j, s in used_right],
            [(used_left.index(i), used_right.index((j, s))) for i, j, s in pairs],
            number(jnp.where(take_near, 0, 1)),
        )

    wide = lambda v: jnp.broadcast_to(v[:, None], (channels, 2 * half * tile_cols))
    gain_in, bias_in = wide(ln_gain), wide(ln_bias)
    shards = range(share)
    waves = []
    for t in range(chunks):
        by_column = [(i, t, s) for i in range(t) for s in shards]
        by_row = [(t, j, s) for j in range(t + 1) for s in shards]
        waves.append(by_column + by_row)

    token, moved, own, exchanged = [], [], [], []

    def keep_own():
        t = len(own)
        lefts[t] = after(lefts[t], *token)
        own.append(product(waves[t], True))
        token[:] = own[-1:]

    def exchange(n, *waits):
        block = (after(pair_act, *waits) if waits else pair_act)[n * step : (n + 1) * step]
        exchanged.append([lax.ppermute(block, "col", [(c, c ^ o) for c in range(n_col)]) for o in range(1, half)])

    def side(candidates, choice, weights):
        made = project(candidates, number(choice), half, weights, centre, after(gain_in, *token), bias_in)
        token[:] = [made]
        return made

    exchange(0)
    gate = gate_of(pair_act, centre, mean, ln_gain[None], ln_bias[None], w_gate)
    token[:] = [gate]
    for n in range(chunks + 1):
        waits = (token if n else []) + (exchanged[n][-1:] if n < chunks else [])
        waits = waits + (moved[n - 3 : n - 2] if n >= 3 else [])
        if n + 1 < chunks:
            exchange(n + 1, *waits)
        if n < chunks:
            block = after(pair_act, *waits)[n * step : (n + 1) * step]
            slabs.append(jnp.concatenate([block] + exchanged[n], axis=0))
            firsts.append(first_step(slabs[n]))
        if n == 0:
            continue
        t = n - 1
        near, far = second_step(slabs[t], firsts[t], *waits)
        lefts.append(side([slabs[t]], 0, w_left))
        units.append([])
        for s in shards:
            units[t].append([side(candidates, choice, w_right) for candidates, choice in (near[s], far[s])])
        if t == chunks - 1:
            while len(own) < t:
                keep_own()
        lefts[t] = after(lefts[t], *token)
        made = product(waves[t], False)
        token[:] = [made]
        waits = moved[t - 1 : t]
        moved.append(lax.ppermute(after(made, *waits) if waits else made, "col", swap_half))
        if t == chunks - 2:
            while len(own) < t // 2:
                keep_own()
    while len(own) < chunks:
        keep_own()
    out = None
    for t in range(chunks):
        out = finish(own[t], moved[t], gate, t, chunks, share, w_last, gain_out, bias_out, out)
    return out


def solution(mesh):
    n_row, n_col = mesh.shape["row"], mesh.shape["col"]
    in_specs = (P(("groups", "row"), "col", None), P(), P(), P(), P(), P(), P(), P())
    out_specs = P(("groups", "row"), "col", None)
    return jax.shard_map(
        functools.partial(on_device, n_row, n_col),
        mesh=mesh,
        in_specs=in_specs,
        out_specs=out_specs,
        check_vma=False,
    )
```

```python
import functools
import math

import jax
import jax.numpy as jnp
from jax import lax
from jax.experimental import pallas as pl
from jax.experimental.pallas import tpu as pltpu
from jax.sharding import PartitionSpec as P

CHUNKS = 6
EPS = 1e-05
F32, BF16 = jnp.float32, jnp.bfloat16
PARAMS = pltpu.CompilerParams(vmem_limit_bytes=52 * 1024 * 1024)


def sigmoid(x):
    return pl.reciprocal(1.0 + jnp.exp(-x), approx=True)


def contract(left, right, left_dim, right_dim):
    return lax.dot_general(
        left, right, (((left_dim,), (right_dim,)), ((), ())), preferred_element_type=F32
    )


def at_least(macs, transcendentals, *arrays):
    return pl.CostEstimate(
        flops=2 * macs,
        transcendentals=transcendentals,
        bytes_accessed=sum(math.prod(x.shape) * x.dtype.itemsize for x in arrays),
    )


def swap_eight(arrays):
    place = lax.broadcasted_iota(jnp.int32, arrays[0].shape, 1)
    for shift in (4, 2, 1):
        low = (place & shift) == 0
        swapped = list(arrays)
        for n in range(8):
            if n & shift == 0:
                one, two = arrays[n], arrays[n + shift]
                swapped[n] = jnp.where(low, one, pltpu.roll(two, shift, 1))
                swapped[n + shift] = jnp.where(low, pltpu.roll(one, 8 - shift, 1), two)
        arrays = swapped
    return arrays


def project_kernel(n_pieces, n_slabs, which, *refs):
    pieces = refs[: n_pieces * n_slabs]
    weights, centre, gain, bias, out, held = refs[n_pieces * n_slabs :]
    eights, _, rows, depth = out.shape
    hidden = eights * 8

    def go(first):
        def two_rows(n, carry):
            values = jnp.concatenate(
                [piece[2 * n + i] for i in range(2) for piece in pieces[first : first + n_pieces]], axis=0
            )
            centred = contract(centre[...], values, 1, 1)
            variance = jnp.mean(centred * centred, axis=0, keepdims=True)
            normed = centred * lax.rsqrt(variance + EPS) * gain[...] + bias[...]
            projected = contract(weights[...], normed.astype(BF16), 1, 0)
            side = sigmoid(projected[:hidden]) * projected[hidden:]
            held[2 * n] = side[:, :depth]
            held[2 * n + 1] = side[:, depth:]
            return carry

        lax.fori_loop(0, rows // 2, two_rows, 0, unroll=2)

    for n in range(n_slabs):
        pl.when(which[0] == n)(functools.partial(go, n * n_pieces))

    def one_group(e, carry):
        at = pl.ds(pl.multiple_of(e * 8, 8), 8)
        for n in range(depth // 128):
            lanes = slice(n * 128, (n + 1) * 128)
            halves = [
                swap_eight([held[first + i, at, lanes][None] for i in range(8)]) for first in range(0, rows, 8)
            ]
            for h in range(8):
                out[e, h, :, lanes] = jnp.concatenate([half[h][0] for half in halves], axis=0).astype(BF16)
        return carry

    lax.fori_loop(0, eights, one_group, 0, unroll=2)


def project(slabs, which, n_pieces, weights, centre, gain, bias):
    rows = 16
    hidden, channels = weights.shape[0] // 2, weights.shape[1]
    count, columns = slabs[0].shape[0] // n_pieces, slabs[0].shape[1]
    depth = n_pieces * columns
    steps = count // rows
    whole = lambda x: pl.BlockSpec(x.shape, lambda i, which: (0,) * x.ndim)

    def piece_spec(n, p):
        return pl.BlockSpec(
            (rows, columns, channels), lambda i, which: (p * steps + jnp.where(which[0] == n, i, 0), 0, 0)
        )

    shape = jax.ShapeDtypeStruct((hidden // 8, 8, count, depth), BF16)
    side = pl.pallas_call(
        functools.partial(project_kernel, n_pieces, len(slabs)),
        grid_spec=pltpu.PrefetchScalarGridSpec(
            num_scalar_prefetch=1,
            grid=(steps,),
            in_specs=[piece_spec(n, p) for n in range(len(slabs)) for p in range(n_pieces)]
            + [whole(x) for x in (weights, centre, gain, bias)],
            out_specs=pl.BlockSpec((hidden // 8, 8, rows, depth), lambda i, which: (0, 0, i, 0)),
            scratch_shapes=[pltpu.VMEM((rows, hidden, depth), F32)],
        ),
        out_shape=shape,
        compiler_params=PARAMS,
        cost_estimate=at_least(count * depth * channels * (channels + 2 * hidden), count * depth * hidden, shape),
        name="project",
    )(which, *[slab for slab in slabs for _ in range(n_pieces)], weights, centre, gain, bias)
    return side.reshape(hidden, count, depth)


def triangle_kernel(n_left, n_sides, group, pairs, which, *refs):
    lefts, out = refs[:n_left], refs[-1]
    sides = refs[n_left:-1]
    step = lefts[0].shape[0]

    def go(choice):
        def one_group(g, carry):
            for n, (i, j) in enumerate(pairs):
                side = sides[j * n_sides + choice]
                parts = [contract(lefts[i][g * group + h], side[g * group + h], 1, 1) for h in range(group)]
                out[n, g] = jnp.concatenate(parts, axis=-1).astype(BF16)
            return carry

        lax.fori_loop(0, step // group, one_group, 0, unroll=2)

    for n in range(n_sides):
        pl.when(which[0] == n)(functools.partial(go, n))


def group_of(columns):
    return 128 // math.gcd(columns, 128)


def triangle(lefts, rights, pairs, which):
    hidden, rows, depth = lefts[0].shape
    columns = rights[0][0].shape[1]
    n_sides = len(rights[0])
    group = group_of(columns)
    step = max(16 if len(rights) > 3 else 32, group)
    shape = jax.ShapeDtypeStruct((len(pairs), hidden // group, rows, group * columns), BF16)

    def side_spec(n):
        return pl.BlockSpec((step, columns, depth), lambda h, which: (jnp.where(which[0] == n, h, 0), 0, 0))

    return pl.pallas_call(
        functools.partial(triangle_kernel, len(lefts), n_sides, group, pairs),
        grid_spec=pltpu.PrefetchScalarGridSpec(
            num_scalar_prefetch=1,
            grid=(hidden // step,),
            in_specs=[pl.BlockSpec((step, rows, depth), lambda h, which: (h, 0, 0))] * len(lefts)
            + [side_spec(n) for _ in rights for n in range(n_sides)],
            out_specs=pl.BlockSpec(
                (len(pairs), step // group, rows, group * columns), lambda h, which: (0, h, 0, 0)
            ),
        ),
        out_shape=shape,
        compiler_params=PARAMS,
        cost_estimate=at_least(
            len(pairs) * hidden * rows * columns * depth, 0, shape, *lefts, *[side[0] for side in rights]
        ),
        name="triangle",
    )(which, *lefts, *[x for side in rights for x in side])


def gate_kernel(pair, centre, mean, gain, bias, weights, out):
    rows, columns, channels = pair.shape
    values = pair[...].reshape(rows * columns, channels)
    centred = contract(values, centre[...], 1, 0)
    square = centred * centred
    high = square.astype(BF16)
    low = (square - high.astype(F32)).astype(BF16)
    variance = contract(jnp.concatenate([high, low], axis=1), mean[...], 1, 0)
    normed = (centred * lax.rsqrt(variance + EPS) * gain[...] + bias[...]).astype(BF16)
    gate = sigmoid(contract(normed, weights[...], 1, 0))
    out[...] = gate.astype(BF16).reshape(rows, columns, channels)


def gate_of(pair, centre, mean, gain, bias, weights):
    rows = 8
    count, columns, channels = pair.shape
    whole = lambda x: pl.BlockSpec(x.shape, lambda i: (0,) * x.ndim)
    block = pl.BlockSpec((rows, columns, channels), lambda i: (i, 0, 0))
    return pl.pallas_call(
        gate_kernel,
        grid=(count // rows,),
        in_specs=[block] + [whole(x) for x in (centre, mean, gain, bias, weights)],
        out_specs=block,
        out_shape=jax.ShapeDtypeStruct(pair.shape, BF16),
        compiler_params=PARAMS,
        cost_estimate=at_least(
            count * columns * channels * 4 * channels, count * columns * channels, pair, pair
        ),
        name="gate",
    )(pair, centre, mean, gain, bias, weights)


def finish_kernel(group, hidden, own, sent, gate, weights, gain, bias, *refs):
    out, rows_of = refs[-2:]
    packed, rows, lanes = own.shape
    columns = lanes // group

    def over_hidden(x):
        total = jnp.sum(x, axis=0)
        shift = columns
        while shift < lanes:
            total = total + pltpu.roll(total, shift, 1)
            shift *= 2
        return total * (1.0 / hidden)

    total = own[...].astype(F32) + sent[...].astype(F32)
    centred = total - over_hidden(total)[None]
    scale = lax.rsqrt(over_hidden(centred * centred) + EPS)
    normed = centred * scale[None] * gain[...] + bias[...]
    rows_of[...] = normed.reshape(packed * rows, lanes)
    for i in range(rows):
        held = rows_of[pl.ds(i, packed, stride=rows), :]
        parts = [held[:, g * columns : (g + 1) * columns] for g in range(group)]
        result = contract(jnp.concatenate(parts, axis=0).astype(BF16), weights[...], 0, 0)
        out[i] = (result * gate[i].astype(F32)).astype(BF16)


def finish(own, sent, gate, t, chunks, share, weights, gain, bias, held):
    pieces, packed, count, lanes = own.shape
    rows = count if count <= 32 else 16
    hidden, channels = weights.shape
    group = hidden // packed
    steps = count // rows
    before = t * share

    def row_of(p):
        return jnp.where(p < before, p // share, t)

    def column_of(p):
        of_row = p - before
        return jnp.where(p < before, (p % share) * chunks + t, (of_row % share) * chunks + of_row // share)

    whole = lambda x: pl.BlockSpec(x.shape, lambda p, r: (0,) * x.ndim)
    part = pl.BlockSpec((None, packed, rows, lanes), lambda p, r: (p, 0, r, 0))
    block = pl.BlockSpec((rows, lanes // group, channels), lambda p, r: (row_of(p) * steps + r, column_of(p), 0))
    earlier = [] if held is None else [held]
    return pl.pallas_call(
        functools.partial(finish_kernel, group, hidden),
        grid=(pieces, steps),
        in_specs=[part, part, block, whole(weights), whole(gain), whole(bias)]
        + [pl.BlockSpec(memory_space=pl.ANY)] * len(earlier),
        out_specs=block,
        out_shape=jax.ShapeDtypeStruct(gate.shape, BF16),
        scratch_shapes=[pltpu.VMEM((packed * rows, lanes), F32)],
        input_output_aliases={6: 0} if earlier else {},
        compiler_params=PARAMS,
        cost_estimate=at_least(
            pieces * count * (lanes // group) * hidden * channels, pieces * count * (lanes // group), own, sent
        ),
        name="finish",
    )(own, sent, gate, weights, gain, bias, *earlier)


def after(value, *others):
    return lax.optimization_barrier((value,) + others)[0]


def on_device(n_row, n_col, pair_act, ln_gain, ln_bias, w_proj, w_gate, out_gain, out_bias, w_out):
    tile_rows, tile_cols, channels = pair_act.shape
    hidden = w_proj.shape[1] // 4
    half = n_col // 2
    top = n_row // 2
    share = n_row // n_col
    row, col = lax.axis_index("row"), lax.axis_index("col")
    axes = ("row", "col")
    place = lambda r, c: r * n_col + c
    chunks = min(CHUNKS, tile_rows // 16)
    step = tile_rows // chunks
    group = group_of(step)
    packed = hidden // group

    w_left, w_right = w_proj.T[: 2 * hidden], w_proj.T[2 * hidden :]
    centre = (jnp.eye(channels, dtype=F32) - 1.0 / channels).astype(BF16)
    mean = jnp.full((2 * channels, channels), 1.0 / channels, BF16)
    by_hidden = lambda v: jnp.repeat(v.reshape(packed, group), step, axis=1)[:, None, :]
    gain_out, bias_out = by_hidden(out_gain), by_hidden(out_bias)
    w_last = w_out.reshape(packed, group, channels).swapaxes(0, 1).reshape(hidden, channels)

    def holds(r, c):
        return (r // share) % half == c % half

    def across_top(near):
        pairs = [(place(r, c), place(r ^ top, c)) for r in range(n_row) for c in range(n_col) if holds(r, c)]
        return lax.ppermute(near, axes, pairs)

    def to_all_rows(held):
        bit = top // 2
        while bit >= share:
            alike = (bit * 2 - 1) & ~(share - 1)
            sends = [
                (place(r, c), place(r ^ bit, c))
                for r in range(n_row)
                for c in range(n_col)
                if (r ^ (c * share)) & alike == 0
            ]
            came = lax.ppermute(held, axes, sends)
            if bit == 1:
                return [[held, came]]
            held = jnp.where(((row ^ (col * share)) & bit) == 0, held, came)
            bit //= 2
        slabs = [held]
        while bit >= 1:
            swap = [(r, r ^ bit) for r in range(n_row)]
            others = [lax.ppermute(x, "row", swap) for x in slabs]
            slabs = [jnp.where((row & bit) == 0, a, b) for a, b in zip(slabs + others, others + slabs)]
            bit //= 2
        return [[x] for x in slabs]

    near_is_own = (row // top) == (col // half)
    swap_half = [(c, c ^ half) for c in range(n_col)]
    two_chips = share == 1 and top == 2
    holder = ((row ^ col) & 1) == 0
    number = lambda x: jnp.asarray(x, jnp.int32).reshape(1)
    payloads, firsts, lefts, spread, right_sent, right_own = [], [], [], {}, {}, {}

    def first_step(slab):
        if not two_chips:
            return across_top(slab)
        pairs = [(place(r, c), place(r ^ top ^ 1, c)) for r in range(n_row) for c in range(n_col) if holds(r, c)]
        return lax.ppermute(slab, axes, pairs)

    def second_step(slab, far, *waits):
        if not two_chips:
            odd = (row ^ col) & 1
            shards_of = zip(to_all_rows(slab), to_all_rows(far))
            return [(a + b, odd if len(a) > 1 else 0, len(a) + (odd if len(a) > 1 else 0)) for a, b in shards_of]
        given = jnp.where(holder, slab, after(far, *waits))
        got = lax.ppermute(given, "row", [(r, r ^ 1) for r in range(n_row)])
        return [([slab, got, far], jnp.where(holder, 0, 1), jnp.where(holder, 1, 2))]

    def product(pairs, rights):
        used_left = sorted({i for i, _, _ in pairs})
        used_right = sorted({(j, s) for _, j, s in pairs})
        return triangle(
            [lefts[i] for i in used_left],
            [[rights[key]] for key in used_right],
            [(used_left.index(i), used_right.index((j, s))) for i, j, s in pairs],
            number(0),
        )

    wide = lambda v: jnp.broadcast_to(v[:, None], (channels, 2 * half * tile_cols))
    gain_in, bias_in = wide(ln_gain), wide(ln_bias)
    shards = range(share)
    waves = []
    for t in range(chunks):
        by_column = [(i, t, s) for i in range(t) for s in shards]
        by_row = [(t, j, s) for j in range(t + 1) for s in shards]
        waves.append(by_column + by_row)

    token, moved, own, exchanged = [], [], [], []

    def side(candidates, choice, weights):
        made = project(candidates, number(choice), half, weights, centre, after(gain_in, *token), bias_in)
        token[:] = [made]
        return made

    def right_of(key, own):
        candidates, near, far = spread[key]
        return side(candidates, jnp.where(near_is_own == own, near, far), w_right)

    def keep_own():
        t = len(own)
        for s in shards:
            right_own[t, s] = right_of((t, s), True)
        lefts[t] = after(lefts[t], *token)
        own.append(product(waves[t], right_own))
        token[:] = own[-1:]

    def exchange(n, *waits):
        block = after(slabs[n], *waits) if waits else slabs[n]
        exchanged.append([lax.ppermute(block, "col", [(c, c ^ o) for c in range(n_col)]) for o in range(1, half)])

    slabs = [pair_act[:step]]
    rest = after(pair_act, slabs[0])
    slabs += [rest[n * step : (n + 1) * step] for n in range(1, chunks)]
    exchange(0)
    gate = gate_of(pair_act, centre, mean, after(ln_gain[None], *slabs), ln_bias[None], w_gate)
    token[:] = [gate]
    for n in range(chunks + 1):
        waits = token + (exchanged[n][-1:] if n < chunks else []) + (moved[n - 3 : n - 2] if 3 <= n < chunks else [])
        if n + 1 < chunks:
            exchange(n + 1, *waits)
        if n < chunks:
            payloads.append(jnp.concatenate([after(slabs[n], *waits)] + exchanged[n], axis=0))
            firsts.append(first_step(payloads[n]))
        if n == 0:
            continue
        t = n - 1
        for s, found in enumerate(second_step(payloads[t], firsts[t], *waits)):
            spread[t, s] = found
        lefts.append(side([payloads[t]], 0, w_left))
        for s in shards:
            right_sent[t, s] = right_of((t, s), False)
        if t == chunks - 1:
            while len(own) < t - 1:
                keep_own()
        lefts[t] = after(lefts[t], *token)
        made = product(waves[t], right_sent)
        token[:] = [made]
        waits = moved[t - 1 : t]
        moved.append(lax.ppermute(after(made, *waits) if waits else made, "col", swap_half))
        if t == chunks - 2:
            while len(own) < t // 2:
                keep_own()
    while len(own) < chunks:
        keep_own()
    out = None
    for t in range(chunks):
        out = finish(own[t], moved[t], gate, t, chunks, share, w_last, gain_out, bias_out, out)
    return out


def solution(mesh):
    n_row, n_col = mesh.shape["row"], mesh.shape["col"]
    in_specs = (P(("groups", "row"), "col", None), P(), P(), P(), P(), P(), P(), P())
    out_specs = P(("groups", "row"), "col", None)
    return jax.shard_map(
        functools.partial(on_device, n_row, n_col),
        mesh=mesh,
        in_specs=in_specs,
        out_specs=out_specs,
        check_vma=False,
    )
```

```python
import functools
import math

import jax
import jax.numpy as jnp
from jax import lax
from jax.experimental import pallas as pl
from jax.experimental.pallas import tpu as pltpu
from jax.sharding import PartitionSpec as P

CHUNKS = 6
EPS = 1e-05
F32, BF16 = jnp.float32, jnp.bfloat16
PARAMS = pltpu.CompilerParams(vmem_limit_bytes=52 * 1024 * 1024)


def sigmoid(x):
    return pl.reciprocal(1.0 + jnp.exp(-x), approx=True)


def contract(left, right, left_dim, right_dim):
    return lax.dot_general(
        left, right, (((left_dim,), (right_dim,)), ((), ())), preferred_element_type=F32
    )


def at_least(macs, transcendentals, *arrays):
    return pl.CostEstimate(
        flops=2 * macs,
        transcendentals=transcendentals,
        bytes_accessed=sum(math.prod(x.shape) * x.dtype.itemsize for x in arrays),
    )


def swap_eight(arrays):
    place = lax.broadcasted_iota(jnp.int32, arrays[0].shape, 1)
    for shift in (4, 2, 1):
        low = (place & shift) == 0
        swapped = list(arrays)
        for n in range(8):
            if n & shift == 0:
                one, two = arrays[n], arrays[n + shift]
                swapped[n] = jnp.where(low, one, pltpu.roll(two, shift, 1))
                swapped[n + shift] = jnp.where(low, pltpu.roll(one, 8 - shift, 1), two)
        arrays = swapped
    return arrays


def project_kernel(n_pieces, n_slabs, which, *refs):
    pieces = refs[: n_pieces * n_slabs]
    weights, centre, gain, bias, out, held = refs[n_pieces * n_slabs :]
    eights, _, rows, depth = out.shape
    hidden = eights * 8

    def go(first):
        def two_rows(n, carry):
            values = jnp.concatenate(
                [piece[2 * n + i] for i in range(2) for piece in pieces[first : first + n_pieces]], axis=0
            )
            centred = contract(centre[...], values, 1, 1)
            variance = jnp.mean(centred * centred, axis=0, keepdims=True)
            normed = centred * lax.rsqrt(variance + EPS) * gain[...] + bias[...]
            projected = contract(weights[...], normed.astype(BF16), 1, 0)
            side = sigmoid(projected[:hidden]) * projected[hidden:]
            held[2 * n] = side[:, :depth]
            held[2 * n + 1] = side[:, depth:]
            return carry

        lax.fori_loop(0, rows // 2, two_rows, 0, unroll=2)

    for n in range(n_slabs):
        pl.when(which[0] == n)(functools.partial(go, n * n_pieces))

    def one_group(e, carry):
        at = pl.ds(pl.multiple_of(e * 8, 8), 8)
        for n in range(depth // 128):
            lanes = slice(n * 128, (n + 1) * 128)
            halves = [
                swap_eight([held[first + i, at, lanes][None] for i in range(8)]) for first in range(0, rows, 8)
            ]
            for h in range(8):
                out[e, h, :, lanes] = jnp.concatenate([half[h][0] for half in halves], axis=0).astype(BF16)
        return carry

    lax.fori_loop(0, eights, one_group, 0, unroll=2)


def project(slabs, which, n_pieces, weights, centre, gain, bias):
    rows = 16
    hidden, channels = weights.shape[0] // 2, weights.shape[1]
    count, columns = slabs[0].shape[0] // n_pieces, slabs[0].shape[1]
    depth = n_pieces * columns
    steps = count // rows
    whole = lambda x: pl.BlockSpec(x.shape, lambda i, which: (0,) * x.ndim)

    def piece_spec(n, p):
        return pl.BlockSpec(
            (rows, columns, channels), lambda i, which: (p * steps + jnp.where(which[0] == n, i, 0), 0, 0)
        )

    shape = jax.ShapeDtypeStruct((hidden // 8, 8, count, depth), BF16)
    side = pl.pallas_call(
        functools.partial(project_kernel, n_pieces, len(slabs)),
        grid_spec=pltpu.PrefetchScalarGridSpec(
            num_scalar_prefetch=1,
            grid=(steps,),
            in_specs=[piece_spec(n, p) for n in range(len(slabs)) for p in range(n_pieces)]
            + [whole(x) for x in (weights, centre, gain, bias)],
            out_specs=pl.BlockSpec((hidden // 8, 8, rows, depth), lambda i, which: (0, 0, i, 0)),
            scratch_shapes=[pltpu.VMEM((rows, hidden, depth), F32)],
        ),
        out_shape=shape,
        compiler_params=PARAMS,
        cost_estimate=at_least(count * depth * channels * (channels + 2 * hidden), count * depth * hidden, shape),
        name="project",
    )(which, *[slab for slab in slabs for _ in range(n_pieces)], weights, centre, gain, bias)
    return side.reshape(hidden, count, depth)


def triangle_kernel(n_left, n_sides, group, pairs, which, *refs):
    lefts, out = refs[:n_left], refs[-1]
    sides = refs[n_left:-1]
    step = lefts[0].shape[0]

    def go(choice):
        def one_group(g, carry):
            for n, (i, j) in enumerate(pairs):
                side = sides[j * n_sides + choice]
                parts = [contract(lefts[i][g * group + h], side[g * group + h], 1, 1) for h in range(group)]
                out[n, g] = jnp.concatenate(parts, axis=-1).astype(BF16)
            return carry

        lax.fori_loop(0, step // group, one_group, 0, unroll=2)

    for n in range(n_sides):
        pl.when(which[0] == n)(functools.partial(go, n))


def group_of(columns):
    return 128 // math.gcd(columns, 128)


def triangle(lefts, rights, pairs, which):
    hidden, rows, depth = lefts[0].shape
    columns = rights[0][0].shape[1]
    n_sides = len(rights[0])
    group = group_of(columns)
    step = max(16 if len(rights) > 3 else 32, group)
    shape = jax.ShapeDtypeStruct((len(pairs), hidden // group, rows, group * columns), BF16)

    def side_spec(n):
        return pl.BlockSpec((step, columns, depth), lambda h, which: (jnp.where(which[0] == n, h, 0), 0, 0))

    return pl.pallas_call(
        functools.partial(triangle_kernel, len(lefts), n_sides, group, pairs),
        grid_spec=pltpu.PrefetchScalarGridSpec(
            num_scalar_prefetch=1,
            grid=(hidden // step,),
            in_specs=[pl.BlockSpec((step, rows, depth), lambda h, which: (h, 0, 0))] * len(lefts)
            + [side_spec(n) for _ in rights for n in range(n_sides)],
            out_specs=pl.BlockSpec(
                (len(pairs), step // group, rows, group * columns), lambda h, which: (0, h, 0, 0)
            ),
        ),
        out_shape=shape,
        compiler_params=PARAMS,
        cost_estimate=at_least(
            len(pairs) * hidden * rows * columns * depth, 0, shape, *lefts, *[side[0] for side in rights]
        ),
        name="triangle",
    )(which, *lefts, *[x for side in rights for x in side])


def gate_kernel(pair, centre, mean, gain, bias, weights, out):
    rows, columns, channels = pair.shape
    values = pair[...].reshape(rows * columns, channels)
    centred = contract(values, centre[...], 1, 0)
    square = centred * centred
    high = square.astype(BF16)
    low = (square - high.astype(F32)).astype(BF16)
    variance = contract(jnp.concatenate([high, low], axis=1), mean[...], 1, 0)
    normed = (centred * lax.rsqrt(variance + EPS) * gain[...] + bias[...]).astype(BF16)
    gate = sigmoid(contract(normed, weights[...], 1, 0))
    out[...] = gate.astype(BF16).reshape(rows, columns, channels)


def gate_of(pair, centre, mean, gain, bias, weights):
    rows = 8
    count, columns, channels = pair.shape
    whole = lambda x: pl.BlockSpec(x.shape, lambda i: (0,) * x.ndim)
    block = pl.BlockSpec((rows, columns, channels), lambda i: (i, 0, 0))
    return pl.pallas_call(
        gate_kernel,
        grid=(count // rows,),
        in_specs=[block] + [whole(x) for x in (centre, mean, gain, bias, weights)],
        out_specs=block,
        out_shape=jax.ShapeDtypeStruct(pair.shape, BF16),
        compiler_params=PARAMS,
        cost_estimate=at_least(
            count * columns * channels * 4 * channels, count * columns * channels, pair, pair
        ),
        name="gate",
    )(pair, centre, mean, gain, bias, weights)


def finish_kernel(group, hidden, own, sent, gate, weights, gain, bias, *refs):
    out, rows_of = refs[-2:]
    packed, rows, lanes = own.shape
    columns = lanes // group

    def over_hidden(x):
        total = jnp.sum(x, axis=0)
        shift = columns
        while shift < lanes:
            total = total + pltpu.roll(total, shift, 1)
            shift *= 2
        return total * (1.0 / hidden)

    total = own[...].astype(F32) + sent[...].astype(F32)
    centred = total - over_hidden(total)[None]
    scale = lax.rsqrt(over_hidden(centred * centred) + EPS)
    normed = centred * scale[None] * gain[...] + bias[...]
    rows_of[...] = normed.reshape(packed * rows, lanes)
    for i in range(rows):
        held = rows_of[pl.ds(i, packed, stride=rows), :]
        parts = [held[:, g * columns : (g + 1) * columns] for g in range(group)]
        result = contract(jnp.concatenate(parts, axis=0).astype(BF16), weights[...], 0, 0)
        out[i] = (result * gate[i].astype(F32)).astype(BF16)


def finish(own, sent, gate, t, before, chunks, share, weights, gain, bias, held):
    pieces, packed, count, lanes = own.shape
    rows = count if count <= 32 else 16
    hidden, channels = weights.shape
    group = hidden // packed
    steps = count // rows

    def row_of(p):
        return jnp.where(p < before, p // share, t)

    def column_of(p):
        of_row = p - before
        return jnp.where(p < before, (p % share) * chunks + t, (of_row % share) * chunks + of_row // share)

    whole = lambda x: pl.BlockSpec(x.shape, lambda p, r: (0,) * x.ndim)
    part = pl.BlockSpec((None, packed, rows, lanes), lambda p, r: (p, 0, r, 0))
    block = pl.BlockSpec((rows, lanes // group, channels), lambda p, r: (row_of(p) * steps + r, column_of(p), 0))
    earlier = [] if held is None else [held]
    return pl.pallas_call(
        functools.partial(finish_kernel, group, hidden),
        grid=(pieces, steps),
        in_specs=[part, part, block, whole(weights), whole(gain), whole(bias)]
        + [pl.BlockSpec(memory_space=pl.ANY)] * len(earlier),
        out_specs=block,
        out_shape=jax.ShapeDtypeStruct(gate.shape, BF16),
        scratch_shapes=[pltpu.VMEM((packed * rows, lanes), F32)],
        input_output_aliases={6: 0} if earlier else {},
        compiler_params=PARAMS,
        cost_estimate=at_least(
            pieces * count * (lanes // group) * hidden * channels, pieces * count * (lanes // group), own, sent
        ),
        name="finish",
    )(own, sent, gate, weights, gain, bias, *earlier)


def after(value, *others):
    return lax.optimization_barrier((value,) + others)[0]


def on_device(n_row, n_col, pair_act, ln_gain, ln_bias, w_proj, w_gate, out_gain, out_bias, w_out):
    tile_rows, tile_cols, channels = pair_act.shape
    hidden = w_proj.shape[1] // 4
    half = n_col // 2
    top = n_row // 2
    share = n_row // n_col
    row, col = lax.axis_index("row"), lax.axis_index("col")
    axes = ("row", "col")
    place = lambda r, c: r * n_col + c
    chunks = min(CHUNKS, tile_rows // 16)
    step = tile_rows // chunks
    group = group_of(step)
    packed = hidden // group

    w_left, w_right = w_proj.T[: 2 * hidden], w_proj.T[2 * hidden :]
    centre = (jnp.eye(channels, dtype=F32) - 1.0 / channels).astype(BF16)
    mean = jnp.full((2 * channels, channels), 1.0 / channels, BF16)
    by_hidden = lambda v: jnp.repeat(v.reshape(packed, group), step, axis=1)[:, None, :]
    gain_out, bias_out = by_hidden(out_gain), by_hidden(out_bias)
    w_last = w_out.reshape(packed, group, channels).swapaxes(0, 1).reshape(hidden, channels)

    def holds(r, c):
        return (r // share) % half == c % half

    def across_top(near):
        pairs = [(place(r, c), place(r ^ top, c)) for r in range(n_row) for c in range(n_col) if holds(r, c)]
        return lax.ppermute(near, axes, pairs)

    def to_all_rows(held):
        bit = top // 2
        while bit >= share:
            alike = (bit * 2 - 1) & ~(share - 1)
            sends = [
                (place(r, c), place(r ^ bit, c))
                for r in range(n_row)
                for c in range(n_col)
                if (r ^ (c * share)) & alike == 0
            ]
            came = lax.ppermute(held, axes, sends)
            if bit == 1:
                return [[held, came]]
            held = jnp.where(((row ^ (col * share)) & bit) == 0, held, came)
            bit //= 2
        slabs = [held]
        while bit >= 1:
            swap = [(r, r ^ bit) for r in range(n_row)]
            others = [lax.ppermute(x, "row", swap) for x in slabs]
            slabs = [jnp.where((row & bit) == 0, a, b) for a, b in zip(slabs + others, others + slabs)]
            bit //= 2
        return [[x] for x in slabs]

    near_is_own = (row // top) == (col // half)
    swap_half = [(c, c ^ half) for c in range(n_col)]
    two_chips = share == 1 and top == 2
    holder = ((row ^ col) & 1) == 0
    number = lambda x: jnp.asarray(x, jnp.int32).reshape(1)
    payloads, firsts, lefts, spread, right_sent, right_own = [], [], [], {}, {}, {}

    def first_step(slab):
        if not two_chips:
            return across_top(slab)
        pairs = [(place(r, c), place(r ^ top ^ 1, c)) for r in range(n_row) for c in range(n_col) if holds(r, c)]
        return lax.ppermute(slab, axes, pairs)

    def second_step(slab, far, *waits):
        if not two_chips:
            odd = (row ^ col) & 1
            shards_of = zip(to_all_rows(slab), to_all_rows(far))
            return [(a + b, odd if len(a) > 1 else 0, len(a) + (odd if len(a) > 1 else 0)) for a, b in shards_of]
        given = jnp.where(holder, slab, after(far, *waits))
        got = lax.ppermute(given, "row", [(r, r ^ 1) for r in range(n_row)])
        return [([slab, got, far], jnp.where(holder, 0, 1), jnp.where(holder, 1, 2))]

    def product(pairs, rights):
        used_left = sorted({i for i, _, _ in pairs})
        used_right = sorted({(j, s) for _, j, s in pairs})
        return triangle(
            [lefts[i] for i in used_left],
            [[rights[key]] for key in used_right],
            [(used_left.index(i), used_right.index((j, s))) for i, j, s in pairs],
            number(0),
        )

    wide = lambda v: jnp.broadcast_to(v[:, None], (channels, 2 * half * tile_cols))
    gain_in, bias_in = wide(ln_gain), wide(ln_bias)
    shards = range(share)
    waves = []
    for t in range(chunks):
        by_column = [(i, t, s) for i in range(t) for s in shards]
        by_row = [(t, j, s) for j in range(t + 1) for s in shards]
        waves.append([by_row, by_column] if t == chunks - 1 and t else [by_column + by_row])

    token, moved, own, exchanged = [], [], [], []

    def side(candidates, choice, weights):
        made = project(candidates, number(choice), half, weights, centre, after(gain_in, *token), bias_in)
        token[:] = [made]
        return made

    def right_of(key, own):
        candidates, near, far = spread[key]
        return side(candidates, jnp.where(near_is_own == own, near, far), w_right)

    def multiply(t, rights):
        made = []
        for pairs in waves[t]:
            lefts[t] = after(lefts[t], *token)
            made.append(product(pairs, rights))
            token[:] = made[-1:]
        return made

    def keep_own():
        t = len(own)
        for s in shards:
            right_own[t, s] = right_of((t, s), True)
        own.append(multiply(t, right_own))

    def exchange(n, *waits):
        block = after(slabs[n], *waits) if waits else slabs[n]
        exchanged.append([lax.ppermute(block, "col", [(c, c ^ o) for c in range(n_col)]) for o in range(1, half)])

    slabs = [pair_act[:step]]
    rest = after(pair_act, slabs[0])
    slabs += [rest[n * step : (n + 1) * step] for n in range(1, chunks)]
    exchange(0)

    def base(n, *waits):
        return jnp.pad(after(slabs[n], *waits) if waits else slabs[n], ((0, (half - 1) * step), (0, 0), (0, 0)))

    bases = [base(n) for n in range(min(2, chunks))]
    gate = gate_of(pair_act, centre, mean, after(ln_gain[None], *slabs, *bases), ln_bias[None], w_gate)
    token[:] = [gate]
    for n in range(chunks + 1):
        waits = token + (exchanged[n][-1:] if n < chunks else [])
        if n >= 3:
            waits = waits + moved[n - 3]
        if n + 1 < chunks:
            exchange(n + 1, *waits)
        if n < chunks:
            payload = after(bases[n], *waits)
            for p, piece in enumerate(exchanged[n]):
                payload = lax.dynamic_update_slice_in_dim(payload, piece, (p + 1) * step, axis=0)
            payloads.append(payload)
            firsts.append(first_step(payloads[n]))
        if n == 0:
            continue
        t = n - 1
        for s, found in enumerate(second_step(payloads[t], firsts[t], *waits)):
            spread[t, s] = found
        if n + 1 < chunks:
            bases.append(base(n + 1, *waits))
            token.append(bases[-1])
        lefts.append(side([payloads[t]], 0, w_left))
        for s in shards:
            right_sent[t, s] = right_of((t, s), False)
        if t == chunks - 1:
            while len(own) < t - 1:
                keep_own()
        made = multiply(t, right_sent)
        waits = moved[t - 1] if t else []
        moved.append([lax.ppermute(after(x, *waits) if waits else x, "col", swap_half) for x in made])
        if t == chunks - 2:
            while len(own) < t // 2:
                keep_own()
    while len(own) < chunks:
        keep_own()
    out = None
    for t in range(chunks):
        for pairs, kept, came in zip(waves[t], own[t], moved[t]):
            before = sum(j == t and i < t for i, j, _ in pairs)
            out = finish(kept, came, gate, t, before, chunks, share, w_last, gain_out, bias_out, out)
    return out


def solution(mesh):
    n_row, n_col = mesh.shape["row"], mesh.shape["col"]
    in_specs = (P(("groups", "row"), "col", None), P(), P(), P(), P(), P(), P(), P())
    out_specs = P(("groups", "row"), "col", None)
    return jax.shard_map(
        functools.partial(on_device, n_row, n_col),
        mesh=mesh,
        in_specs=in_specs,
        out_specs=out_specs,
        check_vma=False,
    )
```

```python
import functools
import math

import jax
import jax.numpy as jnp
from jax import lax
from jax.experimental import pallas as pl
from jax.experimental.pallas import tpu as pltpu
from jax.sharding import PartitionSpec as P

CHUNKS = 6
EPS = 1e-05
F32, BF16 = jnp.float32, jnp.bfloat16
PARAMS = pltpu.CompilerParams(vmem_limit_bytes=52 * 1024 * 1024)


def sigmoid(x):
    return pl.reciprocal(1.0 + jnp.exp(-x), approx=True)


def contract(left, right, left_dim, right_dim):
    return lax.dot_general(
        left, right, (((left_dim,), (right_dim,)), ((), ())), preferred_element_type=F32
    )


def at_least(macs, transcendentals, *arrays):
    return pl.CostEstimate(
        flops=2 * macs,
        transcendentals=transcendentals,
        bytes_accessed=sum(math.prod(x.shape) * x.dtype.itemsize for x in arrays),
    )


def swap_eight(arrays):
    place = lax.broadcasted_iota(jnp.int32, arrays[0].shape, 1)
    for shift in (4, 2, 1):
        low = (place & shift) == 0
        swapped = list(arrays)
        for n in range(8):
            if n & shift == 0:
                one, two = arrays[n], arrays[n + shift]
                swapped[n] = jnp.where(low, one, pltpu.roll(two, shift, 1))
                swapped[n + shift] = jnp.where(low, pltpu.roll(one, 8 - shift, 1), two)
        arrays = swapped
    return arrays


def project_kernel(n_pieces, n_slabs, which, *refs):
    pieces = refs[: n_pieces * n_slabs]
    weights, centre, gain, bias, out, held = refs[n_pieces * n_slabs :]
    eights, _, rows, depth = out.shape
    hidden = eights * 8

    def go(first):
        def two_rows(n, carry):
            values = jnp.concatenate(
                [piece[2 * n + i] for i in range(2) for piece in pieces[first : first + n_pieces]], axis=0
            )
            centred = contract(centre[...], values, 1, 1)
            variance = jnp.mean(centred * centred, axis=0, keepdims=True)
            normed = centred * lax.rsqrt(variance + EPS) * gain[...] + bias[...]
            projected = contract(weights[...], normed.astype(BF16), 1, 0)
            side = sigmoid(projected[:hidden]) * projected[hidden:]
            held[2 * n] = side[:, :depth]
            held[2 * n + 1] = side[:, depth:]
            return carry

        lax.fori_loop(0, rows // 2, two_rows, 0, unroll=2)

    for n in range(n_slabs):
        pl.when(which[0] == n)(functools.partial(go, n * n_pieces))

    def one_group(e, carry):
        at = pl.ds(pl.multiple_of(e * 8, 8), 8)
        for n in range(depth // 128):
            lanes = slice(n * 128, (n + 1) * 128)
            halves = [
                swap_eight([held[first + i, at, lanes][None] for i in range(8)]) for first in range(0, rows, 8)
            ]
            for h in range(8):
                out[e, h, :, lanes] = jnp.concatenate([half[h][0] for half in halves], axis=0).astype(BF16)
        return carry

    lax.fori_loop(0, eights, one_group, 0, unroll=2)


def project(slabs, which, n_pieces, weights, centre, gain, bias):
    rows = 16
    hidden, channels = weights.shape[0] // 2, weights.shape[1]
    count, columns = slabs[0].shape[0] // n_pieces, slabs[0].shape[1]
    depth = n_pieces * columns
    steps = count // rows
    whole = lambda x: pl.BlockSpec(x.shape, lambda i, which: (0,) * x.ndim)

    def piece_spec(n, p):
        return pl.BlockSpec(
            (rows, columns, channels), lambda i, which: (p * steps + jnp.where(which[0] == n, i, 0), 0, 0)
        )

    shape = jax.ShapeDtypeStruct((hidden // 8, 8, count, depth), BF16)
    side = pl.pallas_call(
        functools.partial(project_kernel, n_pieces, len(slabs)),
        grid_spec=pltpu.PrefetchScalarGridSpec(
            num_scalar_prefetch=1,
            grid=(steps,),
            in_specs=[piece_spec(n, p) for n in range(len(slabs)) for p in range(n_pieces)]
            + [whole(x) for x in (weights, centre, gain, bias)],
            out_specs=pl.BlockSpec((hidden // 8, 8, rows, depth), lambda i, which: (0, 0, i, 0)),
            scratch_shapes=[pltpu.VMEM((rows, hidden, depth), F32)],
        ),
        out_shape=shape,
        compiler_params=PARAMS,
        cost_estimate=at_least(count * depth * channels * (channels + 2 * hidden), count * depth * hidden, shape),
        name="project",
    )(which, *[slab for slab in slabs for _ in range(n_pieces)], weights, centre, gain, bias)
    return side.reshape(hidden, count, depth)


def triangle_kernel(n_left, n_sides, group, pairs, which, *refs):
    lefts, out = refs[:n_left], refs[-1]
    sides = refs[n_left:-1]
    step, rows, _ = lefts[0].shape
    columns = sides[0].shape[1]

    def go(choice):
        def pieces_of(h):
            found = {}
            for j in sorted({j for _, j in pairs}):
                same = [n for n, pair in enumerate(pairs) if pair[1] == j]
                if len(same) > 1:
                    rows_of = jnp.concatenate([lefts[pairs[n][0]][h] for n in same], axis=0)
                    made = contract(rows_of, sides[j * n_sides + choice][h], 1, 1)
                    found.update({n: made[p * rows : (p + 1) * rows] for p, n in enumerate(same)})
            for i in sorted({i for i, _ in pairs}):
                same = [n for n, pair in enumerate(pairs) if pair[0] == i and n not in found]
                if same:
                    columns_of = jnp.concatenate([sides[pairs[n][1] * n_sides + choice][h] for n in same], axis=0)
                    made = contract(lefts[i][h], columns_of, 1, 1)
                    found.update({n: made[:, p * columns : (p + 1) * columns] for p, n in enumerate(same)})
            return found

        def one_group(g, carry):
            found = [pieces_of(g * group + h) for h in range(group)]
            for n in range(len(pairs)):
                out[n, g] = jnp.concatenate([x[n] for x in found], axis=-1).astype(BF16)
            return carry

        lax.fori_loop(0, step // group, one_group, 0, unroll=2)

    for n in range(n_sides):
        pl.when(which[0] == n)(functools.partial(go, n))


def group_of(columns):
    return 128 // math.gcd(columns, 128)


def triangle(lefts, rights, pairs, which):
    hidden, rows, depth = lefts[0].shape
    columns = rights[0][0].shape[1]
    n_sides = len(rights[0])
    group = group_of(columns)
    step = max(16 if len(rights) > 3 else 32, group)
    shape = jax.ShapeDtypeStruct((len(pairs), hidden // group, rows, group * columns), BF16)

    def side_spec(n):
        return pl.BlockSpec((step, columns, depth), lambda h, which: (jnp.where(which[0] == n, h, 0), 0, 0))

    return pl.pallas_call(
        functools.partial(triangle_kernel, len(lefts), n_sides, group, pairs),
        grid_spec=pltpu.PrefetchScalarGridSpec(
            num_scalar_prefetch=1,
            grid=(hidden // step,),
            in_specs=[pl.BlockSpec((step, rows, depth), lambda h, which: (h, 0, 0))] * len(lefts)
            + [side_spec(n) for _ in rights for n in range(n_sides)],
            out_specs=pl.BlockSpec(
                (len(pairs), step // group, rows, group * columns), lambda h, which: (0, h, 0, 0)
            ),
        ),
        out_shape=shape,
        compiler_params=PARAMS,
        cost_estimate=at_least(
            len(pairs) * hidden * rows * columns * depth, 0, shape, *lefts, *[side[0] for side in rights]
        ),
        name="triangle",
    )(which, *lefts, *[x for side in rights for x in side])


def gate_kernel(pair, centre, mean, gain, bias, weights, out):
    rows, columns, channels = pair.shape
    values = pair[...].reshape(rows * columns, channels)
    centred = contract(values, centre[...], 1, 0)
    square = centred * centred
    high = square.astype(BF16)
    low = (square - high.astype(F32)).astype(BF16)
    variance = contract(jnp.concatenate([high, low], axis=1), mean[...], 1, 0)
    normed = (centred * lax.rsqrt(variance + EPS) * gain[...] + bias[...]).astype(BF16)
    gate = sigmoid(contract(normed, weights[...], 1, 0))
    out[...] = gate.astype(BF16).reshape(rows, columns, channels)


def gate_of(pair, centre, mean, gain, bias, weights):
    rows = 8
    count, columns, channels = pair.shape
    whole = lambda x: pl.BlockSpec(x.shape, lambda i: (0,) * x.ndim)
    block = pl.BlockSpec((rows, columns, channels), lambda i: (i, 0, 0))
    return pl.pallas_call(
        gate_kernel,
        grid=(count // rows,),
        in_specs=[block] + [whole(x) for x in (centre, mean, gain, bias, weights)],
        out_specs=block,
        out_shape=jax.ShapeDtypeStruct(pair.shape, BF16),
        compiler_params=PARAMS,
        cost_estimate=at_least(
            count * columns * channels * 4 * channels, count * columns * channels, pair, pair
        ),
        name="gate",
    )(pair, centre, mean, gain, bias, weights)


def finish_kernel(group, hidden, own, sent, gate, weights, gain, bias, *refs):
    out, rows_of = refs[-2:]
    packed, rows, lanes = own.shape
    columns = lanes // group

    def over_hidden(x):
        total = jnp.sum(x, axis=0)
        shift = columns
        while shift < lanes:
            total = total + pltpu.roll(total, shift, 1)
            shift *= 2
        return total * (1.0 / hidden)

    total = own[...].astype(F32) + sent[...].astype(F32)
    centred = total - over_hidden(total)[None]
    scale = lax.rsqrt(over_hidden(centred * centred) + EPS)
    normed = centred * scale[None] * gain[...] + bias[...]
    rows_of[...] = normed.reshape(packed * rows, lanes)
    batch = max(1, 128 // columns)
    for first in range(0, rows, batch):
        held = [rows_of[pl.ds(first + i, packed, stride=rows), :] for i in range(batch)]
        parts = [
            jnp.concatenate([x[:, g * columns : (g + 1) * columns] for x in held], axis=1) for g in range(group)
        ]
        result = contract(jnp.concatenate(parts, axis=0).astype(BF16), weights[...], 0, 0)
        for i in range(batch):
            gated = result[i * columns : (i + 1) * columns] * gate[first + i].astype(F32)
            out[first + i] = gated.astype(BF16)


def finish(own, sent, gate, t, before, chunks, share, weights, gain, bias, held):
    pieces, packed, count, lanes = own.shape
    rows = count if count <= 32 else 16
    hidden, channels = weights.shape
    group = hidden // packed
    steps = count // rows

    def row_of(p):
        return jnp.where(p < before, p // share, t)

    def column_of(p):
        of_row = p - before
        return jnp.where(p < before, (p % share) * chunks + t, (of_row % share) * chunks + of_row // share)

    whole = lambda x: pl.BlockSpec(x.shape, lambda p, r: (0,) * x.ndim)
    part = pl.BlockSpec((None, packed, rows, lanes), lambda p, r: (p, 0, r, 0))
    block = pl.BlockSpec((rows, lanes // group, channels), lambda p, r: (row_of(p) * steps + r, column_of(p), 0))
    earlier = [] if held is None else [held]
    return pl.pallas_call(
        functools.partial(finish_kernel, group, hidden),
        grid=(pieces, steps),
        in_specs=[part, part, block, whole(weights), whole(gain), whole(bias)]
        + [pl.BlockSpec(memory_space=pl.ANY)] * len(earlier),
        out_specs=block,
        out_shape=jax.ShapeDtypeStruct(gate.shape, BF16),
        scratch_shapes=[pltpu.VMEM((packed * rows, lanes), F32)],
        input_output_aliases={6: 0} if earlier else {},
        compiler_params=PARAMS,
        cost_estimate=at_least(
            pieces * count * (lanes // group) * hidden * channels, pieces * count * (lanes // group), own, sent
        ),
        name="finish",
    )(own, sent, gate, weights, gain, bias, *earlier)


def after(value, *others):
    return lax.optimization_barrier((value,) + others)[0]


def on_device(n_row, n_col, pair_act, ln_gain, ln_bias, w_proj, w_gate, out_gain, out_bias, w_out):
    tile_rows, tile_cols, channels = pair_act.shape
    hidden = w_proj.shape[1] // 4
    half = n_col // 2
    top = n_row // 2
    share = n_row // n_col
    row, col = lax.axis_index("row"), lax.axis_index("col")
    axes = ("row", "col")
    place = lambda r, c: r * n_col + c
    chunks = min(CHUNKS, tile_rows // 16)
    step = tile_rows // chunks
    group = group_of(step)
    packed = hidden // group

    w_left, w_right = w_proj.T[: 2 * hidden], w_proj.T[2 * hidden :]
    centre = (jnp.eye(channels, dtype=F32) - 1.0 / channels).astype(BF16)
    mean = jnp.full((2 * channels, channels), 1.0 / channels, BF16)
    by_hidden = lambda v: jnp.repeat(v.reshape(packed, group), step, axis=1)[:, None, :]
    gain_out, bias_out = by_hidden(out_gain), by_hidden(out_bias)
    w_last = w_out.reshape(packed, group, channels).swapaxes(0, 1).reshape(hidden, channels)

    def holds(r, c):
        return (r // share) % half == c % half

    def across_top(near):
        pairs = [(place(r, c), place(r ^ top, c)) for r in range(n_row) for c in range(n_col) if holds(r, c)]
        return lax.ppermute(near, axes, pairs)

    def to_all_rows(held):
        bit = top // 2
        while bit >= share:
            alike = (bit * 2 - 1) & ~(share - 1)
            sends = [
                (place(r, c), place(r ^ bit, c))
                for r in range(n_row)
                for c in range(n_col)
                if (r ^ (c * share)) & alike == 0
            ]
            came = lax.ppermute(held, axes, sends)
            if bit == 1:
                return [[held, came]]
            held = jnp.where(((row ^ (col * share)) & bit) == 0, held, came)
            bit //= 2
        slabs = [held]
        while bit >= 1:
            swap = [(r, r ^ bit) for r in range(n_row)]
            others = [lax.ppermute(x, "row", swap) for x in slabs]
            slabs = [jnp.where((row & bit) == 0, a, b) for a, b in zip(slabs + others, others + slabs)]
            bit //= 2
        return [[x] for x in slabs]

    near_is_own = (row // top) == (col // half)
    swap_half = [(c, c ^ half) for c in range(n_col)]
    two_chips = share == 1 and top == 2
    holder = ((row ^ col) & 1) == 0
    number = lambda x: jnp.asarray(x, jnp.int32).reshape(1)
    payloads, firsts, lefts, spread, right_sent, right_own = [], [], [], {}, {}, {}

    def first_step(slab):
        if not two_chips:
            return across_top(slab)
        pairs = [(place(r, c), place(r ^ top ^ 1, c)) for r in range(n_row) for c in range(n_col) if holds(r, c)]
        return lax.ppermute(slab, axes, pairs)

    def second_step(slab, far, *waits):
        if not two_chips:
            odd = (row ^ col) & 1
            shards_of = zip(to_all_rows(slab), to_all_rows(far))
            return [(a + b, odd if len(a) > 1 else 0, len(a) + (odd if len(a) > 1 else 0)) for a, b in shards_of]
        given = jnp.where(holder, slab, after(far, *waits))
        got = lax.ppermute(given, "row", [(r, r ^ 1) for r in range(n_row)])
        return [([slab, got, far], jnp.where(holder, 0, 1), jnp.where(holder, 1, 2))]

    def product(pairs, rights):
        used_left = sorted({i for i, _, _ in pairs})
        used_right = sorted({(j, s) for _, j, s in pairs})
        return triangle(
            [lefts[i] for i in used_left],
            [[rights[key]] for key in used_right],
            [(used_left.index(i), used_right.index((j, s))) for i, j, s in pairs],
            number(0),
        )

    wide = lambda v: jnp.broadcast_to(v[:, None], (channels, 2 * half * tile_cols))
    gain_in, bias_in = wide(ln_gain), wide(ln_bias)
    shards = range(share)
    waves = []
    for t in range(chunks):
        by_column = [(i, t, s) for i in range(t) for s in shards]
        by_row = [(t, j, s) for j in range(t + 1) for s in shards]
        waves.append([by_row, by_column] if t == chunks - 1 and t else [by_column + by_row])

    token, moved, own, exchanged = [], [], [], []

    def side(candidates, choice, weights):
        made = project(candidates, number(choice), half, weights, centre, after(gain_in, *token), bias_in)
        token[:] = [made]
        return made

    def right_of(key, own):
        candidates, near, far = spread[key]
        return side(candidates, jnp.where(near_is_own == own, near, far), w_right)

    def multiply(t, rights):
        made = []
        for pairs in waves[t]:
            lefts[t] = after(lefts[t], *token)
            made.append(product(pairs, rights))
            token[:] = made[-1:]
        return made

    def keep_own():
        t = len(own)
        for s in shards:
            right_own[t, s] = right_of((t, s), True)
        own.append(multiply(t, right_own))

    def exchange(n, *waits):
        block = after(slabs[n], *waits) if waits else slabs[n]
        exchanged.append([lax.ppermute(block, "col", [(c, c ^ o) for c in range(n_col)]) for o in range(1, half)])

    slabs = [pair_act[:step]]
    rest = after(pair_act, slabs[0])
    slabs += [rest[n * step : (n + 1) * step] for n in range(1, chunks)]
    exchange(0)

    def base(n, *waits):
        return jnp.pad(after(slabs[n], *waits) if waits else slabs[n], ((0, (half - 1) * step), (0, 0), (0, 0)))

    bases = [base(n) for n in range(min(2, chunks))]
    gate = gate_of(pair_act, centre, mean, after(ln_gain[None], *slabs, *bases), ln_bias[None], w_gate)
    token[:] = [gate]
    for n in range(chunks + 1):
        waits = token + (exchanged[n][-1:] if n < chunks else [])
        if n >= 3:
            waits = waits + moved[n - 3]
        if n + 1 < chunks:
            exchange(n + 1, *waits)
        if n < chunks:
            payload = after(bases[n], *waits)
            for p, piece in enumerate(exchanged[n]):
                payload = lax.dynamic_update_slice_in_dim(payload, piece, (p + 1) * step, axis=0)
            payloads.append(payload)
            firsts.append(first_step(payloads[n]))
        if n == 0:
            continue
        t = n - 1
        for s, found in enumerate(second_step(payloads[t], firsts[t], *waits)):
            spread[t, s] = found
        if n + 1 < chunks:
            bases.append(base(n + 1, *waits))
            token.append(bases[-1])
        lefts.append(side([payloads[t]], 0, w_left))
        for s in shards:
            right_sent[t, s] = right_of((t, s), False)
        if t == chunks - 1:
            while len(own) < t - 1:
                keep_own()
        made = multiply(t, right_sent)
        waits = moved[t - 1] if t else []
        moved.append([lax.ppermute(after(x, *waits) if waits else x, "col", swap_half) for x in made])
        if t == chunks - 2:
            while len(own) < t // 2:
                keep_own()
    while len(own) < chunks:
        keep_own()
    out = None
    for t in range(chunks):
        for pairs, kept, came in zip(waves[t], own[t], moved[t]):
            before = sum(j == t and i < t for i, j, _ in pairs)
            out = finish(kept, came, gate, t, before, chunks, share, w_last, gain_out, bias_out, out)
    return out


def solution(mesh):
    n_row, n_col = mesh.shape["row"], mesh.shape["col"]
    in_specs = (P(("groups", "row"), "col", None), P(), P(), P(), P(), P(), P(), P())
    out_specs = P(("groups", "row"), "col", None)
    return jax.shard_map(
        functools.partial(on_device, n_row, n_col),
        mesh=mesh,
        in_specs=in_specs,
        out_specs=out_specs,
        check_vma=False,
    )
```

```python
import functools
import math

import jax
import jax.numpy as jnp
from jax import lax
from jax.experimental import pallas as pl
from jax.experimental.pallas import tpu as pltpu
from jax.sharding import PartitionSpec as P

CHUNKS = 6
EPS = 1e-05
F32, BF16 = jnp.float32, jnp.bfloat16
PARAMS = pltpu.CompilerParams(vmem_limit_bytes=52 * 1024 * 1024)


def sigmoid(x):
    return pl.reciprocal(1.0 + jnp.exp(-x), approx=True)


def contract(left, right, left_dim, right_dim):
    return lax.dot_general(
        left, right, (((left_dim,), (right_dim,)), ((), ())), preferred_element_type=F32
    )


def at_least(macs, transcendentals, *arrays):
    return pl.CostEstimate(
        flops=2 * macs,
        transcendentals=transcendentals,
        bytes_accessed=sum(math.prod(x.shape) * x.dtype.itemsize for x in arrays),
    )


def swap_eight(arrays):
    place = lax.broadcasted_iota(jnp.int32, arrays[0].shape, 1)
    for shift in (4, 2, 1):
        low = (place & shift) == 0
        swapped = list(arrays)
        for n in range(8):
            if n & shift == 0:
                one, two = arrays[n], arrays[n + shift]
                swapped[n] = jnp.where(low, one, pltpu.roll(two, shift, 1))
                swapped[n + shift] = jnp.where(low, pltpu.roll(one, 8 - shift, 1), two)
        arrays = swapped
    return arrays


def project_kernel(n_pieces, n_slabs, which, *refs):
    pieces = refs[: n_pieces * n_slabs]
    weights, centre, gain, bias, out, held = refs[n_pieces * n_slabs :]
    eights, _, rows, depth = out.shape
    hidden = eights * 8

    def go(first):
        def two_rows(n, carry):
            values = jnp.concatenate(
                [piece[2 * n + i] for i in range(2) for piece in pieces[first : first + n_pieces]], axis=0
            )
            centred = contract(centre[...], values, 1, 1)
            variance = jnp.mean(centred * centred, axis=0, keepdims=True)
            normed = centred * lax.rsqrt(variance + EPS) * gain[...] + bias[...]
            projected = contract(weights[...], normed.astype(BF16), 1, 0)
            side = sigmoid(projected[:hidden]) * projected[hidden:]
            held[2 * n] = side[:, :depth]
            held[2 * n + 1] = side[:, depth:]
            return carry

        lax.fori_loop(0, rows // 2, two_rows, 0, unroll=2)

    for n in range(n_slabs):
        pl.when(which[0] == n)(functools.partial(go, n * n_pieces))

    def one_group(e, carry):
        at = pl.ds(pl.multiple_of(e * 8, 8), 8)
        for n in range(depth // 128):
            lanes = slice(n * 128, (n + 1) * 128)
            halves = [
                swap_eight([held[first + i, at, lanes][None] for i in range(8)]) for first in range(0, rows, 8)
            ]
            for h in range(8):
                out[e, h, :, lanes] = jnp.concatenate([half[h][0] for half in halves], axis=0).astype(BF16)
        return carry

    lax.fori_loop(0, eights, one_group, 0, unroll=2)


def project(slabs, which, n_pieces, weights, centre, gain, bias):
    rows = 16
    hidden, channels = weights.shape[0] // 2, weights.shape[1]
    count, columns = slabs[0].shape[0] // n_pieces, slabs[0].shape[1]
    depth = n_pieces * columns
    steps = count // rows
    whole = lambda x: pl.BlockSpec(x.shape, lambda i, which: (0,) * x.ndim)

    def piece_spec(n, p):
        return pl.BlockSpec(
            (rows, columns, channels), lambda i, which: (p * steps + jnp.where(which[0] == n, i, 0), 0, 0)
        )

    shape = jax.ShapeDtypeStruct((hidden // 8, 8, count, depth), BF16)
    side = pl.pallas_call(
        functools.partial(project_kernel, n_pieces, len(slabs)),
        grid_spec=pltpu.PrefetchScalarGridSpec(
            num_scalar_prefetch=1,
            grid=(steps,),
            in_specs=[piece_spec(n, p) for n in range(len(slabs)) for p in range(n_pieces)]
            + [whole(x) for x in (weights, centre, gain, bias)],
            out_specs=pl.BlockSpec((hidden // 8, 8, rows, depth), lambda i, which: (0, 0, i, 0)),
            scratch_shapes=[pltpu.VMEM((rows, hidden, depth), F32)],
        ),
        out_shape=shape,
        compiler_params=PARAMS,
        cost_estimate=at_least(count * depth * channels * (channels + 2 * hidden), count * depth * hidden, shape),
        name="project",
    )(which, *[slab for slab in slabs for _ in range(n_pieces)], weights, centre, gain, bias)
    return side.reshape(hidden, count, depth)


def triangle_kernel(n_left, n_sides, group, pairs, which, *refs):
    lefts, out = refs[:n_left], refs[-1]
    sides = refs[n_left:-1]
    step, rows, _ = lefts[0].shape
    columns = sides[0].shape[1]

    def go(choice):
        def pieces_of(h):
            found = {}
            for j in sorted({j for _, j in pairs}):
                same = [n for n, pair in enumerate(pairs) if pair[1] == j]
                if len(same) > 1:
                    rows_of = jnp.concatenate([lefts[pairs[n][0]][h] for n in same], axis=0)
                    made = contract(rows_of, sides[j * n_sides + choice][h], 1, 1)
                    found.update({n: made[p * rows : (p + 1) * rows] for p, n in enumerate(same)})
            for i in sorted({i for i, _ in pairs}):
                same = [n for n, pair in enumerate(pairs) if pair[0] == i and n not in found]
                if same:
                    columns_of = jnp.concatenate([sides[pairs[n][1] * n_sides + choice][h] for n in same], axis=0)
                    made = contract(lefts[i][h], columns_of, 1, 1)
                    found.update({n: made[:, p * columns : (p + 1) * columns] for p, n in enumerate(same)})
            return found

        def one_group(g, carry):
            found = [pieces_of(g * group + h) for h in range(group)]
            for n in range(len(pairs)):
                out[n, g] = jnp.concatenate([x[n] for x in found], axis=-1).astype(BF16)
            return carry

        lax.fori_loop(0, step // group, one_group, 0, unroll=2)

    for n in range(n_sides):
        pl.when(which[0] == n)(functools.partial(go, n))


def group_of(columns):
    return 128 // math.gcd(columns, 128)


def triangle(lefts, rights, pairs, which):
    hidden, rows, depth = lefts[0].shape
    columns = rights[0][0].shape[1]
    n_sides = len(rights[0])
    group = group_of(columns)
    step = max(16 if len(rights) > 3 else 32, group)
    shape = jax.ShapeDtypeStruct((len(pairs), hidden // group, rows, group * columns), BF16)

    def side_spec(n):
        return pl.BlockSpec((step, columns, depth), lambda h, which: (jnp.where(which[0] == n, h, 0), 0, 0))

    return pl.pallas_call(
        functools.partial(triangle_kernel, len(lefts), n_sides, group, pairs),
        grid_spec=pltpu.PrefetchScalarGridSpec(
            num_scalar_prefetch=1,
            grid=(hidden // step,),
            in_specs=[pl.BlockSpec((step, rows, depth), lambda h, which: (h, 0, 0))] * len(lefts)
            + [side_spec(n) for _ in rights for n in range(n_sides)],
            out_specs=pl.BlockSpec(
                (len(pairs), step // group, rows, group * columns), lambda h, which: (0, h, 0, 0)
            ),
        ),
        out_shape=shape,
        compiler_params=PARAMS,
        cost_estimate=at_least(
            len(pairs) * hidden * rows * columns * depth, 0, shape, *lefts, *[side[0] for side in rights]
        ),
        name="triangle",
    )(which, *lefts, *[x for side in rights for x in side])


def gate_kernel(pair, centre, mean, gain, bias, weights, out):
    rows, columns, channels = pair.shape
    values = pair[...].reshape(rows * columns, channels)
    centred = contract(values, centre[...], 1, 0)
    square = centred * centred
    high = square.astype(BF16)
    low = (square - high.astype(F32)).astype(BF16)
    variance = contract(jnp.concatenate([high, low], axis=1), mean[...], 1, 0)
    normed = (centred * lax.rsqrt(variance + EPS) * gain[...] + bias[...]).astype(BF16)
    gate = sigmoid(contract(normed, weights[...], 1, 0))
    out[...] = gate.astype(BF16).reshape(rows, columns, channels)


def gate_of(pair, centre, mean, gain, bias, weights):
    rows = 8
    count, columns, channels = pair.shape
    whole = lambda x: pl.BlockSpec(x.shape, lambda i: (0,) * x.ndim)
    block = pl.BlockSpec((rows, columns, channels), lambda i: (i, 0, 0))
    return pl.pallas_call(
        gate_kernel,
        grid=(count // rows,),
        in_specs=[block] + [whole(x) for x in (centre, mean, gain, bias, weights)],
        out_specs=block,
        out_shape=jax.ShapeDtypeStruct(pair.shape, BF16),
        compiler_params=PARAMS,
        cost_estimate=at_least(
            count * columns * channels * 4 * channels, count * columns * channels, pair, pair
        ),
        name="gate",
    )(pair, centre, mean, gain, bias, weights)


def finish_kernel(group, hidden, own, sent, gate, weights, gain, bias, *refs):
    out, rows_of = refs[-2:]
    packed, rows, lanes = own.shape
    columns = lanes // group

    def over_hidden(x):
        total = jnp.sum(x, axis=0)
        shift = columns
        while shift < lanes:
            total = total + pltpu.roll(total, shift, 1)
            shift *= 2
        return total * (1.0 / hidden)

    total = own[...].astype(F32) + sent[...].astype(F32)
    centred = total - over_hidden(total)[None]
    scale = lax.rsqrt(over_hidden(centred * centred) + EPS)
    normed = centred * scale[None] * gain[...] + bias[...]
    rows_of[...] = normed.reshape(packed * rows, lanes)
    batch = max(1, 128 // columns)
    for first in range(0, rows, batch):
        held = [rows_of[pl.ds(first + i, packed, stride=rows), :] for i in range(batch)]
        parts = [
            jnp.concatenate([x[:, g * columns : (g + 1) * columns] for x in held], axis=1) for g in range(group)
        ]
        result = contract(jnp.concatenate(parts, axis=0).astype(BF16), weights[...], 0, 0)
        for i in range(batch):
            gated = result[i * columns : (i + 1) * columns] * gate[first + i].astype(F32)
            out[first + i] = gated.astype(BF16)


def finish(own, sent, gate, t, before, chunks, share, weights, gain, bias, held):
    pieces, packed, count, lanes = own.shape
    rows = count if count <= 32 else 16
    hidden, channels = weights.shape
    group = hidden // packed
    steps = count // rows

    def row_of(p):
        return jnp.where(p < before, p // share, t)

    def column_of(p):
        of_row = p - before
        return jnp.where(p < before, (p % share) * chunks + t, (of_row % share) * chunks + of_row // share)

    whole = lambda x: pl.BlockSpec(x.shape, lambda p, r: (0,) * x.ndim)
    part = pl.BlockSpec((None, packed, rows, lanes), lambda p, r: (p, 0, r, 0))
    block = pl.BlockSpec((rows, lanes // group, channels), lambda p, r: (row_of(p) * steps + r, column_of(p), 0))
    earlier = [] if held is None else [held]
    return pl.pallas_call(
        functools.partial(finish_kernel, group, hidden),
        grid=(pieces, steps),
        in_specs=[part, part, block, whole(weights), whole(gain), whole(bias)]
        + [pl.BlockSpec(memory_space=pl.ANY)] * len(earlier),
        out_specs=block,
        out_shape=jax.ShapeDtypeStruct(gate.shape, BF16),
        scratch_shapes=[pltpu.VMEM((packed * rows, lanes), F32)],
        input_output_aliases={6: 0} if earlier else {},
        compiler_params=PARAMS,
        cost_estimate=at_least(
            pieces * count * (lanes // group) * hidden * channels, pieces * count * (lanes // group), own, sent
        ),
        name="finish",
    )(own, sent, gate, weights, gain, bias, *earlier)


def after(value, *others):
    return lax.optimization_barrier((value,) + others)[0]


def on_device(n_row, n_col, pair_act, ln_gain, ln_bias, w_proj, w_gate, out_gain, out_bias, w_out):
    tile_rows, tile_cols, channels = pair_act.shape
    hidden = w_proj.shape[1] // 4
    half = n_col // 2
    top = n_row // 2
    share = n_row // n_col
    row, col = lax.axis_index("row"), lax.axis_index("col")
    axes = ("row", "col")
    place = lambda r, c: r * n_col + c
    chunks = min(CHUNKS, tile_rows // 16)
    step = tile_rows // chunks
    group = group_of(step)
    packed = hidden // group

    w_left, w_right = w_proj.T[: 2 * hidden], w_proj.T[2 * hidden :]
    centre = (jnp.eye(channels, dtype=F32) - 1.0 / channels).astype(BF16)
    mean = jnp.full((2 * channels, channels), 1.0 / channels, BF16)
    by_hidden = lambda v: jnp.repeat(v.reshape(packed, group), step, axis=1)[:, None, :]
    gain_out, bias_out = by_hidden(out_gain), by_hidden(out_bias)
    w_last = w_out.reshape(packed, group, channels).swapaxes(0, 1).reshape(hidden, channels)

    def holds(r, c):
        return (r // share) % half == c % half

    def across_top(near):
        pairs = [(place(r, c), place(r ^ top, c)) for r in range(n_row) for c in range(n_col) if holds(r, c)]
        return lax.ppermute(near, axes, pairs)

    def to_all_rows(held):
        bit = top // 2
        while bit >= share:
            alike = (bit * 2 - 1) & ~(share - 1)
            sends = [
                (place(r, c), place(r ^ bit, c))
                for r in range(n_row)
                for c in range(n_col)
                if (r ^ (c * share)) & alike == 0
            ]
            came = lax.ppermute(held, axes, sends)
            if bit == 1:
                return [[held, came]]
            held = jnp.where(((row ^ (col * share)) & bit) == 0, held, came)
            bit //= 2
        slabs = [held]
        while bit >= 1:
            swap = [(r, r ^ bit) for r in range(n_row)]
            others = [lax.ppermute(x, "row", swap) for x in slabs]
            slabs = [jnp.where((row & bit) == 0, a, b) for a, b in zip(slabs + others, others + slabs)]
            bit //= 2
        return [[x] for x in slabs]

    near_is_own = (row // top) == (col // half)
    swap_half = [(c, c ^ half) for c in range(n_col)]
    two_chips = share == 1 and top == 2
    holder = ((row ^ col) & 1) == 0
    number = lambda x: jnp.asarray(x, jnp.int32).reshape(1)
    payloads, firsts, lefts, spread, right_sent, right_own = [], [], [], {}, {}, {}

    def first_step(slab):
        if not two_chips:
            return across_top(slab)
        pairs = [(place(r, c), place(r ^ top ^ 1, c)) for r in range(n_row) for c in range(n_col) if holds(r, c)]
        return lax.ppermute(slab, axes, pairs)

    def second_step(slab, far, *waits):
        if not two_chips:
            odd = (row ^ col) & 1
            shards_of = zip(to_all_rows(slab), to_all_rows(far))
            return [(a + b, odd if len(a) > 1 else 0, len(a) + (odd if len(a) > 1 else 0)) for a, b in shards_of]
        given = jnp.where(holder, slab, after(far, *waits))
        got = lax.ppermute(given, "row", [(r, r ^ 1) for r in range(n_row)])
        return [([slab, got, far], jnp.where(holder, 0, 1), jnp.where(holder, 1, 2))]

    def product(pairs, rights):
        used_left = sorted({i for i, _, _ in pairs})
        used_right = sorted({(j, s) for _, j, s in pairs})
        return triangle(
            [lefts[i] for i in used_left],
            [[rights[key]] for key in used_right],
            [(used_left.index(i), used_right.index((j, s))) for i, j, s in pairs],
            number(0),
        )

    wide = lambda v: jnp.broadcast_to(v[:, None], (channels, 2 * half * tile_cols))
    gain_in, bias_in = wide(ln_gain), wide(ln_bias)
    shards = range(share)
    waves = []
    for t in range(chunks):
        by_column = [(i, t, s) for i in range(t) for s in shards]
        by_row = [(t, j, s) for j in range(t + 1) for s in shards]
        waves.append([by_row, by_column] if t == chunks - 1 and t else [by_column + by_row])

    token, moved, own, exchanged = [], [], [], []

    def side(candidates, choice, weights):
        made = project(candidates, number(choice), half, weights, centre, after(gain_in, *token), bias_in)
        token[:] = [made]
        return made

    def right_of(key, own):
        candidates, near, far = spread[key]
        return side(candidates, jnp.where(near_is_own == own, near, far), w_right)

    def multiply(t, rights):
        made = []
        for pairs in waves[t]:
            lefts[t] = after(lefts[t], *token)
            made.append(product(pairs, rights))
            token[:] = made[-1:]
        return made

    def keep_own(steps):
        for _ in range(steps):
            t = len(own)
            missing = [s for s in shards if (t, s) not in right_own]
            if t < chunks and missing:
                right_own[t, missing[0]] = right_of((t, missing[0]), True)
            elif t < chunks:
                own.append(multiply(t, right_own))

    def exchange(n, *waits):
        block = after(slabs[n], *waits) if waits else slabs[n]
        exchanged.append([lax.ppermute(block, "col", [(c, c ^ o) for c in range(n_col)]) for o in range(1, half)])

    slabs = [pair_act[:step]]
    rest = after(pair_act, slabs[0])
    slabs += [rest[n * step : (n + 1) * step] for n in range(1, chunks)]
    exchange(0)

    def base(n, *waits):
        return jnp.pad(after(slabs[n], *waits) if waits else slabs[n], ((0, (half - 1) * step), (0, 0), (0, 0)))

    bases = [base(n) for n in range(min(2, chunks))]
    token[:] = slabs + bases
    for n in range(chunks + 1):
        waits = token + (exchanged[n][-1:] if n < chunks else [])
        if n >= 3:
            waits = waits + moved[n - 3]
        if n + 1 < chunks:
            exchange(n + 1, *waits)
        if n < chunks:
            payload = after(bases[n], *waits)
            for p, piece in enumerate(exchanged[n]):
                payload = lax.dynamic_update_slice_in_dim(payload, piece, (p + 1) * step, axis=0)
            payloads.append(payload)
            firsts.append(first_step(payloads[n]))
        if n == 0:
            early = after(ln_gain[None], *waits, gain_out, bias_out, w_last)
            gate = gate_of(pair_act, centre, mean, early, ln_bias[None], w_gate)
            token[:] = [gate]
            continue
        t = n - 1
        for s, found in enumerate(second_step(payloads[t], firsts[t], *waits)):
            spread[t, s] = found
        if n + 1 < chunks:
            bases.append(base(n + 1, *waits))
            token.append(bases[-1])
        lefts.append(side([payloads[t]], 0, w_left))
        for s in shards:
            right_sent[t, s] = right_of((t, s), False)
        if t == chunks - 1:
            keep_own(2)
        made = multiply(t, right_sent)
        waits = moved[t - 1] if t else []
        moved.append([lax.ppermute(after(x, *waits) if waits else x, "col", swap_half) for x in made])
        keep_own({chunks - 4: 1, chunks - 3: 2, chunks - 2: 4}.get(t, 0))
    keep_own(chunks * (share + 1))
    out = None
    for t in range(chunks):
        for pairs, kept, came in zip(waves[t], own[t], moved[t]):
            before = sum(j == t and i < t for i, j, _ in pairs)
            out = finish(kept, came, gate, t, before, chunks, share, w_last, gain_out, bias_out, out)
    return out


def solution(mesh):
    n_row, n_col = mesh.shape["row"], mesh.shape["col"]
    in_specs = (P(("groups", "row"), "col", None), P(), P(), P(), P(), P(), P(), P())
    out_specs = P(("groups", "row"), "col", None)
    return jax.shard_map(
        functools.partial(on_device, n_row, n_col),
        mesh=mesh,
        in_specs=in_specs,
        out_specs=out_specs,
        check_vma=False,
    )
```

```python
import functools
import math

import jax
import jax.numpy as jnp
from jax import lax
from jax.experimental import pallas as pl
from jax.experimental.pallas import tpu as pltpu
from jax.sharding import PartitionSpec as P

CHUNKS = 6
EPS = 1e-05
F32, BF16 = jnp.float32, jnp.bfloat16
PARAMS = pltpu.CompilerParams(vmem_limit_bytes=52 * 1024 * 1024)


def sigmoid(x):
    return pl.reciprocal(1.0 + jnp.exp(-x), approx=True)


def contract(left, right, left_dim, right_dim):
    return lax.dot_general(
        left, right, (((left_dim,), (right_dim,)), ((), ())), preferred_element_type=F32
    )


def at_least(macs, transcendentals, *arrays):
    return pl.CostEstimate(
        flops=2 * macs,
        transcendentals=transcendentals,
        bytes_accessed=sum(math.prod(x.shape) * x.dtype.itemsize for x in arrays),
    )


def swap_eight(arrays):
    place = lax.broadcasted_iota(jnp.int32, arrays[0].shape, 1)
    for shift in (4, 2, 1):
        low = (place & shift) == 0
        swapped = list(arrays)
        for n in range(8):
            if n & shift == 0:
                one, two = arrays[n], arrays[n + shift]
                swapped[n] = jnp.where(low, one, pltpu.roll(two, shift, 1))
                swapped[n + shift] = jnp.where(low, pltpu.roll(one, 8 - shift, 1), two)
        arrays = swapped
    return arrays


def project_kernel(n_pieces, n_slabs, which, *refs):
    pieces = refs[: n_pieces * n_slabs]
    weights, centre, gain, bias, out, held = refs[n_pieces * n_slabs :]
    eights, _, rows, depth = out.shape
    hidden = eights * 8

    def go(first):
        def two_rows(n, carry):
            values = jnp.concatenate(
                [piece[2 * n + i] for i in range(2) for piece in pieces[first : first + n_pieces]], axis=0
            )
            centred = contract(centre[...], values, 1, 1)
            variance = jnp.mean(centred * centred, axis=0, keepdims=True)
            normed = centred * lax.rsqrt(variance + EPS) * gain[...] + bias[...]
            projected = contract(weights[...], normed.astype(BF16), 1, 0)
            side = sigmoid(projected[:hidden]) * projected[hidden:]
            held[2 * n] = side[:, :depth]
            held[2 * n + 1] = side[:, depth:]
            return carry

        lax.fori_loop(0, rows // 2, two_rows, 0, unroll=2)

    for n in range(n_slabs):
        pl.when(which[0] == n)(functools.partial(go, n * n_pieces))

    def one_group(e, carry):
        at = pl.ds(pl.multiple_of(e * 8, 8), 8)
        for n in range(depth // 128):
            lanes = slice(n * 128, (n + 1) * 128)
            halves = [
                swap_eight([held[first + i, at, lanes][None] for i in range(8)]) for first in range(0, rows, 8)
            ]
            for h in range(8):
                out[e, h, :, lanes] = jnp.concatenate([half[h][0] for half in halves], axis=0).astype(BF16)
        return carry

    lax.fori_loop(0, eights, one_group, 0, unroll=2)


def project(slabs, which, n_pieces, weights, centre, gain, bias):
    rows = 16
    hidden, channels = weights.shape[0] // 2, weights.shape[1]
    count, columns = slabs[0].shape[0] // n_pieces, slabs[0].shape[1]
    depth = n_pieces * columns
    steps = count // rows
    whole = lambda x: pl.BlockSpec(x.shape, lambda i, which: (0,) * x.ndim)

    def piece_spec(n, p):
        return pl.BlockSpec(
            (rows, columns, channels), lambda i, which: (p * steps + jnp.where(which[0] == n, i, 0), 0, 0)
        )

    shape = jax.ShapeDtypeStruct((hidden // 8, 8, count, depth), BF16)
    side = pl.pallas_call(
        functools.partial(project_kernel, n_pieces, len(slabs)),
        grid_spec=pltpu.PrefetchScalarGridSpec(
            num_scalar_prefetch=1,
            grid=(steps,),
            in_specs=[piece_spec(n, p) for n in range(len(slabs)) for p in range(n_pieces)]
            + [whole(x) for x in (weights, centre, gain, bias)],
            out_specs=pl.BlockSpec((hidden // 8, 8, rows, depth), lambda i, which: (0, 0, i, 0)),
            scratch_shapes=[pltpu.VMEM((rows, hidden, depth), F32)],
        ),
        out_shape=shape,
        compiler_params=PARAMS,
        cost_estimate=at_least(count * depth * channels * (channels + 2 * hidden), count * depth * hidden, shape),
        name="project",
    )(which, *[slab for slab in slabs for _ in range(n_pieces)], weights, centre, gain, bias)
    return side.reshape(hidden, count, depth)


def triangle_kernel(n_left, n_sides, group, pairs, which, *refs):
    lefts, out = refs[:n_left], refs[-1]
    sides = refs[n_left:-1]
    step, rows, _ = lefts[0].shape
    columns = sides[0].shape[1]

    def go(choice):
        def pieces_of(h):
            found = {}
            for j in sorted({j for _, j in pairs}):
                same = [n for n, pair in enumerate(pairs) if pair[1] == j]
                if len(same) > 1:
                    rows_of = jnp.concatenate([lefts[pairs[n][0]][h] for n in same], axis=0)
                    made = contract(rows_of, sides[j * n_sides + choice][h], 1, 1)
                    found.update({n: made[p * rows : (p + 1) * rows] for p, n in enumerate(same)})
            for i in sorted({i for i, _ in pairs}):
                same = [n for n, pair in enumerate(pairs) if pair[0] == i and n not in found]
                if same:
                    columns_of = jnp.concatenate([sides[pairs[n][1] * n_sides + choice][h] for n in same], axis=0)
                    made = contract(lefts[i][h], columns_of, 1, 1)
                    found.update({n: made[:, p * columns : (p + 1) * columns] for p, n in enumerate(same)})
            return found

        def one_group(g, carry):
            found = [pieces_of(g * group + h) for h in range(group)]
            for n in range(len(pairs)):
                out[n, g] = jnp.concatenate([x[n] for x in found], axis=-1).astype(BF16)
            return carry

        lax.fori_loop(0, step // group, one_group, 0, unroll=2)

    for n in range(n_sides):
        pl.when(which[0] == n)(functools.partial(go, n))


def group_of(columns):
    return 128 // math.gcd(columns, 128)


def triangle(lefts, rights, pairs, which):
    hidden, rows, depth = lefts[0].shape
    columns = rights[0][0].shape[1]
    n_sides = len(rights[0])
    group = group_of(columns)
    step = max(16 if len(rights) > 3 else 32, group)
    shape = jax.ShapeDtypeStruct((len(pairs), hidden // group, rows, group * columns), BF16)

    def side_spec(n):
        return pl.BlockSpec((step, columns, depth), lambda h, which: (jnp.where(which[0] == n, h, 0), 0, 0))

    return pl.pallas_call(
        functools.partial(triangle_kernel, len(lefts), n_sides, group, pairs),
        grid_spec=pltpu.PrefetchScalarGridSpec(
            num_scalar_prefetch=1,
            grid=(hidden // step,),
            in_specs=[pl.BlockSpec((step, rows, depth), lambda h, which: (h, 0, 0))] * len(lefts)
            + [side_spec(n) for _ in rights for n in range(n_sides)],
            out_specs=pl.BlockSpec(
                (len(pairs), step // group, rows, group * columns), lambda h, which: (0, h, 0, 0)
            ),
        ),
        out_shape=shape,
        compiler_params=PARAMS,
        cost_estimate=at_least(
            len(pairs) * hidden * rows * columns * depth, 0, shape, *lefts, *[side[0] for side in rights]
        ),
        name="triangle",
    )(which, *lefts, *[x for side in rights for x in side])


def gate_kernel(pair, centre, mean, gain, bias, weights, out):
    rows, columns, channels = pair.shape
    values = pair[...].reshape(rows * columns, channels)
    centred = contract(values, centre[...], 1, 0)
    square = centred * centred
    high = square.astype(BF16)
    low = (square - high.astype(F32)).astype(BF16)
    variance = contract(jnp.concatenate([high, low], axis=1), mean[...], 1, 0)
    normed = (centred * lax.rsqrt(variance + EPS) * gain[...] + bias[...]).astype(BF16)
    gate = sigmoid(contract(normed, weights[...], 1, 0))
    out[...] = gate.astype(BF16).reshape(rows, columns, channels)


def gate_of(pair, centre, mean, gain, bias, weights):
    rows = 8
    count, columns, channels = pair.shape
    whole = lambda x: pl.BlockSpec(x.shape, lambda i: (0,) * x.ndim)
    block = pl.BlockSpec((rows, columns, channels), lambda i: (i, 0, 0))
    return pl.pallas_call(
        gate_kernel,
        grid=(count // rows,),
        in_specs=[block] + [whole(x) for x in (centre, mean, gain, bias, weights)],
        out_specs=block,
        out_shape=jax.ShapeDtypeStruct(pair.shape, BF16),
        compiler_params=PARAMS,
        cost_estimate=at_least(
            count * columns * channels * 4 * channels, count * columns * channels, pair, pair
        ),
        name="gate",
    )(pair, centre, mean, gain, bias, weights)


def finish_kernel(group, hidden, own, sent, gate, weights, gain, bias, *refs):
    out, rows_of = refs[-2:]
    packed, rows, lanes = own.shape
    columns = lanes // group

    def over_hidden(x):
        total = jnp.sum(x, axis=0)
        shift = columns
        while shift < lanes:
            total = total + pltpu.roll(total, shift, 1)
            shift *= 2
        return total * (1.0 / hidden)

    total = own[...].astype(F32) + sent[...].astype(F32)
    centred = total - over_hidden(total)[None]
    scale = lax.rsqrt(over_hidden(centred * centred) + EPS)
    normed = centred * scale[None] * gain[...] + bias[...]
    rows_of[...] = normed.reshape(packed * rows, lanes)
    batch = max(1, 128 // columns)
    for first in range(0, rows, batch):
        held = [rows_of[pl.ds(first + i, packed, stride=rows), :] for i in range(batch)]
        parts = [
            jnp.concatenate([x[:, g * columns : (g + 1) * columns] for x in held], axis=1) for g in range(group)
        ]
        result = contract(jnp.concatenate(parts, axis=0).astype(BF16), weights[...], 0, 0)
        for i in range(batch):
            gated = result[i * columns : (i + 1) * columns] * gate[first + i].astype(F32)
            out[first + i] = gated.astype(BF16)


def finish(own, sent, gate, t, before, chunks, share, weights, gain, bias, held):
    pieces, packed, count, lanes = own.shape
    rows = count if count <= 32 else 16
    hidden, channels = weights.shape
    group = hidden // packed
    steps = count // rows

    def row_of(p):
        return jnp.where(p < before, p // share, t)

    def column_of(p):
        of_row = p - before
        return jnp.where(p < before, (p % share) * chunks + t, (of_row % share) * chunks + of_row // share)

    whole = lambda x: pl.BlockSpec(x.shape, lambda p, r: (0,) * x.ndim)
    part = pl.BlockSpec((None, packed, rows, lanes), lambda p, r: (p, 0, r, 0))
    block = pl.BlockSpec((rows, lanes // group, channels), lambda p, r: (row_of(p) * steps + r, column_of(p), 0))
    earlier = [] if held is None else [held]
    return pl.pallas_call(
        functools.partial(finish_kernel, group, hidden),
        grid=(pieces, steps),
        in_specs=[part, part, block, whole(weights), whole(gain), whole(bias)]
        + [pl.BlockSpec(memory_space=pl.ANY)] * len(earlier),
        out_specs=block,
        out_shape=jax.ShapeDtypeStruct(gate.shape, BF16),
        scratch_shapes=[pltpu.VMEM((packed * rows, lanes), F32)],
        input_output_aliases={6: 0} if earlier else {},
        compiler_params=PARAMS,
        cost_estimate=at_least(
            pieces * count * (lanes // group) * hidden * channels, pieces * count * (lanes // group), own, sent
        ),
        name="finish",
    )(own, sent, gate, weights, gain, bias, *earlier)


def after(value, *others):
    return lax.optimization_barrier((value,) + others)[0]


def on_device(n_row, n_col, pair_act, ln_gain, ln_bias, w_proj, w_gate, out_gain, out_bias, w_out):
    tile_rows, tile_cols, channels = pair_act.shape
    hidden = w_proj.shape[1] // 4
    half = n_col // 2
    top = n_row // 2
    share = n_row // n_col
    row, col = lax.axis_index("row"), lax.axis_index("col")
    axes = ("row", "col")
    place = lambda r, c: r * n_col + c
    chunks = min(CHUNKS, tile_rows // 16)
    step = tile_rows // chunks
    group = group_of(step)
    packed = hidden // group

    w_left, w_right = w_proj.T[: 2 * hidden], w_proj.T[2 * hidden :]
    centre = (jnp.eye(channels, dtype=F32) - 1.0 / channels).astype(BF16)
    mean = jnp.full((2 * channels, channels), 1.0 / channels, BF16)
    by_hidden = lambda v: jnp.repeat(v.reshape(packed, group), step, axis=1)[:, None, :]
    gain_out, bias_out = by_hidden(out_gain), by_hidden(out_bias)
    w_last = w_out.reshape(packed, group, channels).swapaxes(0, 1).reshape(hidden, channels)

    def holds(r, c):
        return (r // share) % half == c % half

    def across_top(near):
        pairs = [(place(r, c), place(r ^ top, c)) for r in range(n_row) for c in range(n_col) if holds(r, c)]
        return lax.ppermute(near, axes, pairs)

    def to_all_rows(held):
        bit = top // 2
        while bit >= share:
            alike = (bit * 2 - 1) & ~(share - 1)
            sends = [
                (place(r, c), place(r ^ bit, c))
                for r in range(n_row)
                for c in range(n_col)
                if (r ^ (c * share)) & alike == 0
            ]
            came = lax.ppermute(held, axes, sends)
            if bit == 1:
                return [[held, came]]
            held = jnp.where(((row ^ (col * share)) & bit) == 0, held, came)
            bit //= 2
        slabs = [held]
        while bit >= 1:
            swap = [(r, r ^ bit) for r in range(n_row)]
            others = [lax.ppermute(x, "row", swap) for x in slabs]
            slabs = [jnp.where((row & bit) == 0, a, b) for a, b in zip(slabs + others, others + slabs)]
            bit //= 2
        return [[x] for x in slabs]

    near_is_own = (row // top) == (col // half)
    swap_half = [(c, c ^ half) for c in range(n_col)]
    two_chips = share == 1 and top == 2
    holder = ((row ^ col) & 1) == 0
    number = lambda x: jnp.asarray(x, jnp.int32).reshape(1)
    payloads, firsts, lefts, spread, right_sent, right_own = [], [], [], {}, {}, {}

    def first_step(slab):
        if not two_chips:
            return across_top(slab)
        pairs = [(place(r, c), place(r ^ top ^ 1, c)) for r in range(n_row) for c in range(n_col) if holds(r, c)]
        return lax.ppermute(slab, axes, pairs)

    def second_step(slab, far, *waits):
        if not two_chips:
            odd = (row ^ col) & 1
            shards_of = zip(to_all_rows(slab), to_all_rows(far))
            return [(a + b, odd if len(a) > 1 else 0, len(a) + (odd if len(a) > 1 else 0)) for a, b in shards_of]
        given = jnp.where(holder, slab, after(far, *waits))
        got = lax.ppermute(given, "row", [(r, r ^ 1) for r in range(n_row)])
        return [([slab, got, far], jnp.where(holder, 0, 1), jnp.where(holder, 1, 2))]

    def product(pairs, rights):
        used_left = sorted({i for i, _, _ in pairs})
        used_right = sorted({(j, s) for _, j, s in pairs})
        return triangle(
            [lefts[i] for i in used_left],
            [[rights[key]] for key in used_right],
            [(used_left.index(i), used_right.index((j, s))) for i, j, s in pairs],
            number(0),
        )

    wide = lambda v: jnp.broadcast_to(v[:, None], (channels, 2 * half * tile_cols))
    gain_in, bias_in = wide(ln_gain), wide(ln_bias)
    shards = range(share)
    waves = []
    for t in range(chunks):
        by_column = [(i, t, s) for i in range(t) for s in shards]
        by_row = [(t, j, s) for j in range(t + 1) for s in shards]
        waves.append([by_row, by_column] if t == chunks - 1 and t else [by_column + by_row])

    token, moved, own, exchanged = [], [], [], []

    def side(candidates, choice, weights):
        made = project(candidates, number(choice), half, weights, centre, after(gain_in, *token), bias_in)
        token[:] = [made]
        return made

    def right_of(key, own):
        candidates, near, far = spread[key]
        return side(candidates, jnp.where(near_is_own == own, near, far), w_right)

    def multiply(t, rights):
        made = []
        for pairs in waves[t]:
            lefts[t] = after(lefts[t], *token)
            made.append(product(pairs, rights))
            token[:] = made[-1:]
        return made

    def keep_own(steps):
        for _ in range(steps):
            t = len(own)
            missing = [s for s in shards if (t, s) not in right_own]
            if t < chunks and missing:
                right_own[t, missing[0]] = right_of((t, missing[0]), True)
            elif t < chunks:
                own.append(multiply(t, right_own))

    def exchange(n, *waits):
        block = after(slabs[n], *waits) if waits else slabs[n]
        exchanged.append([lax.ppermute(block, "col", [(c, c ^ o) for c in range(n_col)]) for o in range(1, half)])

    slabs = [pair_act[:step]]
    rest = after(pair_act, slabs[0])
    slabs += [rest[n * step : (n + 1) * step] for n in range(1, chunks)]
    exchange(0)

    def base(n, *waits):
        return jnp.pad(after(slabs[n], *waits) if waits else slabs[n], ((0, (half - 1) * step), (0, 0), (0, 0)))

    bases = [base(n) for n in range(min(2, chunks))]
    token[:] = slabs + bases
    for n in range(chunks + 1):
        steps = list(token)
        waits = steps + (exchanged[n][-1:] if n < chunks else [])
        if n >= 3:
            waits = waits + moved[n - 3]
        if n + 1 < chunks:
            exchange(n + 1, *waits)
        if n < chunks:
            payload = after(bases[n], *(waits if n >= 3 else steps))
            for p, piece in enumerate(exchanged[n]):
                payload = lax.dynamic_update_slice_in_dim(payload, piece, (p + 1) * step, axis=0)
            payloads.append(payload)
            firsts.append(first_step(payloads[n]))
        if n == 0:
            early = after(ln_gain[None], *waits, gain_out, bias_out, w_last)
            gate = gate_of(pair_act, centre, mean, early, ln_bias[None], w_gate)
            token[:] = [gate]
            continue
        t = n - 1
        for s, found in enumerate(second_step(payloads[t], firsts[t], *steps)):
            spread[t, s] = found
        if n + 1 < chunks:
            bases.append(base(n + 1, *waits))
            token.append(bases[-1])
        lefts.append(side([payloads[t]], 0, w_left))
        for s in shards:
            right_sent[t, s] = right_of((t, s), False)
        if t == chunks - 1:
            keep_own(2)
        made = multiply(t, right_sent)
        waits = moved[t - 1] if t else []
        moved.append([lax.ppermute(after(x, *waits) if waits else x, "col", swap_half) for x in made])
        keep_own({chunks - 4: 1, chunks - 3: 2, chunks - 2: 4}.get(t, 0))
    keep_own(chunks * (share + 1))
    out = None
    for t in range(chunks):
        for pairs, kept, came in zip(waves[t], own[t], moved[t]):
            before = sum(j == t and i < t for i, j, _ in pairs)
            out = finish(kept, came, gate, t, before, chunks, share, w_last, gain_out, bias_out, out)
    return out


def solution(mesh):
    n_row, n_col = mesh.shape["row"], mesh.shape["col"]
    in_specs = (P(("groups", "row"), "col", None), P(), P(), P(), P(), P(), P(), P())
    out_specs = P(("groups", "row"), "col", None)
    return jax.shard_map(
        functools.partial(on_device, n_row, n_col),
        mesh=mesh,
        in_specs=in_specs,
        out_specs=out_specs,
        check_vma=False,
    )
```

```python
import functools
import math

import jax
import jax.numpy as jnp
from jax import lax
from jax.experimental import pallas as pl
from jax.experimental.pallas import tpu as pltpu
from jax.sharding import PartitionSpec as P

CHUNKS = 6
EPS = 1e-05
F32, BF16 = jnp.float32, jnp.bfloat16
PARAMS = pltpu.CompilerParams(vmem_limit_bytes=52 * 1024 * 1024)


def sigmoid(x):
    return pl.reciprocal(1.0 + jnp.exp(-x), approx=True)


def contract(left, right, left_dim, right_dim):
    return lax.dot_general(
        left, right, (((left_dim,), (right_dim,)), ((), ())), preferred_element_type=F32
    )


def at_least(macs, transcendentals, *arrays):
    return pl.CostEstimate(
        flops=2 * macs,
        transcendentals=transcendentals,
        bytes_accessed=sum(math.prod(x.shape) * x.dtype.itemsize for x in arrays),
    )


def swap_eight(arrays):
    place = lax.broadcasted_iota(jnp.int32, arrays[0].shape, 1)
    for shift in (4, 2, 1):
        low = (place & shift) == 0
        swapped = list(arrays)
        for n in range(8):
            if n & shift == 0:
                one, two = arrays[n], arrays[n + shift]
                swapped[n] = jnp.where(low, one, pltpu.roll(two, shift, 1))
                swapped[n + shift] = jnp.where(low, pltpu.roll(one, 8 - shift, 1), two)
        arrays = swapped
    return arrays


def project_kernel(n_pieces, n_slabs, which, *refs):
    pieces = refs[: n_pieces * n_slabs]
    weights, centre, gain, bias, out, held = refs[n_pieces * n_slabs :]
    eights, _, rows, depth = out.shape
    hidden = eights * 8

    def go(first):
        def two_rows(n, carry):
            values = jnp.concatenate(
                [piece[2 * n + i] for i in range(2) for piece in pieces[first : first + n_pieces]], axis=0
            )
            centred = contract(centre[...], values, 1, 1)
            variance = jnp.mean(centred * centred, axis=0, keepdims=True)
            normed = centred * lax.rsqrt(variance + EPS) * gain[...] + bias[...]
            projected = contract(weights[...], normed.astype(BF16), 1, 0)
            side = sigmoid(projected[:hidden]) * projected[hidden:]
            held[2 * n] = side[:, :depth]
            held[2 * n + 1] = side[:, depth:]
            return carry

        lax.fori_loop(0, rows // 2, two_rows, 0, unroll=2)

    for n in range(n_slabs):
        pl.when(which[0] == n)(functools.partial(go, n * n_pieces))

    def one_group(e, carry):
        at = pl.ds(pl.multiple_of(e * 8, 8), 8)
        for n in range(depth // 128):
            lanes = slice(n * 128, (n + 1) * 128)
            halves = [
                swap_eight([held[first + i, at, lanes][None] for i in range(8)]) for first in range(0, rows, 8)
            ]
            for h in range(8):
                out[e, h, :, lanes] = jnp.concatenate([half[h][0] for half in halves], axis=0).astype(BF16)
        return carry

    lax.fori_loop(0, eights, one_group, 0, unroll=2)


def project(slabs, which, n_pieces, weights, centre, gain, bias):
    rows = 16
    hidden, channels = weights.shape[0] // 2, weights.shape[1]
    count, columns = slabs[0].shape[0] // n_pieces, slabs[0].shape[1]
    depth = n_pieces * columns
    steps = count // rows
    whole = lambda x: pl.BlockSpec(x.shape, lambda i, which: (0,) * x.ndim)

    def piece_spec(n, p):
        return pl.BlockSpec(
            (rows, columns, channels), lambda i, which: (p * steps + jnp.where(which[0] == n, i, 0), 0, 0)
        )

    shape = jax.ShapeDtypeStruct((hidden // 8, 8, count, depth), BF16)
    side = pl.pallas_call(
        functools.partial(project_kernel, n_pieces, len(slabs)),
        grid_spec=pltpu.PrefetchScalarGridSpec(
            num_scalar_prefetch=1,
            grid=(steps,),
            in_specs=[piece_spec(n, p) for n in range(len(slabs)) for p in range(n_pieces)]
            + [whole(x) for x in (weights, centre, gain, bias)],
            out_specs=pl.BlockSpec((hidden // 8, 8, rows, depth), lambda i, which: (0, 0, i, 0)),
            scratch_shapes=[pltpu.VMEM((rows, hidden, depth), F32)],
        ),
        out_shape=shape,
        compiler_params=PARAMS,
        cost_estimate=at_least(count * depth * channels * (channels + 2 * hidden), count * depth * hidden, shape),
        name="project",
    )(which, *[slab for slab in slabs for _ in range(n_pieces)], weights, centre, gain, bias)
    return side.reshape(hidden, count, depth)


def triangle_kernel(n_left, n_sides, group, pairs, which, *refs):
    lefts, out = refs[:n_left], refs[-1]
    sides = refs[n_left:-1]
    step, rows, _ = lefts[0].shape
    columns = sides[0].shape[1]

    def go(choice):
        def pieces_of(h):
            found = {}
            for j in sorted({j for _, j in pairs}):
                same = [n for n, pair in enumerate(pairs) if pair[1] == j]
                if len(same) > 1:
                    rows_of = jnp.concatenate([lefts[pairs[n][0]][h] for n in same], axis=0)
                    made = contract(rows_of, sides[j * n_sides + choice][h], 1, 1)
                    found.update({n: made[p * rows : (p + 1) * rows] for p, n in enumerate(same)})
            for i in sorted({i for i, _ in pairs}):
                same = [n for n, pair in enumerate(pairs) if pair[0] == i and n not in found]
                if same:
                    columns_of = jnp.concatenate([sides[pairs[n][1] * n_sides + choice][h] for n in same], axis=0)
                    made = contract(lefts[i][h], columns_of, 1, 1)
                    found.update({n: made[:, p * columns : (p + 1) * columns] for p, n in enumerate(same)})
            return found

        def one_group(g, carry):
            found = [pieces_of(g * group + h) for h in range(group)]
            for n in range(len(pairs)):
                out[n, g] = jnp.concatenate([x[n] for x in found], axis=-1).astype(BF16)
            return carry

        lax.fori_loop(0, step // group, one_group, 0, unroll=2)

    for n in range(n_sides):
        pl.when(which[0] == n)(functools.partial(go, n))


def group_of(columns):
    return 128 // math.gcd(columns, 128)


def triangle(lefts, rights, pairs, which):
    hidden, rows, depth = lefts[0].shape
    columns = rights[0][0].shape[1]
    n_sides = len(rights[0])
    group = group_of(columns)
    step = max(16 if len(rights) > 3 else 32, group)
    shape = jax.ShapeDtypeStruct((len(pairs), hidden // group, rows, group * columns), BF16)

    def side_spec(n):
        return pl.BlockSpec((step, columns, depth), lambda h, which: (jnp.where(which[0] == n, h, 0), 0, 0))

    return pl.pallas_call(
        functools.partial(triangle_kernel, len(lefts), n_sides, group, pairs),
        grid_spec=pltpu.PrefetchScalarGridSpec(
            num_scalar_prefetch=1,
            grid=(hidden // step,),
            in_specs=[pl.BlockSpec((step, rows, depth), lambda h, which: (h, 0, 0))] * len(lefts)
            + [side_spec(n) for _ in rights for n in range(n_sides)],
            out_specs=pl.BlockSpec(
                (len(pairs), step // group, rows, group * columns), lambda h, which: (0, h, 0, 0)
            ),
        ),
        out_shape=shape,
        compiler_params=PARAMS,
        cost_estimate=at_least(
            len(pairs) * hidden * rows * columns * depth, 0, shape, *lefts, *[side[0] for side in rights]
        ),
        name="triangle",
    )(which, *lefts, *[x for side in rights for x in side])


def gate_kernel(pair, centre, mean, gain, bias, weights, out):
    rows, columns, channels = pair.shape
    values = pair[...].reshape(rows * columns, channels)
    centred = contract(values, centre[...], 1, 0)
    square = centred * centred
    high = square.astype(BF16)
    low = (square - high.astype(F32)).astype(BF16)
    variance = contract(jnp.concatenate([high, low], axis=1), mean[...], 1, 0)
    normed = (centred * lax.rsqrt(variance + EPS) * gain[...] + bias[...]).astype(BF16)
    gate = sigmoid(contract(normed, weights[...], 1, 0))
    out[...] = gate.astype(BF16).reshape(rows, columns, channels)


def gate_of(pair, centre, mean, gain, bias, weights):
    rows = 8
    count, columns, channels = pair.shape
    whole = lambda x: pl.BlockSpec(x.shape, lambda i: (0,) * x.ndim)
    block = pl.BlockSpec((rows, columns, channels), lambda i: (i, 0, 0))
    return pl.pallas_call(
        gate_kernel,
        grid=(count // rows,),
        in_specs=[block] + [whole(x) for x in (centre, mean, gain, bias, weights)],
        out_specs=block,
        out_shape=jax.ShapeDtypeStruct(pair.shape, BF16),
        compiler_params=PARAMS,
        cost_estimate=at_least(
            count * columns * channels * 4 * channels, count * columns * channels, pair, pair
        ),
        name="gate",
    )(pair, centre, mean, gain, bias, weights)


def finish_kernel(group, hidden, own, sent, gate, weights, gain, bias, *refs):
    out, rows_of = refs[-2:]
    packed, rows, lanes = own.shape
    columns = lanes // group

    def over_hidden(x):
        total = jnp.sum(x, axis=0)
        shift = columns
        while shift < lanes:
            total = total + pltpu.roll(total, shift, 1)
            shift *= 2
        return total * (1.0 / hidden)

    total = own[...].astype(F32) + sent[...].astype(F32)
    centred = total - over_hidden(total)[None]
    scale = lax.rsqrt(over_hidden(centred * centred) + EPS)
    normed = centred * scale[None] * gain[...] + bias[...]
    rows_of[...] = normed.reshape(packed * rows, lanes)
    batch = max(1, 128 // columns)
    for first in range(0, rows, batch):
        held = [rows_of[pl.ds(first + i, packed, stride=rows), :] for i in range(batch)]
        parts = [
            jnp.concatenate([x[:, g * columns : (g + 1) * columns] for x in held], axis=1) for g in range(group)
        ]
        result = contract(jnp.concatenate(parts, axis=0).astype(BF16), weights[...], 0, 0)
        for i in range(batch):
            gated = result[i * columns : (i + 1) * columns] * gate[first + i].astype(F32)
            out[first + i] = gated.astype(BF16)


def finish(own, sent, gate, t, before, chunks, share, weights, gain, bias, held):
    pieces, packed, count, lanes = own.shape
    rows = count if count <= 32 else 16
    hidden, channels = weights.shape
    group = hidden // packed
    steps = count // rows

    def row_of(p):
        return jnp.where(p < before, p // share, t)

    def column_of(p):
        of_row = p - before
        return jnp.where(p < before, (p % share) * chunks + t, (of_row % share) * chunks + of_row // share)

    whole = lambda x: pl.BlockSpec(x.shape, lambda p, r: (0,) * x.ndim)
    part = pl.BlockSpec((None, packed, rows, lanes), lambda p, r: (p, 0, r, 0))
    block = pl.BlockSpec((rows, lanes // group, channels), lambda p, r: (row_of(p) * steps + r, column_of(p), 0))
    earlier = [] if held is None else [held]
    return pl.pallas_call(
        functools.partial(finish_kernel, group, hidden),
        grid=(pieces, steps),
        in_specs=[part, part, block, whole(weights), whole(gain), whole(bias)]
        + [pl.BlockSpec(memory_space=pl.ANY)] * len(earlier),
        out_specs=block,
        out_shape=jax.ShapeDtypeStruct(gate.shape, BF16),
        scratch_shapes=[pltpu.VMEM((packed * rows, lanes), F32)],
        input_output_aliases={6: 0} if earlier else {},
        compiler_params=PARAMS,
        cost_estimate=at_least(
            pieces * count * (lanes // group) * hidden * channels, pieces * count * (lanes // group), own, sent
        ),
        name="finish",
    )(own, sent, gate, weights, gain, bias, *earlier)


def after(value, *others):
    return lax.optimization_barrier((value,) + others)[0]


def on_device(n_row, n_col, pair_act, ln_gain, ln_bias, w_proj, w_gate, out_gain, out_bias, w_out):
    tile_rows, tile_cols, channels = pair_act.shape
    hidden = w_proj.shape[1] // 4
    half = n_col // 2
    top = n_row // 2
    share = n_row // n_col
    row, col = lax.axis_index("row"), lax.axis_index("col")
    axes = ("row", "col")
    place = lambda r, c: r * n_col + c
    chunks = min(CHUNKS, tile_rows // 16)
    step = tile_rows // chunks
    group = group_of(step)
    packed = hidden // group

    w_left, w_right = w_proj.T[: 2 * hidden], w_proj.T[2 * hidden :]
    centre = (jnp.eye(channels, dtype=F32) - 1.0 / channels).astype(BF16)
    mean = jnp.full((2 * channels, channels), 1.0 / channels, BF16)
    by_hidden = lambda v: jnp.repeat(v.reshape(packed, group), step, axis=1)[:, None, :]
    gain_out, bias_out = by_hidden(out_gain), by_hidden(out_bias)
    w_last = w_out.reshape(packed, group, channels).swapaxes(0, 1).reshape(hidden, channels)

    def holds(r, c):
        return (r // share) % half == c % half

    def across_top(near):
        pairs = [(place(r, c), place(r ^ top, c)) for r in range(n_row) for c in range(n_col) if holds(r, c)]
        return lax.ppermute(near, axes, pairs)

    def to_all_rows(held):
        bit = top // 2
        while bit >= share:
            alike = (bit * 2 - 1) & ~(share - 1)
            sends = [
                (place(r, c), place(r ^ bit, c))
                for r in range(n_row)
                for c in range(n_col)
                if (r ^ (c * share)) & alike == 0
            ]
            came = lax.ppermute(held, axes, sends)
            if bit == 1:
                return [[held, came]]
            held = jnp.where(((row ^ (col * share)) & bit) == 0, held, came)
            bit //= 2
        slabs = [held]
        while bit >= 1:
            swap = [(r, r ^ bit) for r in range(n_row)]
            others = [lax.ppermute(x, "row", swap) for x in slabs]
            slabs = [jnp.where((row & bit) == 0, a, b) for a, b in zip(slabs + others, others + slabs)]
            bit //= 2
        return [[x] for x in slabs]

    near_is_own = (row // top) == (col // half)
    swap_half = [(c, c ^ half) for c in range(n_col)]
    two_chips = share == 1 and top == 2
    holder = ((row ^ col) & 1) == 0
    number = lambda x: jnp.asarray(x, jnp.int32).reshape(1)
    payloads, firsts, lefts, spread, right_sent, right_own = [], [], [], {}, {}, {}

    def first_step(slab):
        if not two_chips:
            return across_top(slab)
        pairs = [(place(r, c), place(r ^ top ^ 1, c)) for r in range(n_row) for c in range(n_col) if holds(r, c)]
        return lax.ppermute(slab, axes, pairs)

    def second_step(slab, far, *waits):
        if not two_chips:
            odd = (row ^ col) & 1
            shards_of = zip(to_all_rows(slab), to_all_rows(far))
            return [(a + b, odd if len(a) > 1 else 0, len(a) + (odd if len(a) > 1 else 0)) for a, b in shards_of]
        given = jnp.where(holder, slab, after(far, *waits))
        got = lax.ppermute(given, "row", [(r, r ^ 1) for r in range(n_row)])
        return [([slab, got, far], jnp.where(holder, 0, 1), jnp.where(holder, 1, 2))]

    def product(pairs, rights):
        used_left = sorted({i for i, _, _ in pairs})
        used_right = sorted({(j, s) for _, j, s in pairs})
        return triangle(
            [lefts[i] for i in used_left],
            [[rights[key]] for key in used_right],
            [(used_left.index(i), used_right.index((j, s))) for i, j, s in pairs],
            number(0),
        )

    wide = lambda v: jnp.broadcast_to(v[:, None], (channels, 2 * half * tile_cols))
    gain_in, bias_in = wide(ln_gain), wide(ln_bias)
    shards = range(share)
    waves = []
    for t in range(chunks):
        by_column = [(i, t, s) for i in range(t) for s in shards]
        by_row = [(t, j, s) for j in range(t + 1) for s in shards]
        waves.append([by_row, by_column] if t == chunks - 1 and t else [by_column + by_row])

    token, moved, own, exchanged = [], [], [], []

    def side(candidates, choice, weights):
        made = project(candidates, number(choice), half, weights, centre, after(gain_in, *token), bias_in)
        token[:] = [made]
        return made

    def right_of(key, own):
        candidates, near, far = spread[key]
        return side(candidates, jnp.where(near_is_own == own, near, far), w_right)

    def multiply(t, rights):
        made = []
        for pairs in waves[t]:
            lefts[t] = after(lefts[t], *token)
            made.append(product(pairs, rights))
            token[:] = made[-1:]
        return made

    def keep_own(steps):
        for _ in range(steps):
            t = len(own)
            missing = [s for s in shards if (t, s) not in right_own]
            if t < chunks and missing:
                right_own[t, missing[0]] = right_of((t, missing[0]), True)
            elif t < chunks:
                own.append(multiply(t, right_own))

    def exchange(n, *waits):
        block = after(slabs[n], *waits) if waits else slabs[n]
        exchanged.append([lax.ppermute(block, "col", [(c, c ^ o) for c in range(n_col)]) for o in range(1, half)])

    slabs = [pair_act[:step]]
    rest = after(pair_act, slabs[0])
    slabs += [rest[n * step : (n + 1) * step] for n in range(1, chunks)]
    exchange(0)

    def base(n, *waits):
        return jnp.pad(after(slabs[n], *waits) if waits else slabs[n], ((0, (half - 1) * step), (0, 0), (0, 0)))

    bases = [base(n) for n in range(min(2, chunks))]
    token[:] = slabs + bases
    for n in range(chunks + 1):
        steps = list(token)
        waits = steps + (exchanged[n][-1:] if n < chunks else [])
        if n >= 3:
            waits = waits + moved[n - 3]
        if n + 1 < chunks:
            exchange(n + 1, *waits)
        if n < chunks:
            payload = after(bases[n], *(waits if n >= 3 else steps))
            for p, piece in enumerate(exchanged[n]):
                payload = lax.dynamic_update_slice_in_dim(payload, piece, (p + 1) * step, axis=0)
            payloads.append(payload)
            firsts.append(first_step(payloads[n]))
        if n == 0:
            early = after(ln_gain[None], *waits, gain_out, bias_out, w_last)
            gate = gate_of(pair_act, centre, mean, early, ln_bias[None], w_gate)
            token[:] = [gate]
            continue
        t = n - 1
        for s, found in enumerate(second_step(payloads[t], firsts[t], *steps)):
            spread[t, s] = found
        if n + 1 < chunks:
            bases.append(base(n + 1, *waits))
            token.append(bases[-1])
        lefts.append(side([payloads[t]], 0, w_left))
        for s in shards:
            right_sent[t, s] = right_of((t, s), False)
        if t == chunks - 1:
            keep_own(3)
        made = multiply(t, right_sent)
        waits = moved[t - 1] if t else []
        moved.append([lax.ppermute(after(x, *waits) if waits else x, "col", swap_half) for x in made])
        keep_own({chunks - 4: 1, chunks - 3: 2, chunks - 2: 3}.get(t, 0))
    keep_own(chunks * (share + 1))
    out = None
    for t in range(chunks):
        for pairs, kept, came in zip(waves[t], own[t], moved[t]):
            before = sum(j == t and i < t for i, j, _ in pairs)
            out = finish(kept, came, gate, t, before, chunks, share, w_last, gain_out, bias_out, out)
    return out


def solution(mesh):
    n_row, n_col = mesh.shape["row"], mesh.shape["col"]
    in_specs = (P(("groups", "row"), "col", None), P(), P(), P(), P(), P(), P(), P())
    out_specs = P(("groups", "row"), "col", None)
    return jax.shard_map(
        functools.partial(on_device, n_row, n_col),
        mesh=mesh,
        in_specs=in_specs,
        out_specs=out_specs,
        check_vma=False,
    )
```
